32 devices in a mesh: row: 8 (over z, x), col: 4 (over y, core).
Axes of the slice: x: 2, y: 2, z: 4, core: 2. Of those that a mesh axis runs over, the one named last changes fastest.
Arguments:
- a_blocks: bfloat16 [192, 32, 4096], P('row', 'col'), may hold values from -0.125 to 0.125
- a_cols: int32 [192, 32], P('row'), may hold values from 0 to 191, as said below
- counts: int32 [192], P('row'), may hold values from 8 to 32
- p_blocks: bfloat16 [192, 4, 4096], P('row'), may hold values from -0.8984375 to 0.8984375
- p_cols: int32 [192, 4], replicated, may hold values from 0 to 63, as said below
Outputs:
- coarse: bfloat16 [64, 56, 4096], P('row')
The draws below stay inside these ranges and needn't reach their ends.
Inputs may be any that keep to these rules, and one draw needn't show every extreme that they name: `a_cols`: slot 0 of block row i names i itself; every slot's column lies within 24 of its row. `p_cols`: the four columns of fine block row i are distinct before clipping to the grid and lie within 8 of (i // 24) * 8 + ((i % 24) * 8) // 24.
All inputs are finite; a program needn't handle non-finite values.
Results may differ from the reference program's by a relative error of at most 0.015.
Values may be sent and summed in bfloat16 or wider, within the bound.
No kernel may reach another device: no remote copies, remote signals or barrier semaphores. Data moves between devices by JAX's collectives and lax.ppermute only.
A program may use at most 192 MiB of HBM per device.

```python
import jax
import jax.numpy as jnp
from jax import lax

BS = 64
KA = 32
RB = 24
CB = 8
NFB = 192
NCB = 64
N_ROW = 8


def draw_a_cols(key, part):
    key = jax.random.fold_in(key, 11)
    rows = jnp.arange(NFB, dtype=jnp.int32)
    offsets = jax.random.randint(key, (NFB, KA), -RB, RB + 1, dtype=jnp.int32)
    offsets = offsets.at[:, 0].set(0)
    return jnp.clip(rows[:, None] + offsets, 0, NFB - 1).astype(jnp.int32)


def draw_p_cols(key, part):
    key = jax.random.fold_in(key, 23)
    choices_n = 2 * CB + 1
    scores = jax.random.randint(key, (NFB, choices_n), 0, 1 << 20, dtype=jnp.int32)
    scores = scores * choices_n + jnp.arange(choices_n, dtype=jnp.int32)[None, :]
    order = jnp.argsort(scores, axis=1, stable=True).astype(jnp.int32)
    offsets = order[:, :4] - CB
    rows = jnp.arange(NFB, dtype=jnp.int32)
    center = rows // RB * CB + rows % RB * CB // RB
    return jnp.clip(center[:, None] + offsets, 0, NCB - 1).astype(jnp.int32)


def place_ends(values, rng, low, largest):
    shape = values.shape
    index_at = [jax.random.randint(jax.random.fold_in(rng, axis), (), 0, shape[axis]) for axis in range(len(shape))]
    values = values.at[tuple(index_at)].set(low)
    longest = shape.index(max(shape))
    index_at[longest] = (index_at[longest] + 1) % shape[longest]
    return values.at[tuple(index_at)].set(largest)


def block_scale(own_key, dims, pieces, smallest, high):
    loudness, own = 1.0, jax.random.fold_in(own_key, 6)
    for dim, blocks in pieces:
        draws = jnp.exp(jax.random.uniform(jax.random.fold_in(own, dim), (blocks,), jnp.float32, smallest / len(pieces), high / len(pieces)))
        loudness = loudness * jnp.repeat(draws, dims[dim] // blocks).reshape([-1 if axis == dim else 1 for axis in range(len(dims))])
    return loudness


def normal_values(own_key, dims, deviation, limit, pieces=(), held_as=jnp.bfloat16):
    array = jax.random.normal(own_key, dims, jnp.float32) * deviation
    if len(pieces) > 0:
        array = block_scale(own_key, dims, pieces, -0.22, 0.18) * array
    return jnp.clip(array, min=-limit, max=limit).astype(held_as)


def setup_inputs(seed: int = 0) -> dict:
    key_list = jax.random.split(jax.random.key(seed), 6)
    return {
        "a_blocks": normal_values(key_list[0], (NFB, KA, BS * BS), (BS * KA) ** -0.5, 0.125, ((0, 8), (1, 4))),
        "a_cols": draw_a_cols(jax.random.fold_in(key_list[5], 71), 0),
        "counts": place_ends(jax.random.randint(key_list[2], (NFB,), 8, KA + 1), jax.random.fold_in(key_list[2], 1), 8, KA).astype(jnp.int32),
        "p_blocks": normal_values(key_list[3], (NFB, 4, BS * BS), 0.15, 0.8984375, ((0, 8),)),
        "p_cols": draw_p_cols(jax.random.fold_in(key_list[5], 71), 0),
    }


def reference(a_blocks, a_cols, counts, p_blocks, p_cols):
    a_full = a_blocks.reshape(NFB, KA, BS, BS)
    p_full = p_blocks.reshape(NFB, 4, BS, BS)
    p_pad = jnp.pad(p_full, ((RB, RB), (0, 0), (0, 0), (0, 0)))
    ids_pad = jnp.pad(p_cols, ((RB, RB), (0, 0)), constant_values=-1000000)
    span = 5 * CB

    def slab(index):
        index = index.astype(jnp.int32)
        start = (index * RB).astype(jnp.int32)
        rows_a = lax.dynamic_slice_in_dim(a_full, start, RB, 0).astype(jnp.float32)
        cols = lax.dynamic_slice_in_dim(a_cols, start, RB, 0)
        live_count = lax.dynamic_slice_in_dim(counts, start, RB, 0)
        live = jnp.arange(KA, dtype=jnp.int32)[None, :] < live_count[:, None]
        near = lax.dynamic_slice_in_dim(p_pad, start, 3 * RB, 0)
        near_ids = lax.dynamic_slice_in_dim(ids_pad, start, 3 * RB, 0)
        local = (cols - (index - 1) * RB).astype(jnp.int32)
        picked = near[local].astype(jnp.float32)
        prods = jnp.einsum('nkab,nktbc->nktac', rows_a, picked)
        window = near_ids[local] - (index - 2) * CB
        onehot = ((window[..., None] == jnp.arange(span, dtype=jnp.int32)) & live[:, :, None, None]).astype(jnp.float32)
        product_ap = jnp.einsum('nktw,nktac->nwac', onehot, prods).astype(jnp.bfloat16)
        own = lax.dynamic_slice_in_dim(p_full, start, RB, 0).astype(jnp.float32)
        own_ids = lax.dynamic_slice_in_dim(p_cols, start, RB, 0) - (index - 1) * CB
        onehot_rows = (own_ids[..., None] == jnp.arange(3 * CB, dtype=jnp.int32)).astype(jnp.float32)
        second = jnp.einsum('nsba,nwbc->nswac', own, product_ap.astype(jnp.float32))
        return jnp.einsum('nsi,nswac->iwac', onehot_rows, second)

    parts = lax.map(slab, jnp.arange(N_ROW, dtype=jnp.int32))
    zero = jnp.zeros((1, CB, 5 * CB, BS, BS), jnp.float32)
    lower = jnp.concatenate([zero, parts[:-1, 2 * CB:]], axis=0)
    upper = jnp.concatenate([parts[1:, :CB], zero], axis=0)
    middle = parts[:, CB:2 * CB]
    total = jnp.pad(lower, ((0, 0), (0, 0), (0, 2 * CB), (0, 0), (0, 0)))
    total = total + jnp.pad(middle, ((0, 0), (0, 0), (CB, CB), (0, 0), (0, 0)))
    total = total + jnp.pad(upper, ((0, 0), (0, 0), (2 * CB, 0), (0, 0), (0, 0)))
    return total.reshape(N_ROW * CB, 7 * CB, BS * BS).astype(jnp.bfloat16)
```

```python
import functools

import jax
import jax.numpy as jnp
from jax import lax
from jax.experimental import pallas as pl
from jax.experimental.pallas import tpu as pltpu
from jax.sharding import PartitionSpec as P

BS = 64
CB = 8
GROUPS = 5
LANES = 128
BF = jnp.bfloat16
F32 = jnp.float32
MIB = 1 << 20

VM = pl.BlockSpec(memory_space=pltpu.VMEM)
SM = pl.BlockSpec(memory_space=pltpu.SMEM)


def params(mib):
    return pltpu.CompilerParams(vmem_limit_bytes=mib * MIB)


def low_lanes(rows):
    return lax.broadcasted_iota(jnp.int32, (rows, LANES), 1) < BS


def dot(a, b):
    return lax.dot_general(a, b, (((1,), (0,)), ((), ())), preferred_element_type=F32)


def relayout_kernel(x_ref, o_ref, scr):
    rows, nb, _ = x_ref.shape
    low = low_lanes(32)
    for r in range(rows):
        for q in range(32):
            scr[r, pl.ds(q * 8, nb), :] = x_ref[r, :, q * LANES : (q + 1) * LANES].astype(F32)
        for k in range(0, nb, 2):
            x0 = scr[r, pl.ds(k, 32, stride=8), :]
            x1 = scr[r, pl.ds(k + 1, 32, stride=8), :]
            o_ref[r, 0:32, k * BS : (k + 2) * BS] = jnp.where(low, x0, pltpu.roll(x1, BS, 1)).astype(BF)
            o_ref[r, 32:64, k * BS : (k + 2) * BS] = jnp.where(low, pltpu.roll(x0, BS, 1), x1).astype(BF)


def relayout(x, first, rows):
    nb = x.shape[1]
    step = 4
    return pl.pallas_call(
        relayout_kernel,
        grid=(rows // step,),
        out_shape=jax.ShapeDtypeStruct((rows, BS, nb * BS), BF),
        in_specs=[pl.BlockSpec((step, nb, BS * BS), lambda i: (i + first // step, 0, 0))],
        out_specs=pl.BlockSpec((step, BS, nb * BS), lambda i: (i, 0, 0)),
        scratch_shapes=[pltpu.VMEM((step, 256, LANES), F32)],
        compiler_params=params(16),
        name="relayout",
    )(x)


def left_kernel(rb, chunks, pct_ref, pl_ref, o_ref):
    slab = lax.axis_index("row")
    ac = BS // chunks
    low = low_lanes(4 * BS)
    o_ref[...] = jnp.zeros_like(o_ref)

    def pair(ip, carry):
        for half in range(2):
            i = ip * 2 + half
            x = pl_ref[i].astype(F32)
            xt = jnp.concatenate([x, x], axis=0).T
            keep = jnp.where(low if half == 0 else jnp.logical_not(low), xt, 0.0)
            for s in range(4):
                w = pct_ref[s, slab * rb + i] - (slab - 1) * CB
                place = jnp.where(w < CB, w, jnp.where(w < 2 * CB, w + CB, w - CB))
                for ch in range(chunks):
                    piece = keep[s * BS + ch * ac : s * BS + (ch + 1) * ac]
                    old = o_ref[ch, ip, place].astype(F32)
                    o_ref[ch, ip, place] = (old + piece).astype(BF)
        return carry

    lax.fori_loop(0, rb // 2, pair, 0)


def left_factor(pct, p_own, chunks):
    rb = p_own.shape[0]
    return pl.pallas_call(
        functools.partial(left_kernel, rb, chunks),
        out_shape=jax.ShapeDtypeStruct((chunks, rb // 2, 3 * CB, BS // chunks, LANES), BF),
        in_specs=[SM, VM],
        out_specs=VM,
        compiler_params=params(24),
        name="left_factor",
    )(pct, p_own)


def right_kernel(rb, ka, nfb, share, tiles, pct_ref, cols_ref, counts_ref, own, pr, ps, nr, ns, o_ref, place_ref):
    slab = lax.axis_index("row")
    col = lax.axis_index("col")
    core = lax.rem(col, 2)
    half = rb // 2
    base = (slab - 1) * rb
    low1 = lax.broadcasted_iota(jnp.int32, (1, LANES), 1) < BS
    low = low_lanes(BS)
    rows = lax.broadcasted_iota(jnp.int32, (BS, BS), 0)
    cols = lax.broadcasted_iota(jnp.int32, (BS, BS), 1)
    order = (rows == 2 * lax.rem(cols, 32) + cols // 32).astype(F32).astype(BF)

    def window(n):
        if n >= GROUPS * share:
            return jnp.int32(-7)
        return CB * (n % GROUPS) + share * col + n // GROUPS

    wants = [jnp.where(low1, window(p), window(tiles + p)) for p in range(tiles)]

    def fill(src, count, near_first, out_first):
        def one(jj, carry):
            fine = base + near_first + jj
            valid = (fine >= 0) & (fine < nfb)
            at = jnp.clip(fine, 0, nfb - 1)
            x = dot(order, src[jj])
            dups = []
            for t in range(0, 4, 2):
                pair = x[:, t * BS : (t + 2) * BS]
                swapped = pltpu.roll(pair, BS, 1)
                dups += [jnp.where(low, pair, swapped), jnp.where(low, swapped, pair)]
            idx = [jnp.where(valid, pct_ref[t, at] - (slab - 2) * CB, -1000000) for t in range(4)]
            for p in range(tiles):
                total = jnp.zeros((BS, LANES), F32)
                for t in range(4):
                    total = total + jnp.where(wants[p] == idx[t], dups[t], 0.0)
                o_ref[out_first + jj, :, p * LANES : (p + 1) * LANES] = total.astype(BF)
            return carry

        lax.fori_loop(0, count, one, 0)

    fill(own, rb, rb, 0)
    fill(pr, half, half * core, rb)
    fill(ps, half, half * (1 - core), rb + half)
    fill(nr, half, 2 * rb + half * core, 2 * rb)
    fill(ns, half, 2 * rb + half * (1 - core), 2 * rb + half)
    o_ref[3 * rb] = jnp.zeros((BS, tiles * LANES), BF)

    def places(i, carry):
        live = counts_ref[i]
        for k in range(ka):
            near = cols_ref[i, k] - base
            side = near // rb
            inside = near - side * rb
            far = lax.div(inside, half)
            off = inside - half * far + half * lax.rem(far + core, 2)
            spot = jnp.where(side == 1, inside, jnp.where(side == 0, rb + off, 2 * rb + off))
            place_ref[i, k] = jnp.where(k < live, spot, 3 * rb)
        return carry

    lax.fori_loop(0, rb, places, 0)


def right_factor(pct, a_cols, counts, pieces, nfb, share, tiles):
    rb, ka = a_cols.shape
    return pl.pallas_call(
        functools.partial(right_kernel, rb, ka, nfb, share, tiles),
        out_shape=(
            jax.ShapeDtypeStruct((3 * rb + 1, BS, tiles * LANES), BF),
            jax.ShapeDtypeStruct((rb, ka), jnp.int32),
        ),
        in_specs=[SM, SM, SM] + [VM] * 5,
        out_specs=(VM, SM),
        compiler_params=params(24),
        name="right_factor",
    )(pct, a_cols, counts, *pieces)


def product_kernel(first, shifts, has_acc, ks, place_ref, right_ref, *refs):
    col = lax.axis_index("col")
    ny = lax.axis_size("col") // 2
    srcs = refs[: len(shifts)]
    acc_ref = refs[len(shifts)] if has_acc else None
    o_ref = refs[-1]
    rows = o_ref.shape[0]
    width = o_ref.shape[2]
    y, core = col // 2, lax.rem(col, 2)
    firsts = []
    for s, flip in shifts:
        c = core if flip == 0 else 1 - core
        firsts.append((lax.rem(y - s + ny, ny) * 2 + c) * ks)

    def one(i, carry):
        spots = [[place_ref[first + i, f + k] for k in range(ks)] for f in firsts]
        for n0 in range(0, width, 256):
            n1 = min(n0 + 256, width)
            acc = acc_ref[i, :, n0:n1] if has_acc else jnp.zeros((BS, n1 - n0), F32)
            for src, spot in zip(srcs, spots):
                for k in range(0, ks, 4):
                    lhs = src[i, :, k * BS : (k + 4) * BS]
                    rhs = jnp.concatenate([right_ref[spot[k + d], :, n0:n1] for d in range(4)], axis=0)
                    acc = acc + dot(lhs, rhs)
            o_ref[i, :, n0:n1] = acc.astype(o_ref.dtype)
        return carry

    lax.fori_loop(0, rows, one, 0)


def product(place, right, srcs, shifts, first, acc, dtype):
    rows, _, wide = srcs[0].shape
    return pl.pallas_call(
        functools.partial(product_kernel, first, shifts, acc is not None, wide // BS),
        out_shape=jax.ShapeDtypeStruct((rows, BS, right.shape[2]), dtype),
        in_specs=[SM, VM] + [VM] * (len(srcs) + (acc is not None)),
        out_specs=VM,
        compiler_params=params(24),
        name="product",
    )(place, right, *srcs, *([] if acc is None else [acc]))


def coarse_kernel(sets, left_ref, *refs):
    aps = refs[:2]
    outs = refs[2 : 2 + len(sets)]
    scr = refs[-1]
    ac = left_ref.shape[3]
    half = aps[0].shape[0]
    tiles = aps[0].shape[2] // LANES
    low = low_lanes(CB)
    for out, part in zip(outs, sets):
        for n0 in range(0, tiles * LANES, 256):
            n1 = min(n0 + 256, tiles * LANES)
            acc = jnp.zeros((CB * ac, n1 - n0), F32)
            for side, ap in enumerate(aps):
                for g in range(0, half // 2, 2):
                    ip = side * (half // 2) + g
                    lhs = jnp.concatenate(
                        [left_ref[0, ip + d, part * CB : (part + 1) * CB].reshape(CB * ac, LANES) for d in range(2)],
                        axis=1,
                    )
                    rhs = ap[2 * g : 2 * g + 4, :, n0:n1].reshape(4 * BS, n1 - n0)
                    acc = acc + dot(lhs, rhs)
            for p in range(n0 // LANES, n1 // LANES):
                scr[p] = acc[:, p * LANES - n0 : (p + 1) * LANES - n0]
        for p in range(tiles):
            for a in range(0, ac, 2):
                x0 = scr[p, pl.ds(a, CB, stride=ac), :]
                x1 = scr[p, pl.ds(a + 1, CB, stride=ac), :]
                at = slice(a * BS, (a + 2) * BS)
                out[p, :, at] = jnp.where(low, x0, pltpu.roll(x1, BS, 1)).astype(out.dtype)
                out[tiles + p, :, at] = jnp.where(low, pltpu.roll(x0, BS, 1), x1).astype(out.dtype)


def coarse_parts(left, aps, chunk, sets, dtype):
    _, pairs, spots, ac, _ = left.shape
    tiles = aps[0].shape[2] // LANES
    shape = jax.ShapeDtypeStruct((2 * tiles, CB, ac * BS), dtype)
    return pl.pallas_call(
        functools.partial(coarse_kernel, sets),
        grid=(1,),
        out_shape=[shape] * len(sets),
        in_specs=[pl.BlockSpec((1, pairs, spots, ac, LANES), lambda i: (chunk, 0, 0, 0, 0))] + [VM] * 2,
        out_specs=[pl.BlockSpec(shape.shape, lambda i: (0, 0, 0))] * len(sets),
        scratch_shapes=[pltpu.VMEM((tiles, CB * ac, LANES), F32)],
        compiler_params=params(32),
        name="coarse",
    )(left, *aps)


def assemble_kernel(order_ref, *refs):
    out = refs[-1]
    srcs = refs[:-1] if len(refs) % 2 else refs[1:-1]
    x = jnp.concatenate([s[...].reshape(-1, s.shape[2]) for s in srcs], axis=0)
    res = dot(order_ref[...], x)
    wide = out.shape[1]
    for i in range(CB):
        out[i] = res[i * wide : (i + 1) * wide].astype(BF)


def assemble(order, srcs, chunk, total, before):
    n, _, lanes = srcs[0].shape
    step = 512
    per = lanes // step
    wide = n * len(srcs)
    specs = [pl.BlockSpec(order.shape, lambda i: (0, 0))]
    args = [order]
    alias = {}
    if before is not None:
        specs.append(pl.BlockSpec(memory_space=pl.ANY))
        args.append(before)
        alias = {1: 0}
    specs += [pl.BlockSpec((n, CB, step), lambda i: (0, 0, i))] * len(srcs)
    return pl.pallas_call(
        assemble_kernel,
        grid=(per,),
        out_shape=jax.ShapeDtypeStruct((CB, wide, total), BF),
        in_specs=specs,
        out_specs=pl.BlockSpec((CB, wide, step), lambda i: (0, 0, chunk * per + i)),
        input_output_aliases=alias,
        compiler_params=params(24),
        name="assemble",
    )(*args, *srcs)


def assembly_order(shifts, ncol, share):
    col = lax.axis_index("col")
    y, core = col // 2, col % 2
    groups = GROUPS + 2
    size = ncol * share * groups * CB
    out_row = lax.broadcasted_iota(jnp.int32, (size, size), 0)
    src_row = lax.broadcasted_iota(jnp.int32, (size, size), 1)
    per = share * groups * CB
    which, rest = src_row // per, src_row % per
    e, g, i = rest // (groups * CB), rest // CB % groups, rest % CB
    src_col = jnp.zeros_like(which)
    for z, (s, flip) in enumerate(shifts):
        c = (y - s) % (ncol // 2) * 2 + (core + flip) % 2
        src_col = jnp.where(which == z, c, src_col)
    return (out_row == i * (groups * CB) + g * CB + share * src_col + e).astype(BF)


def body(a_blocks, a_cols, counts, p_blocks, p_cols):
    rb, ks, _ = a_blocks.shape
    nrow, ncol = lax.axis_size("row"), lax.axis_size("col")
    ny = ncol // 2
    nfb = p_cols.shape[0]
    share = CB // ncol
    tiles = (GROUPS * share + 1) // 2
    half = rb // 2
    chunks = 2
    core = lax.axis_index("col") % 2

    def over_y(x, s):
        return lax.ppermute(x, "col", [(y * 2 + c, (y + s) % ny * 2 + c) for y in range(ny) for c in range(2)])

    def over_core(x):
        return lax.ppermute(x, "col", [(c, c ^ 1) for c in range(ncol)])

    def upward(x):
        return lax.ppermute(x, "row", [(i, i + 1) for i in range(nrow - 1)])

    def downward(x):
        return lax.ppermute(x, "row", [(i + 1, i) for i in range(nrow - 1)])

    shifts = tuple((s, f) for s in range(ny) for f in range(2))
    pct = p_cols.T

    def gather(x):
        got = [x] + [over_y(x, s) for s in range(1, ny)]
        return [z for g in got for z in (g, over_core(g))]

    a_parts = [gather(relayout(a_blocks, h * half, half)) for h in range(2)]
    p_own = relayout(p_blocks, 0, rb)
    mine = lax.dynamic_slice_in_dim(p_own, core * half, half, 0)
    prev, after = upward(mine), downward(mine)
    pieces = [p_own, prev, over_core(prev), after, over_core(after)]
    left = left_factor(pct, p_own, chunks)
    order = assembly_order(shifts, ncol, share)
    right, place = right_factor(pct, a_cols, counts, pieces, nfb, share, tiles)
    aps = []
    for h in range(2):
        near = product(place, right, a_parts[h][:2], shifts[:2], h * half, None, F32)
        aps.append(product(place, right, a_parts[h][2:], shifts[2:], h * half, near, BF))

    def columns(x, g):
        y = x[: GROUPS * share].reshape((share, GROUPS) + x.shape[1:])
        return jnp.pad(y.astype(F32), ((0, 0), (g, 2 - g), (0, 0), (0, 0)))

    rims = [coarse_parts(left, aps, ch, (0, 1), BF) for ch in range(chunks)]
    mids = [coarse_parts(left, aps, ch, (2,), F32)[0] for ch in range(chunks)]
    out = None
    for ch in range(chunks):
        low, high = rims[ch]
        total = columns(upward(high), 0) + columns(mids[ch], 1) + columns(downward(low), 2)
        total = total.astype(BF).reshape((share * (GROUPS + 2),) + total.shape[2:])
        out = assemble(order, gather(total), ch, BS * BS, out)
    return out


def solution(mesh):
    return jax.shard_map(
        body,
        mesh=mesh,
        in_specs=(P("row", "col", None), P("row", None), P("row"), P("row", None, None), P()),
        out_specs=P("row", None, None),
        check_vma=False,
    )
```

```python
import functools

import jax
import jax.numpy as jnp
from jax import lax
from jax.experimental import pallas as pl
from jax.experimental.pallas import tpu as pltpu
from jax.sharding import PartitionSpec as P

BS = 64
CB = 8
GROUPS = 5
LANES = 128
BF = jnp.bfloat16
F32 = jnp.float32
MIB = 1 << 20

VM = pl.BlockSpec(memory_space=pltpu.VMEM)
SM = pl.BlockSpec(memory_space=pltpu.SMEM)


def params(mib):
    return pltpu.CompilerParams(vmem_limit_bytes=mib * MIB)


def cost(us):
    return pl.CostEstimate(flops=0, bytes_accessed=int(us * 3.7e6), transcendentals=0)


def low_lanes(rows):
    return lax.broadcasted_iota(jnp.int32, (rows, LANES), 1) < BS


def dot(a, b):
    return lax.dot_general(a, b, (((1,), (0,)), ((), ())), preferred_element_type=F32)


def relayout_kernel(x_ref, o_ref, scr):
    rows, nb, _ = x_ref.shape
    low = low_lanes(32)
    for r in range(rows):
        for q in range(32):
            scr[r, pl.ds(q * 8, nb), :] = x_ref[r, :, q * LANES : (q + 1) * LANES].astype(F32)
        for k in range(0, nb, 2):
            x0 = scr[r, pl.ds(k, 32, stride=8), :]
            x1 = scr[r, pl.ds(k + 1, 32, stride=8), :]
            o_ref[r, 0:32, k * BS : (k + 2) * BS] = jnp.where(low, x0, pltpu.roll(x1, BS, 1)).astype(BF)
            o_ref[r, 32:64, k * BS : (k + 2) * BS] = jnp.where(low, pltpu.roll(x0, BS, 1), x1).astype(BF)


def relayout(x, first, rows):
    nb = x.shape[1]
    step = 4
    return pl.pallas_call(
        relayout_kernel,
        grid=(rows // step,),
        out_shape=jax.ShapeDtypeStruct((rows, BS, nb * BS), BF),
        in_specs=[pl.BlockSpec((step, nb, BS * BS), lambda i: (i + first // step, 0, 0))],
        out_specs=pl.BlockSpec((step, BS, nb * BS), lambda i: (i, 0, 0)),
        scratch_shapes=[pltpu.VMEM((step, 256, LANES), F32)],
        compiler_params=params(16),
        cost_estimate=cost(0.6),
        name="relayout",
    )(x)


def relayout_both_kernel(x_ref, o_ref, nat_ref, scr, mix):
    relayout_kernel(x_ref, o_ref, scr)
    rows, nb, _ = x_ref.shape
    for r in range(rows):
        for k in range(0, nb, 2):
            at = slice(k * BS, (k + 2) * BS)
            mix[r, k // 2, pl.ds(0, 32, stride=2), :] = o_ref[r, 0:32, at].astype(F32)
            mix[r, k // 2, pl.ds(1, 32, stride=2), :] = o_ref[r, 32:64, at].astype(F32)
            nat_ref[r, :, at] = mix[r, k // 2].astype(BF)


def relayout_both(x):
    rows, nb, _ = x.shape
    step = 4
    shape = jax.ShapeDtypeStruct((rows, BS, nb * BS), BF)
    spec = pl.BlockSpec((step, BS, nb * BS), lambda i: (i, 0, 0))
    return pl.pallas_call(
        relayout_both_kernel,
        grid=(rows // step,),
        out_shape=(shape, shape),
        in_specs=[pl.BlockSpec((step, nb, BS * BS), lambda i: (i, 0, 0))],
        out_specs=(spec, spec),
        scratch_shapes=[pltpu.VMEM((step, 256, LANES), F32), pltpu.VMEM((step, nb // 2, BS, LANES), F32)],
        compiler_params=params(16),
        cost_estimate=cost(1.5),
        name="relayout_both",
    )(x)


def left_kernel(rb, pct_ref, pl_ref, o_ref):
    slab = lax.axis_index("row")
    low = low_lanes(4 * BS)
    o_ref[...] = jnp.zeros_like(o_ref)

    def pair(ip, carry):
        for half in range(2):
            i = ip * 2 + half
            x = pl_ref[i].astype(F32)
            xt = jnp.concatenate([x, x], axis=0).T
            keep = jnp.where(low if half == 0 else jnp.logical_not(low), xt, 0.0)
            for s in range(4):
                w = pct_ref[s, slab * rb + i] - (slab - 1) * CB
                o_ref[ip, w] = (o_ref[ip, w].astype(F32) + keep[s * BS : (s + 1) * BS]).astype(BF)
        return carry

    lax.fori_loop(0, rb // 2, pair, 0)


def left_factor(pct, p_own):
    rb = p_own.shape[0]
    return pl.pallas_call(
        functools.partial(left_kernel, rb),
        out_shape=jax.ShapeDtypeStruct((rb // 2, 3 * CB, BS, LANES), BF),
        in_specs=[SM, VM],
        out_specs=VM,
        compiler_params=params(24),
        cost_estimate=cost(2.9),
        name="left_factor",
    )(pct, p_own)


def right_kernel(rb, nfb, share, tiles, pct_ref, own, pr, ps, nr, ns, o_ref):
    slab = lax.axis_index("row")
    col = lax.axis_index("col")
    core = lax.rem(col, 2)
    half = rb // 2
    base = (slab - 1) * rb
    low = low_lanes(BS)

    def fill(src, count, near_first, out_first):
        def one(jj, carry):
            fine = base + near_first + jj
            valid = (fine >= 0) & (fine < nfb)
            at = jnp.clip(fine, 0, nfb - 1)
            spot = out_first + jj
            for p in range(tiles):
                o_ref[spot, p] = jnp.zeros((BS, LANES), BF)
            for t in range(4):
                w = pct_ref[t, at] - (slab - 2) * CB
                e = (w & (CB - 1)) - share * col

                @pl.when(valid & (e >= 0) & (e < share))
                def _():
                    n = e * GROUPS + (w >> 3)
                    upper = n >= tiles
                    tile = jnp.where(upper, n - tiles, n)
                    pair = src[jj, :, t // 2 * LANES : (t // 2 + 1) * LANES].astype(F32)
                    other = pltpu.roll(pair, BS, 1)
                    both = jnp.where(low, pair, other) if t % 2 == 0 else jnp.where(low, other, pair)
                    keep = jnp.where(low == jnp.logical_not(upper), both, 0.0)
                    o_ref[spot, tile] = (o_ref[spot, tile].astype(F32) + keep).astype(BF)

            return carry

        lax.fori_loop(0, count, one, 0)

    fill(own, rb, rb, 0)
    fill(pr, half, half * core, rb)
    fill(ps, half, half * (1 - core), rb + half)
    fill(nr, half, 2 * rb + half * core, 2 * rb)
    fill(ns, half, 2 * rb + half * (1 - core), 2 * rb + half)
    o_ref[3 * rb] = jnp.zeros((tiles, BS, LANES), BF)


def right_factor(pct, pieces, nfb, share, tiles):
    rb = pieces[0].shape[0]
    return pl.pallas_call(
        functools.partial(right_kernel, rb, nfb, share, tiles),
        out_shape=jax.ShapeDtypeStruct((3 * rb + 1, tiles, BS, LANES), BF),
        in_specs=[SM] + [VM] * 5,
        out_specs=VM,
        compiler_params=params(24),
        cost_estimate=cost(4.0),
        name="right_factor",
    )(pct, *pieces)


def slot_places(a_cols, counts):
    rb, ka = a_cols.shape
    half = rb // 2
    core = lax.axis_index("col") % 2
    near = a_cols - (lax.axis_index("row") - 1) * rb
    before, behind = near < rb, near >= 2 * rb
    inside = near - jnp.where(before, 0, jnp.where(behind, 2 * rb, rb))
    far = (inside >= half).astype(jnp.int32)
    off = inside - half * far + half * jnp.where(far == core, 0, 1)
    spot = jnp.where(before, rb + off, jnp.where(behind, 2 * rb + off, inside))
    live = jnp.arange(ka, dtype=jnp.int32)[None, :] < counts[:, None]
    return jnp.where(live, spot, 3 * rb)


def product_kernel(first, shifts, has_acc, ks, place_ref, right_ref, *refs):
    col = lax.axis_index("col")
    ny = lax.axis_size("col") // 2
    srcs = refs[: len(shifts)]
    acc_ref = refs[len(shifts)] if has_acc else None
    o_ref = refs[-1]
    rows = o_ref.shape[0]
    tiles = right_ref.shape[1]
    y, core = col // 2, lax.rem(col, 2)
    firsts = []
    for s, flip in shifts:
        c = core if flip == 0 else 1 - core
        firsts.append((lax.rem(y - s + ny, ny) * 2 + c) * ks)

    def one(i, carry):
        spots = [[place_ref[first + i, f + k] for k in range(ks)] for f in firsts]
        for p0 in range(0, tiles, 2):
            ps = range(p0, min(p0 + 2, tiles))
            at = slice(p0 * LANES, (ps[-1] + 1) * LANES)
            acc = acc_ref[i, :, at] if has_acc else jnp.zeros((BS, len(ps) * LANES), F32)
            for src, spot in zip(srcs, spots):
                for k in range(0, ks, 4):
                    rhs = [jnp.concatenate([right_ref[spot[k + d], p] for d in range(4)], axis=0) for p in ps]
                    acc = acc + dot(src[i, :, k * BS : (k + 4) * BS], jnp.concatenate(rhs, axis=1))
            o_ref[i, :, at] = acc.astype(o_ref.dtype)
        return carry

    lax.fori_loop(0, rows, one, 0, unroll=4)


def product(place, right, srcs, shifts, first, acc, dtype):
    rows, _, wide = srcs[0].shape
    return pl.pallas_call(
        functools.partial(product_kernel, first, shifts, acc is not None, wide // BS),
        out_shape=jax.ShapeDtypeStruct((rows, BS, right.shape[1] * LANES), dtype),
        in_specs=[SM, VM] + [VM] * (len(srcs) + (acc is not None)),
        out_specs=VM,
        compiler_params=params(24),
        cost_estimate=cost(4.0),
        name="product",
    )(place, right, *srcs, *([] if acc is None else [acc]))


def coarse_kernel(sets, a0, a1, left_ref, *refs):
    outs = refs[-1 - len(sets) : -1]
    aps = refs[: -1 - len(sets)]
    scr = refs[-1]
    ac = a1 - a0
    half = aps[0].shape[0]
    tiles = aps[0].shape[2] // LANES
    for out, (i0, i1) in zip(outs, sets):
        rows = i1 - i0
        low = low_lanes(rows)
        for p0 in range(0, tiles, 2):
            p1 = min(p0 + 2, tiles)
            acc = jnp.zeros((rows * ac, (p1 - p0) * LANES), F32)
            for side, ap in enumerate(aps):
                for g in range(0, half // 2, 2):
                    ip = side * (half // 2) + g
                    lhs = [left_ref[ip + d, i0:i1, a0:a1].reshape(rows * ac, LANES) for d in range(2)]
                    rhs = ap[2 * g : 2 * g + 4, :, p0 * LANES : p1 * LANES].reshape(4 * BS, (p1 - p0) * LANES)
                    acc = acc + dot(jnp.concatenate(lhs, axis=1), rhs)
            for p in range(p0, p1):
                scr[p, 0 : rows * ac] = acc[:, (p - p0) * LANES : (p - p0 + 1) * LANES]
        for p in range(tiles):
            for a in range(0, ac, 2):
                x0 = scr[p, pl.ds(a, rows, stride=ac), :]
                x1 = scr[p, pl.ds(a + 1, rows, stride=ac), :]
                at = slice(a * BS, (a + 2) * BS)
                out[p, :, at] = jnp.where(low, x0, pltpu.roll(x1, BS, 1)).astype(out.dtype)
                out[tiles + p, :, at] = jnp.where(low, pltpu.roll(x0, BS, 1), x1).astype(out.dtype)


def coarse_rows(left, aps, sets, a0, a1, dtype, us):
    tiles = aps[0].shape[2] // LANES
    return pl.pallas_call(
        functools.partial(coarse_kernel, sets, a0, a1),
        out_shape=[jax.ShapeDtypeStruct((2 * tiles, i1 - i0, (a1 - a0) * BS), dtype) for i0, i1 in sets],
        in_specs=[VM] * (1 + len(aps)),
        out_specs=[VM] * len(sets),
        scratch_shapes=[pltpu.VMEM((tiles, max(i1 - i0 for i0, i1 in sets) * (a1 - a0), LANES), F32)],
        compiler_params=params(32),
        cost_estimate=cost(us),
        name="coarse",
    )(left, *aps)


def assemble_kernel(order_ref, *refs):
    out = refs[-1]
    srcs = refs[:-1] if len(refs) % 2 else refs[1:-1]
    x = jnp.concatenate([s[...].reshape(-1, s.shape[2]) for s in srcs], axis=0)
    res = dot(order_ref[...], x)
    wide = out.shape[1]
    for i in range(CB):
        out[i] = res[i * wide : (i + 1) * wide].astype(BF)


def assemble(order, srcs, a0, total, before):
    n, _, lanes = srcs[0].shape
    step = 512
    per = lanes // step
    wide = n * len(srcs)
    specs = [pl.BlockSpec(order.shape, lambda i: (0, 0))]
    args = [order]
    alias = {}
    if before is not None:
        specs.append(pl.BlockSpec(memory_space=pl.ANY))
        args.append(before)
        alias = {1: 0}
    specs += [pl.BlockSpec((n, CB, step), lambda i: (0, 0, i))] * len(srcs)
    return pl.pallas_call(
        assemble_kernel,
        grid=(per,),
        out_shape=jax.ShapeDtypeStruct((CB, wide, total), BF),
        in_specs=specs,
        out_specs=pl.BlockSpec((CB, wide, step), lambda i: (0, 0, a0 * BS // step + i)),
        input_output_aliases=alias,
        compiler_params=params(24),
        cost_estimate=cost(2.9),
        name="assemble",
    )(*args, *srcs)


def assembly_order(shifts, ncol, share):
    col = lax.axis_index("col")
    y, core = col // 2, col % 2
    groups = GROUPS + 2
    size = ncol * share * groups * CB
    out_row = lax.broadcasted_iota(jnp.int32, (size, size), 0)
    src_row = lax.broadcasted_iota(jnp.int32, (size, size), 1)
    per = share * groups * CB
    which, rest = src_row // per, src_row % per
    e, g, i = rest // (groups * CB), rest // CB % groups, rest % CB
    src_col = jnp.zeros_like(which)
    for z, (s, flip) in enumerate(shifts):
        c = (y - s) % (ncol // 2) * 2 + (core + flip) % 2
        src_col = jnp.where(which == z, c, src_col)
    return (out_row == i * (groups * CB) + g * CB + share * src_col + e).astype(BF)


def body(a_blocks, a_cols, counts, p_blocks, p_cols):
    rb, ks, _ = a_blocks.shape
    nrow, ncol = lax.axis_size("row"), lax.axis_size("col")
    ny = ncol // 2
    nfb = p_cols.shape[0]
    share = CB // ncol
    tiles = (GROUPS * share + 1) // 2
    half = rb // 2
    chunks = ((0, 32), (32, 64))
    core = lax.axis_index("col") % 2

    def over_y(x, s):
        return lax.ppermute(x, "col", [(y * 2 + c, (y + s) % ny * 2 + c) for y in range(ny) for c in range(2)])

    def over_core(x):
        return lax.ppermute(x, "col", [(c, c ^ 1) for c in range(ncol)])

    def upward(x):
        return lax.ppermute(x, "row", [(i, i + 1) for i in range(nrow - 1)])

    def downward(x):
        return lax.ppermute(x, "row", [(i + 1, i) for i in range(nrow - 1)])

    shifts = tuple((s, f) for s in range(ny) for f in range(2))
    pct = p_cols.T

    def gather(x):
        got = [x] + [over_y(x, s) for s in range(1, ny)]
        return [z for g in got for z in (g, over_core(g))]

    a_parts = [gather(relayout(a_blocks, h * half, half)) for h in range(2)]
    p_mixed, p_own = relayout_both(p_blocks)
    mine = lax.dynamic_slice_in_dim(p_own, core * half, half, 0)
    prev, after = upward(mine), downward(mine)
    left = left_factor(pct, p_mixed)
    order = assembly_order(shifts, ncol, share)
    place = slot_places(a_cols, counts)
    pieces = [p_own, prev, over_core(prev), after, over_core(after)]
    right = right_factor(pct, pieces, nfb, share, tiles)
    aps = []
    for h in range(2):
        near = product(place, right, a_parts[h][:2], shifts[:2], h * half, None, F32)
        aps.append(product(place, right, a_parts[h][2:], shifts[2:], h * half, near, BF))
        if h == 0:
            early = downward(coarse_rows(left, aps, ((0, CB // 2),), 0, BS, BF, 1.0)[0])

    def columns(x, g):
        y = x[: GROUPS * share].reshape((share, GROUPS) + x.shape[1:])
        return jnp.pad(y.astype(F32), ((0, 0), (g, 2 - g), (0, 0), (0, 0)))

    rims = [coarse_rows(left, aps, ((CB // 2, CB), (2 * CB, 3 * CB)), a0, a1, BF, 2.0) for a0, a1 in chunks]
    mids = [coarse_rows(left, aps, ((CB, 2 * CB),), a0, a1, F32, 1.0)[0] for a0, a1 in chunks]
    out = None
    for (a0, a1), (low, high), mid in zip(chunks, rims, mids):
        lower = jnp.concatenate([early[:, :, a0 * BS : a1 * BS], downward(low)], axis=1)
        total = columns(upward(high), 0) + columns(mid, 1) + columns(lower, 2)
        total = total.astype(BF).reshape((share * (GROUPS + 2),) + total.shape[2:])
        out = assemble(order, gather(total), a0, BS * BS, out)
    return out


def solution(mesh):
    return jax.shard_map(
        body,
        mesh=mesh,
        in_specs=(P("row", "col", None), P("row", None), P("row"), P("row", None, None), P()),
        out_specs=P("row", None, None),
        check_vma=False,
    )
```

```python
import functools

import jax
import jax.numpy as jnp
from jax import lax
from jax.experimental import pallas as pl
from jax.experimental.pallas import tpu as pltpu
from jax.sharding import PartitionSpec as P

BS = 64
CB = 8
GROUPS = 5
LANES = 128
BF = jnp.bfloat16
F32 = jnp.float32
MIB = 1 << 20

VM = pl.BlockSpec(memory_space=pltpu.VMEM)
SM = pl.BlockSpec(memory_space=pltpu.SMEM)


def params(mib):
    return pltpu.CompilerParams(vmem_limit_bytes=mib * MIB)


def cost(us):
    return pl.CostEstimate(flops=int(us * 1e8), bytes_accessed=int(us * 3.7e6), transcendentals=0)


def low_lanes(rows):
    return lax.broadcasted_iota(jnp.int32, (rows, LANES), 1) < BS


def dot(a, b):
    return lax.dot_general(a, b, (((1,), (0,)), ((), ())), preferred_element_type=F32)


def relayout_kernel(x_ref, o_ref, scr):
    rows, nb, _ = x_ref.shape
    low = low_lanes(32)
    for r in range(rows):
        for q in range(32):
            scr[r, pl.ds(q * 8, nb), :] = x_ref[r, :, q * LANES : (q + 1) * LANES].astype(F32)
        for k in range(0, nb, 2):
            x0 = scr[r, pl.ds(k, 32, stride=8), :]
            x1 = scr[r, pl.ds(k + 1, 32, stride=8), :]
            o_ref[r, 0:32, k * BS : (k + 2) * BS] = jnp.where(low, x0, pltpu.roll(x1, BS, 1)).astype(BF)
            o_ref[r, 32:64, k * BS : (k + 2) * BS] = jnp.where(low, pltpu.roll(x0, BS, 1), x1).astype(BF)


def relayout(x, first, rows):
    nb = x.shape[1]
    step = 4
    return pl.pallas_call(
        relayout_kernel,
        grid=(rows // step,),
        out_shape=jax.ShapeDtypeStruct((rows, BS, nb * BS), BF),
        in_specs=[pl.BlockSpec((step, nb, BS * BS), lambda i: (i + first // step, 0, 0))],
        out_specs=pl.BlockSpec((step, BS, nb * BS), lambda i: (i, 0, 0)),
        scratch_shapes=[pltpu.VMEM((step, 256, LANES), F32)],
        compiler_params=params(16),
        cost_estimate=cost(0.6),
        name="relayout",
    )(x)


def relayout_both_kernel(x_ref, o_ref, nat_ref, scr, mix):
    relayout_kernel(x_ref, o_ref, scr)
    rows, nb, _ = x_ref.shape
    for r in range(rows):
        for k in range(0, nb, 2):
            at = slice(k * BS, (k + 2) * BS)
            mix[r, k // 2, pl.ds(0, 32, stride=2), :] = o_ref[r, 0:32, at].astype(F32)
            mix[r, k // 2, pl.ds(1, 32, stride=2), :] = o_ref[r, 32:64, at].astype(F32)
            nat_ref[r, :, at] = mix[r, k // 2].astype(BF)


def relayout_both(x):
    rows, nb, _ = x.shape
    step = 4
    shape = jax.ShapeDtypeStruct((rows, BS, nb * BS), BF)
    spec = pl.BlockSpec((step, BS, nb * BS), lambda i: (i, 0, 0))
    return pl.pallas_call(
        relayout_both_kernel,
        grid=(rows // step,),
        out_shape=(shape, shape),
        in_specs=[pl.BlockSpec((step, nb, BS * BS), lambda i: (i, 0, 0))],
        out_specs=(spec, spec),
        scratch_shapes=[pltpu.VMEM((step, 256, LANES), F32), pltpu.VMEM((step, nb // 2, BS, LANES), F32)],
        compiler_params=params(16),
        cost_estimate=cost(1.5),
        name="relayout_both",
    )(x)


def left_kernel(rb, pct_ref, pl_ref, o_ref):
    slab = lax.axis_index("row")
    low = low_lanes(4 * BS)
    o_ref[...] = jnp.zeros_like(o_ref)

    def pair(ip, carry):
        for half in range(2):
            i = ip * 2 + half
            x = pl_ref[i].astype(F32)
            xt = jnp.concatenate([x, x], axis=0).T
            keep = jnp.where(low if half == 0 else jnp.logical_not(low), xt, 0.0)
            for s in range(4):
                w = pct_ref[s, slab * rb + i] - (slab - 1) * CB
                o_ref[ip, w] = (o_ref[ip, w].astype(F32) + keep[s * BS : (s + 1) * BS]).astype(BF)
        return carry

    lax.fori_loop(0, rb // 2, pair, 0)


def left_factor(pct, p_own):
    rb = p_own.shape[0]
    return pl.pallas_call(
        functools.partial(left_kernel, rb),
        out_shape=jax.ShapeDtypeStruct((rb // 2, 3 * CB, BS, LANES), BF),
        in_specs=[SM, VM],
        out_specs=VM,
        compiler_params=params(24),
        cost_estimate=cost(2.9),
        name="left_factor",
    )(pct, p_own)


def column_table(pct, rb, share):
    slab = lax.axis_index("row")
    padded = jnp.pad(pct, ((0, 0), (rb, rb)), constant_values=-1000000)
    near = lax.dynamic_slice_in_dim(padded, slab * rb, 3 * rb, 1)
    w = near - (slab - 2) * CB
    e = (w & (CB - 1)) - share * lax.axis_index("col")
    return jnp.where((w >= 0) & (e >= 0) & (e < share), e * GROUPS + (w >> 3), -1)


def right_kernel(rb, tiles, table_ref, *refs):
    o_ref = refs[-1]
    core = lax.rem(lax.axis_index("col"), 2)
    low = lax.broadcasted_iota(jnp.int32, (1, LANES), 1) < BS
    wants = [jnp.where(low, p, tiles + p) for p in range(tiles)]

    def fill(src, count, near_first, out_first):
        def one(jj, carry):
            dups = []
            for t in range(4):
                x = src[jj, :, t * BS : (t + 1) * BS]
                dups.append(jnp.concatenate([x, x], axis=1))
            at = [table_ref[t, near_first + jj] for t in range(4)]
            for p in range(tiles):
                total = None
                for t in range(4):
                    keep = dups[t] * jnp.where(wants[p] == at[t], 1.0, 0.0).astype(BF)
                    total = keep if total is None else total + keep
                o_ref[out_first + jj, p] = total
            return carry

        lax.fori_loop(0, count, one, 0, unroll=4)

    if len(refs) == 2:
        fill(refs[0], rb, rb, 0)
        o_ref[rb] = jnp.zeros((tiles, BS, LANES), BF)
    else:
        done = refs[0].shape[0]

        def copy(jj, carry):
            o_ref[jj] = refs[0][jj]
            return carry

        lax.fori_loop(0, done, copy, 0)
        for z in range(2):
            there = core if z == 0 else 1 - core
            fill(refs[1 + z], rb, 2 * rb * there, done + rb * z)


def right_factor(table, srcs, tiles, us):
    rb = table.shape[1] // 3
    spots = rb + 1 if len(srcs) == 1 else 3 * rb + 1
    return pl.pallas_call(
        functools.partial(right_kernel, rb, tiles),
        out_shape=jax.ShapeDtypeStruct((spots, tiles, BS, LANES), BF),
        in_specs=[SM] + [VM] * len(srcs),
        out_specs=VM,
        compiler_params=params(24),
        cost_estimate=cost(us),
        name="right_factor",
    )(table, *srcs)


def slot_places(a_cols, counts):
    rb, ka = a_cols.shape
    core = lax.axis_index("col") % 2
    near = a_cols - (lax.axis_index("row") - 1) * rb
    before = near + jnp.where(core == 0, rb + 1, 2 * rb + 1)
    after = near - 2 * rb + jnp.where(core == 0, 2 * rb + 1, rb + 1)
    spot = jnp.where(near < rb, before, jnp.where(near >= 2 * rb, after, near - rb))
    live = jnp.arange(ka, dtype=jnp.int32)[None, :] < counts[:, None]
    return jnp.where(live, spot, rb)


def product_kernel(first, shifts, has_acc, ks, place_ref, right_ref, *refs):
    col = lax.axis_index("col")
    ny = lax.axis_size("col") // 2
    srcs = refs[: len(shifts)]
    acc_ref = refs[len(shifts)] if has_acc else None
    o_ref = refs[-1]
    rows = o_ref.shape[0]
    tiles = right_ref.shape[1]
    y, core = col // 2, lax.rem(col, 2)
    firsts = []
    for s, flip in shifts:
        c = core if flip == 0 else 1 - core
        firsts.append((lax.rem(y - s + ny, ny) * 2 + c) * ks)

    def one(i, carry):
        spots = [[place_ref[first + i, f + k] for k in range(ks)] for f in firsts]
        for p0 in range(0, tiles, 2):
            ps = range(p0, min(p0 + 2, tiles))
            at = slice(p0 * LANES, (ps[-1] + 1) * LANES)
            acc = acc_ref[i, :, at] if has_acc else jnp.zeros((BS, len(ps) * LANES), F32)
            for src, spot in zip(srcs, spots):
                for k in range(0, ks, 4):
                    rhs = [jnp.concatenate([right_ref[spot[k + d], p] for d in range(4)], axis=0) for p in ps]
                    acc = acc + dot(src[i, :, k * BS : (k + 4) * BS], jnp.concatenate(rhs, axis=1))
            o_ref[i, :, at] = acc.astype(o_ref.dtype)
        return carry

    lax.fori_loop(0, rows, one, 0, unroll=4)


def product(place, right, srcs, shifts, first, acc, dtype):
    rows, _, wide = srcs[0].shape
    return pl.pallas_call(
        functools.partial(product_kernel, first, shifts, acc is not None, wide // BS),
        out_shape=jax.ShapeDtypeStruct((rows, BS, right.shape[1] * LANES), dtype),
        in_specs=[SM, VM] + [VM] * (len(srcs) + (acc is not None)),
        out_specs=VM,
        compiler_params=params(24),
        cost_estimate=cost(4.0),
        name="product",
    )(place, right, *srcs, *([] if acc is None else [acc]))


def coarse_kernel(sets, a0, a1, left_ref, *refs):
    outs = refs[-1 - len(sets) : -1]
    aps = refs[: -1 - len(sets)]
    scr = refs[-1]
    ac = a1 - a0
    tiles = aps[0].shape[2] // LANES
    for out, (i0, i1) in zip(outs, sets):
        rows = i1 - i0
        low = low_lanes(rows)
        for p0 in range(0, tiles, 2):
            p1 = min(p0 + 2, tiles)
            acc = jnp.zeros((rows * ac, (p1 - p0) * LANES), F32)
            ip = 0
            for ap in aps:
                for g in range(0, ap.shape[0] // 2, 2):
                    lhs = [left_ref[ip + d, i0:i1, a0:a1].reshape(rows * ac, LANES) for d in range(2)]
                    rhs = ap[2 * g : 2 * g + 4, :, p0 * LANES : p1 * LANES].reshape(4 * BS, (p1 - p0) * LANES)
                    acc = acc + dot(jnp.concatenate(lhs, axis=1), rhs)
                    ip += 2
            for p in range(p0, p1):
                scr[p, 0 : rows * ac] = acc[:, (p - p0) * LANES : (p - p0 + 1) * LANES]
        for p in range(tiles):
            for a in range(0, ac, 2):
                x0 = scr[p, pl.ds(a, rows, stride=ac), :]
                x1 = scr[p, pl.ds(a + 1, rows, stride=ac), :]
                at = slice(a * BS, (a + 2) * BS)
                out[p, :, at] = jnp.where(low, x0, pltpu.roll(x1, BS, 1)).astype(out.dtype)
                out[tiles + p, :, at] = jnp.where(low, pltpu.roll(x0, BS, 1), x1).astype(out.dtype)


def coarse_rows(left, aps, sets, a0, a1, dtype, us):
    tiles = aps[0].shape[2] // LANES
    return pl.pallas_call(
        functools.partial(coarse_kernel, sets, a0, a1),
        out_shape=[jax.ShapeDtypeStruct((2 * tiles, i1 - i0, (a1 - a0) * BS), dtype) for i0, i1 in sets],
        in_specs=[VM] * (1 + len(aps)),
        out_specs=[VM] * len(sets),
        scratch_shapes=[pltpu.VMEM((tiles, max(i1 - i0 for i0, i1 in sets) * (a1 - a0), LANES), F32)],
        compiler_params=params(32),
        cost_estimate=cost(us),
        name="coarse",
    )(left, *aps)


def assemble_kernel(order_ref, *refs):
    out = refs[-1]
    srcs = refs[:-1] if len(refs) % 2 else refs[1:-1]
    x = jnp.concatenate([s[...].reshape(-1, s.shape[2]) for s in srcs], axis=0)
    res = dot(order_ref[...], x)
    wide = out.shape[1]
    for i in range(CB):
        out[i] = res[i * wide : (i + 1) * wide].astype(BF)


def assemble(order, srcs, a0, total, before):
    n, _, lanes = srcs[0].shape
    step = 512
    per = lanes // step
    wide = n * len(srcs)
    specs = [pl.BlockSpec(order.shape, lambda i: (0, 0))]
    args = [order]
    alias = {}
    if before is not None:
        specs.append(pl.BlockSpec(memory_space=pl.ANY))
        args.append(before)
        alias = {1: 0}
    specs += [pl.BlockSpec((n, CB, step), lambda i: (0, 0, i))] * len(srcs)
    return pl.pallas_call(
        assemble_kernel,
        grid=(per,),
        out_shape=jax.ShapeDtypeStruct((CB, wide, total), BF),
        in_specs=specs,
        out_specs=pl.BlockSpec((CB, wide, step), lambda i: (0, 0, a0 * BS // step + i)),
        input_output_aliases=alias,
        compiler_params=params(24),
        cost_estimate=cost(2.9),
        name="assemble",
    )(*args, *srcs)


def assembly_order(shifts, ncol, share):
    col = lax.axis_index("col")
    y, core = col // 2, col % 2
    groups = GROUPS + 2
    size = ncol * share * groups * CB
    out_row = lax.broadcasted_iota(jnp.int32, (size, size), 0)
    src_row = lax.broadcasted_iota(jnp.int32, (size, size), 1)
    per = share * groups * CB
    which, rest = src_row // per, src_row % per
    e, g, i = rest // (groups * CB), rest // CB % groups, rest % CB
    src_col = jnp.zeros_like(which)
    for z, (s, flip) in enumerate(shifts):
        c = (y - s) % (ncol // 2) * 2 + (core + flip) % 2
        src_col = jnp.where(which == z, c, src_col)
    return (out_row == i * (groups * CB) + g * CB + share * src_col + e).astype(BF)


def body(a_blocks, a_cols, counts, p_blocks, p_cols):
    rb, ks, _ = a_blocks.shape
    nrow, ncol = lax.axis_size("row"), lax.axis_size("col")
    ny = ncol // 2
    nfb = p_cols.shape[0]
    share = CB // ncol
    tiles = (GROUPS * share + 1) // 2
    parts = ((0, rb * 2 // 3), (rb * 2 // 3, rb // 3))
    chunks = ((0, 32), (32, 64))

    def outward(x):
        pairs = [(r * ncol + c, (r + 1 - 2 * (c % 2)) * ncol + c) for r in range(nrow) for c in range(ncol)]
        return lax.ppermute(x, ("row", "col"), [(a, b) for a, b in pairs if 0 <= b < nrow * ncol])

    def over_y(x, s):
        return lax.ppermute(x, "col", [(y * 2 + c, (y + s) % ny * 2 + c) for y in range(ny) for c in range(2)])

    def over_core(x):
        return lax.ppermute(x, "col", [(c, c ^ 1) for c in range(ncol)])

    def upward(x):
        return lax.ppermute(x, "row", [(i, i + 1) for i in range(nrow - 1)])

    def downward(x):
        return lax.ppermute(x, "row", [(i + 1, i) for i in range(nrow - 1)])

    shifts = tuple((s, f) for s in range(ny) for f in range(2))
    pct = p_cols.T

    def gather(x):
        got = [x] + [over_y(x, s) for s in range(1, ny)]
        return [z for g in got for z in (g, over_core(g))]

    own_a, side_a, far_a = [], [], []
    for h, (first, rows) in enumerate(parts):
        x = relayout(a_blocks, first, rows)
        own_a.append(x)
        far_a.append([over_y(x, s) for s in range(1, ny)])
        side_a.append(over_core(x))
        if h == 0:
            a_blocks, p_blocks, side_a[0] = lax.optimization_barrier((a_blocks, p_blocks, side_a[0]))
    p_mixed, p_own = relayout_both(p_blocks)
    beside = outward(p_own)
    p_mixed, p_own, side_a[1] = lax.optimization_barrier((p_mixed, p_own, side_a[1]))
    table = column_table(pct, rb, share)
    left = left_factor(pct, p_mixed)
    right = right_factor(table, [p_own], tiles, 2.0)
    order = assembly_order(shifts, ncol, share)
    place = slot_places(a_cols, counts)
    beside, left, right, order, place = lax.optimization_barrier((beside, left, right, order, place))
    right = right_factor(table, [right, beside, over_core(beside)], tiles, 4.0)
    near = [product(place, right, [own_a[h], side_a[h]], shifts[:2], parts[h][0], None, F32) for h in range(2)]
    far_a[1], near = lax.optimization_barrier((far_a[1], near))
    aps = []
    for h in range(2):
        srcs = [z for g in far_a[h] for z in (g, over_core(g))]
        aps.append(product(place, right, srcs, shifts[2:], parts[h][0], near[h], BF))
        if h == 0:
            early = downward(coarse_rows(left, aps, ((0, CB // 2),), 0, BS, BF, 1.0)[0])

    def columns(x, g):
        y = x[: GROUPS * share].reshape((share, GROUPS) + x.shape[1:])
        return jnp.pad(y.astype(F32), ((0, 0), (g, 2 - g), (0, 0), (0, 0)))

    rims = [coarse_rows(left, aps, ((CB // 2, CB), (2 * CB, 3 * CB)), a0, a1, BF, 2.0) for a0, a1 in chunks]
    mids = [coarse_rows(left, aps, ((CB, 2 * CB),), a0, a1, F32, 1.0)[0] for a0, a1 in chunks]
    out = None
    for (a0, a1), (low, high), mid in zip(chunks, rims, mids):
        lower = jnp.concatenate([early[:, :, a0 * BS : a1 * BS], downward(low)], axis=1)
        total = columns(upward(high), 0) + columns(mid, 1) + columns(lower, 2)
        total = total.astype(BF).reshape((share * (GROUPS + 2),) + total.shape[2:])
        out = assemble(order, gather(total), a0, BS * BS, out)
    return out


def solution(mesh):
    return jax.shard_map(
        body,
        mesh=mesh,
        in_specs=(P("row", "col", None), P("row", None), P("row"), P("row", None, None), P()),
        out_specs=P("row", None, None),
        check_vma=False,
    )
```

```python
import functools

import jax
import jax.numpy as jnp
from jax import lax
from jax.experimental import pallas as pl
from jax.experimental.pallas import tpu as pltpu
from jax.sharding import PartitionSpec as P

BS = 64
CB = 8
GROUPS = 5
LANES = 128
BF = jnp.bfloat16
F32 = jnp.float32
MIB = 1 << 20

VM = pl.BlockSpec(memory_space=pltpu.VMEM)
SM = pl.BlockSpec(memory_space=pltpu.SMEM)


def params(mib):
    return pltpu.CompilerParams(vmem_limit_bytes=mib * MIB)


def cost(us):
    return pl.CostEstimate(flops=int(us * 1e8), bytes_accessed=int(us * 3.7e6), transcendentals=0)


def low_lanes(rows):
    return lax.broadcasted_iota(jnp.int32, (rows, LANES), 1) < BS


def dot(a, b):
    return lax.dot_general(a, b, (((1,), (0,)), ((), ())), preferred_element_type=F32)


def relayout_kernel(x_ref, o_ref, scr):
    rows, nb, _ = x_ref.shape
    low = low_lanes(32)
    for r in range(rows):
        for q in range(32):
            scr[r, pl.ds(q * 8, nb), :] = x_ref[r, :, q * LANES : (q + 1) * LANES].astype(F32)
        for k in range(0, nb, 2):
            x0 = scr[r, pl.ds(k, 32, stride=8), :]
            x1 = scr[r, pl.ds(k + 1, 32, stride=8), :]
            o_ref[r, 0:32, k * BS : (k + 2) * BS] = jnp.where(low, x0, pltpu.roll(x1, BS, 1)).astype(BF)
            o_ref[r, 32:64, k * BS : (k + 2) * BS] = jnp.where(low, pltpu.roll(x0, BS, 1), x1).astype(BF)


def relayout(x, first, rows):
    nb = x.shape[1]
    step = 4
    return pl.pallas_call(
        relayout_kernel,
        grid=(rows // step,),
        out_shape=jax.ShapeDtypeStruct((rows, BS, nb * BS), BF),
        in_specs=[pl.BlockSpec((step, nb, BS * BS), lambda i: (i + first // step, 0, 0))],
        out_specs=pl.BlockSpec((step, BS, nb * BS), lambda i: (i, 0, 0)),
        scratch_shapes=[pltpu.VMEM((step, 256, LANES), F32)],
        compiler_params=params(4),
        cost_estimate=cost(0.6),
        name="relayout",
    )(x)


def relayout_rows_kernel(x_ref, o_ref, scr, mix):
    rows, nb, _ = x_ref.shape
    low = low_lanes(32)
    for r in range(rows):
        for q in range(32):
            scr[r, pl.ds(q * 8, nb), :] = x_ref[r, :, q * LANES : (q + 1) * LANES].astype(F32)
        for k in range(0, nb, 2):
            x0 = scr[r, pl.ds(k, 32, stride=8), :]
            x1 = scr[r, pl.ds(k + 1, 32, stride=8), :]
            mix[r, k // 2, pl.ds(0, 32, stride=2), :] = jnp.where(low, x0, pltpu.roll(x1, BS, 1))
            mix[r, k // 2, pl.ds(1, 32, stride=2), :] = jnp.where(low, pltpu.roll(x0, BS, 1), x1)
            o_ref[r, :, k * BS : (k + 2) * BS] = mix[r, k // 2].astype(BF)


def relayout_rows(x):
    rows, nb, _ = x.shape
    step = 4
    return pl.pallas_call(
        relayout_rows_kernel,
        grid=(rows // step,),
        out_shape=jax.ShapeDtypeStruct((rows, BS, nb * BS), BF),
        in_specs=[pl.BlockSpec((step, nb, BS * BS), lambda i: (i, 0, 0))],
        out_specs=pl.BlockSpec((step, BS, nb * BS), lambda i: (i, 0, 0)),
        scratch_shapes=[pltpu.VMEM((step, 256, LANES), F32), pltpu.VMEM((step, nb // 2, BS, LANES), F32)],
        compiler_params=params(4),
        cost_estimate=cost(1.0),
        name="relayout_rows",
    )(x)


def left_kernel(rb, pct_ref, pl_ref, o_ref):
    slab = lax.axis_index("row")
    low = low_lanes(4 * BS)
    o_ref[...] = jnp.zeros_like(o_ref)

    def pair(ip, carry):
        for half in range(2):
            i = ip * 2 + half
            x = pl_ref[i].astype(F32)
            xt = jnp.concatenate([x, x], axis=0).T
            keep = jnp.where(low if half == 0 else jnp.logical_not(low), xt, 0.0)
            for s in range(4):
                w = pct_ref[s, slab * rb + i] - (slab - 1) * CB
                o_ref[ip, w] = (o_ref[ip, w].astype(F32) + keep[s * BS : (s + 1) * BS]).astype(BF)
        return carry

    lax.fori_loop(0, rb // 2, pair, 0)


def left_factor(pct, p_own):
    rb = p_own.shape[0]
    return pl.pallas_call(
        functools.partial(left_kernel, rb),
        out_shape=jax.ShapeDtypeStruct((rb // 2, 3 * CB, BS, LANES), BF),
        in_specs=[SM, VM],
        out_specs=VM,
        compiler_params=params(24),
        cost_estimate=cost(2.9),
        name="left_factor",
    )(pct, p_own)


def column_table(pct, rb, share):
    slab = lax.axis_index("row")
    padded = jnp.pad(pct, ((0, 0), (rb, rb)), constant_values=-1000000)
    near = lax.dynamic_slice_in_dim(padded, slab * rb, 3 * rb, 1)
    w = near - (slab - 2) * CB
    e = (w & (CB - 1)) - share * lax.axis_index("col")
    return jnp.where((w >= 0) & (e >= 0) & (e < share), e * GROUPS + (w >> 3), -1)


def touched(side, tiles):
    return (side, side + 3) if tiles == GROUPS else (0, tiles)


def right_kernel(rb, tiles, table_ref, *refs):
    o_ref = refs[-1]
    core = lax.rem(lax.axis_index("col"), 2)
    low = lax.broadcasted_iota(jnp.int32, (1, LANES), 1) < BS
    wants = [jnp.where(low, p, tiles + p) for p in range(tiles)]

    def fill(src, side, out_first):
        def four(jq, carry):
            for d in range(4):
                jj = 4 * jq + d
                dups = []
                for t in range(4):
                    x = src[jj, :, t * BS : (t + 1) * BS]
                    dups.append(jnp.concatenate([x, x], axis=1))
                at = [table_ref[t, side * rb + jj] for t in range(4)]
                for p in range(*touched(side, tiles)):
                    total = None
                    for t in range(4):
                        keep = dups[t] * jnp.where(wants[p] == at[t], 1.0, 0.0).astype(BF)
                        total = keep if total is None else total + keep
                    o_ref[out_first + jq, p, d * BS : (d + 1) * BS] = total
            return carry

        lax.fori_loop(0, rb // 4, four, 0)

    if len(refs) == 2:
        fill(refs[0], 1, 0)
    else:
        first = refs[0]
        second = refs[1]

        @pl.when(core == 0)
        def _():
            fill(first, 0, 0)
            fill(second, 2, rb // 4)

        @pl.when(core == 1)
        def _():
            fill(second, 0, 0)
            fill(first, 2, rb // 4)


def right_factor(table, srcs, tiles, us):
    rb = table.shape[1] // 3
    return pl.pallas_call(
        functools.partial(right_kernel, rb, tiles),
        out_shape=jax.ShapeDtypeStruct((len(srcs) * rb // 4, tiles, 4 * BS, LANES), BF),
        in_specs=[SM] + [VM] * len(srcs),
        out_specs=VM,
        compiler_params=params(16),
        cost_estimate=cost(us),
        name="right_factor",
    )(table, *srcs)


def slot_places(a_cols, counts):
    rb, ka = a_cols.shape
    row = jnp.arange(rb, dtype=jnp.int32)[:, None]
    near = a_cols - (lax.axis_index("row") - 1) * rb - row // 4 * 4
    live = jnp.arange(ka, dtype=jnp.int32)[None, :] < counts[:, None]
    return jnp.where(live, near, -1)


def product_kernel(first, rb, shifts, place_ref, own_ref, near_ref, *refs):
    col = lax.axis_index("col")
    ny = lax.axis_size("col") // 2
    srcs, o_ref, band, acc = refs[: len(shifts)], refs[-3], refs[-2], refs[-1]
    rows = o_ref.shape[0]
    ks = srcs[0].shape[2] // BS
    tiles = own_ref.shape[1]
    y, core = col // 2, lax.rem(col, 2)
    wide = band.shape[1]
    half_of = lax.broadcasted_iota(jnp.int32, (1, LANES), 1) // BS
    slots = []
    for s, flip in shifts:
        c = core if flip == 0 else 1 - core
        slots.append((lax.rem(y - s + ny, ny) * 2 + c) * ks)

    def lay(g, carry):
        for t in range(wide):
            band[g, t] = jnp.zeros((4 * BS, LANES), BF)
        for src, slot in zip(srcs, slots):
            for k in range(0, ks, 2):
                pairs = [src[4 * g + d, :, k * BS : (k + 2) * BS] for d in range(4)]
                turned = [jnp.concatenate([x[:, BS:], x[:, :BS]], axis=1) for x in pairs]
                for e in range(2):
                    at = [place_ref[first + 4 * g + d, slot + k + e] for d in range(4)]
                    tile = [jnp.maximum(a, 0) >> 1 for a in at]
                    old = [band[g, tile[d], d * BS : (d + 1) * BS] for d in range(4)]
                    for d in range(4):
                        half = jnp.where(at[d] < 0, 2, at[d] & 1)
                        keep = jnp.where(half_of == half, 1.0, 0.0)
                        stay = (keep * jnp.where(half_of == e, 1.0, 0.0)).astype(BF)
                        move = (keep * jnp.where(half_of == e, 0.0, 1.0)).astype(BF)
                        old[d] = old[d] + (pairs[d] * stay + turned[d] * move)
                    for d in range(4):
                        band[g, tile[d], d * BS : (d + 1) * BS] = old[d]
        return carry

    lax.fori_loop(0, rows // 4, lay, 0)

    quads = rb // 4
    for g in range(rows // 4):
        start = first // 4 + g
        acc[...] = jnp.zeros_like(acc)
        for side in range(3):
            k0, k1 = max(start, side * quads), min(start + wide // 2, (side + 1) * quads)
            if k0 >= k1:
                continue
            p0, p1 = touched(side, tiles)
            ref, base = (own_ref, quads) if side == 1 else (near_ref, 0 if side == 0 else quads)
            total = None
            for k in range(k0, k1):
                lhs = jnp.concatenate([band[g, 2 * (k - start)], band[g, 2 * (k - start) + 1]], axis=1)
                rhs = jnp.concatenate([ref[k - base, p] for p in range(p0, p1)], axis=1)
                part = dot(lhs, rhs)
                total = part if total is None else total + part
            acc[:, p0 * LANES : p1 * LANES] += total
        for d in range(4):
            o_ref[4 * g + d] = acc[d * BS : (d + 1) * BS].astype(BF)


def product(place, own, near, srcs, shifts, first, us):
    rows = srcs[0].shape[0]
    rb = place.shape[0]
    tiles = own.shape[1]
    return pl.pallas_call(
        functools.partial(product_kernel, first, rb, shifts),
        out_shape=jax.ShapeDtypeStruct((rows, BS, tiles * LANES), BF),
        in_specs=[SM] + [VM] * (2 + len(srcs)),
        out_specs=VM,
        scratch_shapes=[
            pltpu.VMEM((rows // 4, rb + 2, 4 * BS, LANES), BF),
            pltpu.VMEM((4 * BS, tiles * LANES), F32),
        ],
        compiler_params=params(32),
        cost_estimate=cost(us),
        name="product",
    )(place, own, near, *srcs)


def coarse_kernel(sets, a0, a1, left_ref, *refs):
    outs = refs[-1 - len(sets) : -1]
    aps = refs[: -1 - len(sets)]
    scr = refs[-1]
    ac = a1 - a0
    tiles = aps[0].shape[2] // LANES
    for out, (i0, i1) in zip(outs, sets):
        rows = i1 - i0
        low = low_lanes(rows)
        for p0 in range(0, tiles, 2):
            p1 = min(p0 + 2, tiles)
            acc = jnp.zeros((rows * ac, (p1 - p0) * LANES), F32)
            ip = 0
            for ap in aps:
                for g in range(0, ap.shape[0] // 2, 2):
                    lhs = [left_ref[ip + d, i0:i1, a0:a1].reshape(rows * ac, LANES) for d in range(2)]
                    rhs = ap[2 * g : 2 * g + 4, :, p0 * LANES : p1 * LANES].reshape(4 * BS, (p1 - p0) * LANES)
                    acc = acc + dot(jnp.concatenate(lhs, axis=1), rhs)
                    ip += 2
            for p in range(p0, p1):
                scr[p, 0 : rows * ac] = acc[:, (p - p0) * LANES : (p - p0 + 1) * LANES]
        for p in range(tiles):
            for a in range(0, ac, 2):
                x0 = scr[p, pl.ds(a, rows, stride=ac), :]
                x1 = scr[p, pl.ds(a + 1, rows, stride=ac), :]
                at = slice(a * BS, (a + 2) * BS)
                out[p, :, at] = jnp.where(low, x0, pltpu.roll(x1, BS, 1)).astype(out.dtype)
                out[tiles + p, :, at] = jnp.where(low, pltpu.roll(x0, BS, 1), x1).astype(out.dtype)


def coarse_rows(left, aps, sets, a0, a1, dtype, us):
    tiles = aps[0].shape[2] // LANES
    return pl.pallas_call(
        functools.partial(coarse_kernel, sets, a0, a1),
        out_shape=[jax.ShapeDtypeStruct((2 * tiles, i1 - i0, (a1 - a0) * BS), dtype) for i0, i1 in sets],
        in_specs=[VM] * (1 + len(aps)),
        out_specs=[VM] * len(sets),
        scratch_shapes=[pltpu.VMEM((tiles, max(i1 - i0 for i0, i1 in sets) * (a1 - a0), LANES), F32)],
        compiler_params=params(32),
        cost_estimate=cost(us),
        name="coarse",
    )(left, *aps)


def assemble_kernel(order_ref, *refs):
    out = refs[-1]
    srcs = refs[:-1] if len(refs) % 2 else refs[1:-1]
    x = jnp.concatenate([s[...].reshape(-1, s.shape[2]) for s in srcs], axis=0)
    res = dot(order_ref[...], x)
    wide = out.shape[1]
    for i in range(CB):
        out[i] = res[i * wide : (i + 1) * wide].astype(BF)


def assemble(order, srcs, a0, total, before):
    n, _, lanes = srcs[0].shape
    step = 512
    per = lanes // step
    wide = n * len(srcs)
    specs = [pl.BlockSpec(order.shape, lambda i: (0, 0))]
    args = [order]
    alias = {}
    if before is not None:
        specs.append(pl.BlockSpec(memory_space=pl.ANY))
        args.append(before)
        alias = {1: 0}
    specs += [pl.BlockSpec((n, CB, step), lambda i: (0, 0, i))] * len(srcs)
    return pl.pallas_call(
        assemble_kernel,
        grid=(per,),
        out_shape=jax.ShapeDtypeStruct((CB, wide, total), BF),
        in_specs=specs,
        out_specs=pl.BlockSpec((CB, wide, step), lambda i: (0, 0, a0 * BS // step + i)),
        input_output_aliases=alias,
        compiler_params=params(24),
        cost_estimate=cost(2.9),
        name="assemble",
    )(*args, *srcs)


def assembly_order(shifts, ncol, share):
    col = lax.axis_index("col")
    y, core = col // 2, col % 2
    groups = GROUPS + 2
    size = ncol * share * groups * CB
    out_row = lax.broadcasted_iota(jnp.int32, (size, size), 0)
    src_row = lax.broadcasted_iota(jnp.int32, (size, size), 1)
    per = share * groups * CB
    which, rest = src_row // per, src_row % per
    e, g, i = rest // (groups * CB), rest // CB % groups, rest % CB
    src_col = jnp.zeros_like(which)
    for z, (s, flip) in enumerate(shifts):
        c = (y - s) % (ncol // 2) * 2 + (core + flip) % 2
        src_col = jnp.where(which == z, c, src_col)
    return (out_row == i * (groups * CB) + g * CB + share * src_col + e).astype(BF)


def body(a_blocks, a_cols, counts, p_blocks, p_cols):
    rb, ks, _ = a_blocks.shape
    nrow, ncol = lax.axis_size("row"), lax.axis_size("col")
    ny = ncol // 2
    nfb = p_cols.shape[0]
    share = CB // ncol
    tiles = (GROUPS * share + 1) // 2
    parts = ((0, rb * 2 // 3), (rb * 2 // 3, rb // 3))
    chunks = ((0, 32), (32, 64))

    def outward(x):
        pairs = [(r * ncol + c, (r + 1 - 2 * (c % 2)) * ncol + c) for r in range(nrow) for c in range(ncol)]
        return lax.ppermute(x, ("row", "col"), [(a, b) for a, b in pairs if 0 <= b < nrow * ncol])

    def over_y(x, s):
        return lax.ppermute(x, "col", [(y * 2 + c, (y + s) % ny * 2 + c) for y in range(ny) for c in range(2)])

    def over_core(x):
        return lax.ppermute(x, "col", [(c, c ^ 1) for c in range(ncol)])

    def upward(x):
        return lax.ppermute(x, "row", [(i, i + 1) for i in range(nrow - 1)])

    def downward(x):
        return lax.ppermute(x, "row", [(i + 1, i) for i in range(nrow - 1)])

    shifts = tuple((s, f) for s in range(ny) for f in range(2))
    pct = p_cols.T

    own_a, side_a, far_a = [], [], []
    for h, (first, rows) in enumerate(parts):
        x = relayout(a_blocks, first, rows)
        own_a.append(x)
        far_a.append([over_y(x, s) for s in range(1, ny)])
        side_a.append(over_core(x))
        if h == 0:
            a_blocks, p_blocks, side_a[0] = lax.optimization_barrier((a_blocks, p_blocks, side_a[0]))
    p_own = relayout_rows(p_blocks)
    beside = outward(p_own)
    p_blocks, p_own, side_a[1] = lax.optimization_barrier((p_blocks, p_own, side_a[1]))
    table = column_table(pct, rb, share)
    left = left_factor(pct, relayout(p_blocks, 0, rb))
    own = right_factor(table, [p_own], tiles, 2.0)
    order = assembly_order(shifts, ncol, share)
    place = slot_places(a_cols, counts)
    beside, left, own, order, place = lax.optimization_barrier((beside, left, own, order, place))
    near = right_factor(table, [beside, over_core(beside)], tiles, 3.0)
    aps = []
    for h in range(2):
        srcs = [own_a[h], side_a[h]] + [z for g in far_a[h] for z in (g, over_core(g))]
        aps.append(product(place, own, near, srcs, shifts, parts[h][0], 0.3 * parts[h][1]))
        if h == 0:
            far_a[1], aps[0] = lax.optimization_barrier((far_a[1], aps[0]))
            early = downward(coarse_rows(left, aps, ((0, CB // 2),), 0, BS, BF, 1.0)[0])

    def columns(x, g):
        y = x[: GROUPS * share].reshape((share, GROUPS) + x.shape[1:])
        return jnp.pad(y.astype(F32), ((0, 0), (g, 2 - g), (0, 0), (0, 0)))

    late = downward(coarse_rows(left, aps, ((CB // 2, CB),), 0, BS, BF, 1.0)[0])
    highs = [upward(coarse_rows(left, aps, ((2 * CB, 3 * CB),), a0, a1, BF, 1.0)[0]) for a0, a1 in chunks]
    mids = [coarse_rows(left, aps, ((CB, 2 * CB),), a0, a1, F32, 1.0)[0] for a0, a1 in chunks]
    early, mids = lax.optimization_barrier((early, mids))
    lower = jnp.concatenate([early, late], axis=1)
    out = None
    for (a0, a1), high, mid in zip(chunks, highs, mids):
        total = columns(high, 0) + columns(mid, 1) + columns(lower[:, :, a0 * BS : a1 * BS], 2)
        total = total.astype(BF).reshape((share * (GROUPS + 2),) + total.shape[2:])
        far = [over_y(total, s) for s in range(1, ny)]
        if out is not None:
            far, out = lax.optimization_barrier((far, out))
        srcs = [z for g in [total] + far for z in (g, over_core(g))]
        out = assemble(order, srcs, a0, BS * BS, out)
    return out


def solution(mesh):
    return jax.shard_map(
        body,
        mesh=mesh,
        in_specs=(P("row", "col", None), P("row", None), P("row"), P("row", None, None), P()),
        out_specs=P("row", None, None),
        check_vma=False,
    )
```

```python
import functools

import jax
import jax.numpy as jnp
from jax import lax
from jax.experimental import pallas as pl
from jax.experimental.pallas import tpu as pltpu
from jax.sharding import PartitionSpec as P

BS = 64
CB = 8
GROUPS = 5
LANES = 128
BF = jnp.bfloat16
F32 = jnp.float32
MIB = 1 << 20

VM = pl.BlockSpec(memory_space=pltpu.VMEM)
SM = pl.BlockSpec(memory_space=pltpu.SMEM)


def params(mib):
    return pltpu.CompilerParams(vmem_limit_bytes=mib * MIB)


def cost(us):
    return pl.CostEstimate(flops=int(us * 1e8), bytes_accessed=int(us * 3.7e6), transcendentals=0)


def low_lanes(rows):
    return lax.broadcasted_iota(jnp.int32, (rows, LANES), 1) < BS


def dot(a, b):
    return lax.dot_general(a, b, (((1,), (0,)), ((), ())), preferred_element_type=F32)


def relayout_kernel(x_ref, o_ref, scr):
    rows, nb, _ = x_ref.shape
    low = low_lanes(32)
    for r in range(rows):
        for q in range(32):
            scr[r, pl.ds(q * 8, nb), :] = x_ref[r, :, q * LANES : (q + 1) * LANES].astype(F32)
        for k in range(0, nb, 2):
            x0 = scr[r, pl.ds(k, 32, stride=8), :]
            x1 = scr[r, pl.ds(k + 1, 32, stride=8), :]
            o_ref[r, k // 2, 0:32] = jnp.where(low, x0, pltpu.roll(x1, BS, 1)).astype(BF)
            o_ref[r, k // 2, 32:64] = jnp.where(low, pltpu.roll(x0, BS, 1), x1).astype(BF)


def relayout(x, first, rows):
    nb = x.shape[1]
    step = 4
    return pl.pallas_call(
        relayout_kernel,
        grid=(rows // step,),
        out_shape=jax.ShapeDtypeStruct((rows, nb // 2, BS, LANES), BF),
        in_specs=[pl.BlockSpec((step, nb, BS * BS), lambda i: (i + first // step, 0, 0))],
        out_specs=pl.BlockSpec((step, nb // 2, BS, LANES), lambda i: (i, 0, 0, 0)),
        scratch_shapes=[pltpu.VMEM((step, 256, LANES), F32)],
        compiler_params=params(4),
        cost_estimate=cost(0.6),
        name="relayout",
    )(x)


def relayout_rows_kernel(x_ref, o_ref, scr, mix):
    rows, nb, _ = x_ref.shape
    low = low_lanes(32)
    for r in range(rows):
        for q in range(32):
            scr[r, pl.ds(q * 8, nb), :] = x_ref[r, :, q * LANES : (q + 1) * LANES].astype(F32)
        for k in range(0, nb, 2):
            x0 = scr[r, pl.ds(k, 32, stride=8), :]
            x1 = scr[r, pl.ds(k + 1, 32, stride=8), :]
            mix[r, k // 2, pl.ds(0, 32, stride=2), :] = jnp.where(low, x0, pltpu.roll(x1, BS, 1))
            mix[r, k // 2, pl.ds(1, 32, stride=2), :] = jnp.where(low, pltpu.roll(x0, BS, 1), x1)
            o_ref[r, k // 2] = mix[r, k // 2].astype(BF)


def relayout_rows(x):
    rows, nb, _ = x.shape
    step = 4
    return pl.pallas_call(
        relayout_rows_kernel,
        grid=(rows // step,),
        out_shape=jax.ShapeDtypeStruct((rows, nb // 2, BS, LANES), BF),
        in_specs=[pl.BlockSpec((step, nb, BS * BS), lambda i: (i, 0, 0))],
        out_specs=pl.BlockSpec((step, nb // 2, BS, LANES), lambda i: (i, 0, 0, 0)),
        scratch_shapes=[pltpu.VMEM((step, 256, LANES), F32), pltpu.VMEM((step, nb // 2, BS, LANES), F32)],
        compiler_params=params(4),
        cost_estimate=cost(1.0),
        name="relayout_rows",
    )(x)


def left_kernel(rb, pct_ref, pl_ref, o_ref):
    slab = lax.axis_index("row")
    low = low_lanes(4 * BS)
    o_ref[...] = jnp.zeros_like(o_ref)

    def pair(ip, carry):
        for half in range(2):
            i = ip * 2 + half
            x = jnp.concatenate([pl_ref[i, 0], pl_ref[i, 1]], axis=1).astype(F32)
            xt = jnp.concatenate([x, x], axis=0).T
            keep = jnp.where(low if half == 0 else jnp.logical_not(low), xt, 0.0)
            for s in range(4):
                w = pct_ref[s, slab * rb + i] - (slab - 1) * CB
                o_ref[ip, w] = (o_ref[ip, w].astype(F32) + keep[s * BS : (s + 1) * BS]).astype(BF)
        return carry

    lax.fori_loop(0, rb // 2, pair, 0)


def left_factor(pct, p_own):
    rb = p_own.shape[0]
    return pl.pallas_call(
        functools.partial(left_kernel, rb),
        out_shape=jax.ShapeDtypeStruct((rb // 2, 3 * CB, BS, LANES), BF),
        in_specs=[SM, VM],
        out_specs=VM,
        compiler_params=params(24),
        cost_estimate=cost(2.9),
        name="left_factor",
    )(pct, p_own)


def column_table(pct, rb, share):
    slab = lax.axis_index("row")
    padded = jnp.pad(pct, ((0, 0), (rb, rb)), constant_values=-1000000)
    near = lax.dynamic_slice_in_dim(padded, slab * rb, 3 * rb, 1)
    w = near - (slab - 2) * CB
    e = (w & (CB - 1)) - share * lax.axis_index("col")
    return jnp.where((w >= 0) & (e >= 0) & (e < share), e * GROUPS + (w >> 3), -1)


def touched(side, tiles):
    return (side, side + 3) if tiles == GROUPS else (0, tiles)


def right_kernel(rb, tiles, table_ref, *refs):
    o_ref = refs[-1]
    core = lax.rem(lax.axis_index("col"), 2)
    low = lax.broadcasted_iota(jnp.int32, (1, LANES), 1) < BS
    wants = [jnp.where(low, p, tiles + p) for p in range(tiles)]

    def fill(src, side, out_first):
        def four(jq, carry):
            for d in range(4):
                jj = 4 * jq + d
                dups = []
                for t in range(4):
                    x = src[jj, t // 2, :, t % 2 * BS : (t % 2 + 1) * BS]
                    dups.append(jnp.concatenate([x, x], axis=1))
                at = [table_ref[t, side * rb + jj] for t in range(4)]
                for p in range(*touched(side, tiles)):
                    total = None
                    for t in range(4):
                        keep = dups[t] * jnp.where(wants[p] == at[t], 1.0, 0.0).astype(BF)
                        total = keep if total is None else total + keep
                    o_ref[out_first + jq, p, d * BS : (d + 1) * BS] = total
            return carry

        lax.fori_loop(0, rb // 4, four, 0)

    if len(refs) == 2:
        fill(refs[0], 1, 0)
    else:
        first = refs[0]
        second = refs[1]

        @pl.when(core == 0)
        def _():
            fill(first, 0, 0)
            fill(second, 2, rb // 4)

        @pl.when(core == 1)
        def _():
            fill(second, 0, 0)
            fill(first, 2, rb // 4)


def right_factor(table, srcs, tiles, us):
    rb = table.shape[1] // 3
    return pl.pallas_call(
        functools.partial(right_kernel, rb, tiles),
        out_shape=jax.ShapeDtypeStruct((len(srcs) * rb // 4, tiles, 4 * BS, LANES), BF),
        in_specs=[SM] + [VM] * len(srcs),
        out_specs=VM,
        compiler_params=params(16),
        cost_estimate=cost(us),
        name="right_factor",
    )(table, *srcs)


def slot_places(a_cols, counts):
    rb, ka = a_cols.shape
    row = jnp.arange(rb, dtype=jnp.int32)[:, None]
    near = a_cols - (lax.axis_index("row") - 1) * rb - row // 4 * 4
    live = jnp.arange(ka, dtype=jnp.int32)[None, :] < counts[:, None]
    return jnp.where(live, near, 2 * (rb + 2))


def first_slots(shifts, ks):
    col = lax.axis_index("col")
    ny = lax.axis_size("col") // 2
    y, core = col // 2, lax.rem(col, 2)
    slots = []
    for s, flip in shifts:
        c = core if flip == 0 else 1 - core
        slots.append((lax.rem(y - s + ny, ny) * 2 + c) * ks)
    return slots


def lay(first, place_ref, srcs, slots, band, start):
    low = low_lanes(BS)
    zero = jnp.zeros((BS, LANES), BF)

    def group(g, carry):
        for t in range(band.shape[1]):
            band[g, t] = start(g, t)
        for src, slot in zip(srcs, slots):
            for k in range(src.shape[1]):
                for d0 in range(0, 4, 2):
                    cuts = []
                    for d in range(d0, d0 + 2):
                        x = src[4 * g + d, k]
                        r = jnp.concatenate([x[:, BS:], x[:, :BS]], axis=1)
                        cuts.append(
                            (
                                (jnp.where(low, x, zero), jnp.where(low, zero, r)),
                                (jnp.where(low, r, zero), jnp.where(low, zero, x)),
                            )
                        )
                    for e in range(2):
                        at = [place_ref[first + 4 * g + d0 + d, slot + 2 * k + e] for d in range(2)]
                        spots = [(g, a >> 1, slice((d0 + d) * BS, (d0 + d + 1) * BS)) for d, a in enumerate(at)]
                        old = [band[spot] for spot in spots]
                        for spot, a, x, cut in zip(spots, at, old, cuts):
                            band[spot] = x + jnp.where((a & 1) == 0, cut[e][0], cut[e][1])
        return carry

    lax.fori_loop(0, band.shape[0], group, 0)


def band_kernel(first, shifts, place_ref, *refs):
    srcs, band = refs[:-1], refs[-1]
    slots = first_slots(shifts, srcs[0].shape[1] * 2)
    lay(first, place_ref, srcs, slots, band, lambda g, t: jnp.zeros((4 * BS, LANES), BF))


def near_band(place, srcs, shifts, first):
    rows = srcs[0].shape[0]
    return pl.pallas_call(
        functools.partial(band_kernel, first, shifts),
        out_shape=jax.ShapeDtypeStruct((rows // 4, place.shape[0] + 3, 4 * BS, LANES), BF),
        in_specs=[SM] + [VM] * len(srcs),
        out_specs=VM,
        compiler_params=params(24),
        cost_estimate=cost(0.16 * rows),
        name="near_band",
    )(place, *srcs)


def product_kernel(first, rb, shifts, place_ref, own_ref, near_ref, start_ref, *refs):
    srcs = refs[: len(shifts)]
    o_ref, band, acc = refs[len(shifts) :]
    rows = o_ref.shape[0]
    tiles = own_ref.shape[1]
    wide = rb + 2
    slots = first_slots(shifts, srcs[0].shape[1] * 2)
    lay(first, place_ref, srcs, slots, band, lambda g, t: start_ref[g, t])
    quads = rb // 4
    for g in range(rows // 4):
        start = first // 4 + g
        acc[...] = jnp.zeros_like(acc)
        for side in range(3):
            k0, k1 = max(start, side * quads), min(start + wide // 2, (side + 1) * quads)
            if k0 >= k1:
                continue
            p0, p1 = touched(side, tiles)
            ref, base = (own_ref, quads) if side == 1 else (near_ref, 0 if side == 0 else quads)
            total = None
            for k in range(k0, k1):
                lhs = jnp.concatenate([band[g, 2 * (k - start)], band[g, 2 * (k - start) + 1]], axis=1)
                rhs = jnp.concatenate([ref[k - base, p] for p in range(p0, p1)], axis=1)
                part = dot(lhs, rhs)
                total = part if total is None else total + part
            acc[:, p0 * LANES : p1 * LANES] += total
        for d in range(4):
            o_ref[4 * g + d] = acc[d * BS : (d + 1) * BS].astype(BF)


def product(place, own, near, start, srcs, shifts, first, us):
    rows = srcs[0].shape[0]
    rb = place.shape[0]
    tiles = own.shape[1]
    return pl.pallas_call(
        functools.partial(product_kernel, first, rb, shifts),
        out_shape=jax.ShapeDtypeStruct((rows, BS, tiles * LANES), BF),
        in_specs=[SM] + [VM] * (3 + len(srcs)),
        out_specs=VM,
        scratch_shapes=[
            pltpu.VMEM(start.shape, BF),
            pltpu.VMEM((4 * BS, tiles * LANES), F32),
        ],
        compiler_params=params(40),
        cost_estimate=cost(us),
        name="product",
    )(place, own, near, start, *srcs)


def coarse_kernel(sets, a0, a1, left_ref, *refs):
    outs = refs[-1 - len(sets) : -1]
    aps = refs[: -1 - len(sets)]
    scr = refs[-1]
    ac = a1 - a0
    tiles = aps[0].shape[2] // LANES
    for out, (i0, i1) in zip(outs, sets):
        rows = i1 - i0
        low = low_lanes(rows)
        for p0 in range(0, tiles, 2):
            p1 = min(p0 + 2, tiles)
            acc = jnp.zeros((rows * ac, (p1 - p0) * LANES), F32)
            ip = 0
            for ap in aps:
                for g in range(0, ap.shape[0] // 2, 2):
                    lhs = [left_ref[ip + d, i0:i1, a0:a1].reshape(rows * ac, LANES) for d in range(2)]
                    rhs = ap[2 * g : 2 * g + 4, :, p0 * LANES : p1 * LANES].reshape(4 * BS, (p1 - p0) * LANES)
                    acc = acc + dot(jnp.concatenate(lhs, axis=1), rhs)
                    ip += 2
            for p in range(p0, p1):
                scr[p, 0 : rows * ac] = acc[:, (p - p0) * LANES : (p - p0 + 1) * LANES]
        for p in range(tiles):
            for a in range(0, ac, 2):
                x0 = scr[p, pl.ds(a, rows, stride=ac), :]
                x1 = scr[p, pl.ds(a + 1, rows, stride=ac), :]
                at = slice(a * BS, (a + 2) * BS)
                out[p, :, at] = jnp.where(low, x0, pltpu.roll(x1, BS, 1)).astype(out.dtype)
                out[tiles + p, :, at] = jnp.where(low, pltpu.roll(x0, BS, 1), x1).astype(out.dtype)


def coarse_rows(left, aps, sets, a0, a1, dtype, us):
    tiles = aps[0].shape[2] // LANES
    return pl.pallas_call(
        functools.partial(coarse_kernel, sets, a0, a1),
        out_shape=[jax.ShapeDtypeStruct((2 * tiles, i1 - i0, (a1 - a0) * BS), dtype) for i0, i1 in sets],
        in_specs=[VM] * (1 + len(aps)),
        out_specs=[VM] * len(sets),
        scratch_shapes=[pltpu.VMEM((tiles, max(i1 - i0 for i0, i1 in sets) * (a1 - a0), LANES), F32)],
        compiler_params=params(32),
        cost_estimate=cost(us),
        name="coarse",
    )(left, *aps)


def assemble_kernel(order_ref, *refs):
    out = refs[-1]
    srcs = refs[:-1] if len(refs) % 2 else refs[1:-1]
    x = jnp.concatenate([s[...].reshape(-1, s.shape[2]) for s in srcs], axis=0)
    res = dot(order_ref[...], x)
    wide = out.shape[1]
    for i in range(CB):
        out[i] = res[i * wide : (i + 1) * wide].astype(BF)


def assemble(order, srcs, a0, total, before):
    n, _, lanes = srcs[0].shape
    step = 512
    per = lanes // step
    wide = n * len(srcs)
    specs = [pl.BlockSpec(order.shape, lambda i: (0, 0))]
    args = [order]
    alias = {}
    if before is not None:
        specs.append(pl.BlockSpec(memory_space=pl.ANY))
        args.append(before)
        alias = {1: 0}
    specs += [pl.BlockSpec((n, CB, step), lambda i: (0, 0, i))] * len(srcs)
    return pl.pallas_call(
        assemble_kernel,
        grid=(per,),
        out_shape=jax.ShapeDtypeStruct((CB, wide, total), BF),
        in_specs=specs,
        out_specs=pl.BlockSpec((CB, wide, step), lambda i: (0, 0, a0 * BS // step + i)),
        input_output_aliases=alias,
        compiler_params=params(24),
        cost_estimate=cost(2.9),
        name="assemble",
    )(*args, *srcs)


def assembly_order(shifts, ncol, share):
    col = lax.axis_index("col")
    y, core = col // 2, col % 2
    groups = GROUPS + 2
    size = ncol * share * groups * CB
    out_row = lax.broadcasted_iota(jnp.int32, (size, size), 0)
    src_row = lax.broadcasted_iota(jnp.int32, (size, size), 1)
    per = share * groups * CB
    which, rest = src_row // per, src_row % per
    e, g, i = rest // (groups * CB), rest // CB % groups, rest % CB
    src_col = jnp.zeros_like(which)
    for z, (s, flip) in enumerate(shifts):
        c = (y - s) % (ncol // 2) * 2 + (core + flip) % 2
        src_col = jnp.where(which == z, c, src_col)
    return (out_row == i * (groups * CB) + g * CB + share * src_col + e).astype(BF)


def body(a_blocks, a_cols, counts, p_blocks, p_cols):
    rb, ks, _ = a_blocks.shape
    nrow, ncol = lax.axis_size("row"), lax.axis_size("col")
    ny = ncol // 2
    nfb = p_cols.shape[0]
    share = CB // ncol
    tiles = (GROUPS * share + 1) // 2
    parts = ((0, rb * 2 // 3), (rb * 2 // 3, rb // 3))
    chunks = ((0, 32), (32, 64))

    def outward(x):
        pairs = [(r * ncol + c, (r + 1 - 2 * (c % 2)) * ncol + c) for r in range(nrow) for c in range(ncol)]
        return lax.ppermute(x, ("row", "col"), [(a, b) for a, b in pairs if 0 <= b < nrow * ncol])

    def over_y(x, s):
        return lax.ppermute(x, "col", [(y * 2 + c, (y + s) % ny * 2 + c) for y in range(ny) for c in range(2)])

    def over_core(x):
        return lax.ppermute(x, "col", [(c, c ^ 1) for c in range(ncol)])

    def upward(x):
        return lax.ppermute(x, "row", [(i, i + 1) for i in range(nrow - 1)])

    def downward(x):
        return lax.ppermute(x, "row", [(i + 1, i) for i in range(nrow - 1)])

    shifts = tuple((s, f) for s in range(ny) for f in range(2))
    pct = p_cols.T

    own_a, side_a, far_a = [], [], []
    for h, (first, rows) in enumerate(parts):
        x = relayout(a_blocks, first, rows)
        own_a.append(x)
        far_a.append([over_y(x, s) for s in range(1, ny)])
        side_a.append(over_core(x))
        if h == 0:
            a_blocks, p_blocks, side_a[0] = lax.optimization_barrier((a_blocks, p_blocks, side_a[0]))
    p_own = relayout_rows(p_blocks)
    beside = outward(p_own)
    p_blocks, p_own, side_a[1] = lax.optimization_barrier((p_blocks, p_own, side_a[1]))
    table = column_table(pct, rb, share)
    left = left_factor(pct, relayout(p_blocks, 0, rb))
    own = right_factor(table, [p_own], tiles, 2.0)
    order = assembly_order(shifts, ncol, share)
    place = slot_places(a_cols, counts)
    bands = [near_band(place, [own_a[h], side_a[h]], shifts[:2], parts[h][0]) for h in range(2)]
    beside, far_a[0], left, own, order, bands = lax.optimization_barrier((beside, far_a[0], left, own, order, bands))
    near = right_factor(table, [beside, over_core(beside)], tiles, 3.0)
    aps = []
    for h in range(2):
        srcs = [z for g in far_a[h] for z in (g, over_core(g))]
        aps.append(product(place, own, near, bands[h], srcs, shifts[2:], parts[h][0], 0.3 * parts[h][1]))
        if h == 0:
            far_a[1], aps[0] = lax.optimization_barrier((far_a[1], aps[0]))
            early = downward(coarse_rows(left, aps, ((0, CB // 2),), 0, BS, BF, 1.0)[0])

    def columns(x, g):
        y = x[: GROUPS * share].reshape((share, GROUPS) + x.shape[1:])
        return jnp.pad(y.astype(F32), ((0, 0), (g, 2 - g), (0, 0), (0, 0)))

    late = downward(coarse_rows(left, aps, ((CB // 2, CB),), 0, BS, BF, 1.0)[0])
    highs = [coarse_rows(left, aps, ((2 * CB, 3 * CB),), a0, a1, BF, 1.0)[0] for a0, a1 in chunks]
    left, highs = lax.optimization_barrier((left, highs))
    highs = [upward(x) for x in highs]
    mids = [coarse_rows(left, aps, ((CB, 2 * CB),), a0, a1, F32, 1.0)[0] for a0, a1 in chunks]
    early, mids = lax.optimization_barrier((early, mids))
    lower = jnp.concatenate([early, late], axis=1)
    totals, fars = [], []
    for (a0, a1), high, mid in zip(chunks, highs, mids):
        total = columns(high, 0) + columns(mid, 1) + columns(lower[:, :, a0 * BS : a1 * BS], 2)
        totals.append(total.astype(BF).reshape((share * (GROUPS + 2),) + total.shape[2:]))
        fars.append([over_y(totals[-1], s) for s in range(1, ny)])
    fars[0], totals[1] = lax.optimization_barrier((fars[0], totals[1]))
    out = None
    for (a0, a1), total, far in zip(chunks, totals, fars):
        if out is not None:
            far, out = lax.optimization_barrier((far, out))
        srcs = [z for g in [total] + far for z in (g, over_core(g))]
        out = assemble(order, srcs, a0, BS * BS, out)
    return out


def solution(mesh):
    return jax.shard_map(
        body,
        mesh=mesh,
        in_specs=(P("row", "col", None), P("row", None), P("row"), P("row", None, None), P()),
        out_specs=P("row", None, None),
        check_vma=False,
    )
```

```python
import functools

import jax
import jax.numpy as jnp
from jax import lax
from jax.experimental import pallas as pl
from jax.experimental.pallas import tpu as pltpu
from jax.sharding import PartitionSpec as P

BS = 64
CB = 8
GROUPS = 5
LANES = 128
BF = jnp.bfloat16
F32 = jnp.float32
MIB = 1 << 20

VM = pl.BlockSpec(memory_space=pltpu.VMEM)
SM = pl.BlockSpec(memory_space=pltpu.SMEM)


def params(mib):
    return pltpu.CompilerParams(vmem_limit_bytes=mib * MIB)


def cost(us):
    return pl.CostEstimate(flops=int(us * 1e8), bytes_accessed=int(us * 3.7e6), transcendentals=0)


def low_lanes(rows):
    return lax.broadcasted_iota(jnp.int32, (rows, LANES), 1) < BS


def dot(a, b):
    return lax.dot_general(a, b, (((1,), (0,)), ((), ())), preferred_element_type=F32)


def relayout_kernel(x_ref, o_ref, scr):
    rows, nb, _ = x_ref.shape
    low = low_lanes(32)
    for r in range(rows):
        for q in range(32):
            scr[r, pl.ds(q * 8, nb), :] = x_ref[r, :, q * LANES : (q + 1) * LANES].astype(F32)
        for k in range(0, nb, 2):
            x0 = scr[r, pl.ds(k, 32, stride=8), :]
            x1 = scr[r, pl.ds(k + 1, 32, stride=8), :]
            o_ref[r, k // 2, 0:32] = jnp.where(low, x0, pltpu.roll(x1, BS, 1)).astype(BF)
            o_ref[r, k // 2, 32:64] = jnp.where(low, pltpu.roll(x0, BS, 1), x1).astype(BF)


def relayout(x, first, rows):
    nb = x.shape[1]
    step = 4
    return pl.pallas_call(
        relayout_kernel,
        grid=(rows // step,),
        out_shape=jax.ShapeDtypeStruct((rows, nb // 2, BS, LANES), BF),
        in_specs=[pl.BlockSpec((step, nb, BS * BS), lambda i: (i + first // step, 0, 0))],
        out_specs=pl.BlockSpec((step, nb // 2, BS, LANES), lambda i: (i, 0, 0, 0)),
        scratch_shapes=[pltpu.VMEM((step, 256, LANES), F32)],
        compiler_params=params(4),
        cost_estimate=cost(0.6),
        name="relayout",
    )(x)


def relayout_rows_kernel(x_ref, o_ref, scr, mix):
    rows, nb, _ = x_ref.shape
    low = low_lanes(32)
    for r in range(rows):
        for q in range(32):
            scr[r, pl.ds(q * 8, nb), :] = x_ref[r, :, q * LANES : (q + 1) * LANES].astype(F32)
        for k in range(0, nb, 2):
            x0 = scr[r, pl.ds(k, 32, stride=8), :]
            x1 = scr[r, pl.ds(k + 1, 32, stride=8), :]
            mix[r, k // 2, pl.ds(0, 32, stride=2), :] = jnp.where(low, x0, pltpu.roll(x1, BS, 1))
            mix[r, k // 2, pl.ds(1, 32, stride=2), :] = jnp.where(low, pltpu.roll(x0, BS, 1), x1)
            o_ref[r, k // 2] = mix[r, k // 2].astype(BF)


def relayout_rows(x):
    rows, nb, _ = x.shape
    step = 4
    return pl.pallas_call(
        relayout_rows_kernel,
        grid=(rows // step,),
        out_shape=jax.ShapeDtypeStruct((rows, nb // 2, BS, LANES), BF),
        in_specs=[pl.BlockSpec((step, nb, BS * BS), lambda i: (i, 0, 0))],
        out_specs=pl.BlockSpec((step, nb // 2, BS, LANES), lambda i: (i, 0, 0, 0)),
        scratch_shapes=[pltpu.VMEM((step, 256, LANES), F32), pltpu.VMEM((step, nb // 2, BS, LANES), F32)],
        compiler_params=params(4),
        cost_estimate=cost(1.0),
        name="relayout_rows",
    )(x)


def left_kernel(rb, pct_ref, pl_ref, o_ref):
    slab = lax.axis_index("row")
    low = low_lanes(4 * BS)
    o_ref[...] = jnp.zeros_like(o_ref)

    def pair(ip, carry):
        for half in range(2):
            i = ip * 2 + half
            x = jnp.concatenate([pl_ref[i, 0], pl_ref[i, 1]], axis=1).astype(F32)
            xt = jnp.concatenate([x, x], axis=0).T
            keep = jnp.where(low if half == 0 else jnp.logical_not(low), xt, 0.0)
            for s in range(4):
                w = pct_ref[s, slab * rb + i] - (slab - 1) * CB
                o_ref[ip, w] = (o_ref[ip, w].astype(F32) + keep[s * BS : (s + 1) * BS]).astype(BF)
        return carry

    lax.fori_loop(0, rb // 2, pair, 0)


def left_factor(pct, p_own):
    rb = p_own.shape[0]
    return pl.pallas_call(
        functools.partial(left_kernel, rb),
        out_shape=jax.ShapeDtypeStruct((rb // 2, 3 * CB, BS, LANES), BF),
        in_specs=[SM, VM],
        out_specs=VM,
        compiler_params=params(12),
        cost_estimate=cost(2.9),
        name="left_factor",
    )(pct, p_own)


def column_table(pct, rb, share):
    slab = lax.axis_index("row")
    padded = jnp.pad(pct, ((0, 0), (rb, rb)), constant_values=-1000000)
    near = lax.dynamic_slice_in_dim(padded, slab * rb, 3 * rb, 1)
    w = near - (slab - 2) * CB
    e = (w & (CB - 1)) - share * lax.axis_index("col")
    return jnp.where((w >= 0) & (e >= 0) & (e < share), e * GROUPS + (w >> 3), -1)


def touched(side, tiles):
    return (side, side + 3) if tiles == GROUPS else (0, tiles)


def right_kernel(rb, tiles, table_ref, *refs):
    o_ref = refs[-1]
    core = lax.rem(lax.axis_index("col"), 2)
    low = lax.broadcasted_iota(jnp.int32, (1, LANES), 1) < BS
    wants = [jnp.where(low, p, tiles + p) for p in range(tiles)]

    def fill(src, side, out_first):
        def four(jq, carry):
            for d in range(4):
                jj = 4 * jq + d
                dups = []
                for t in range(4):
                    x = src[jj, t // 2, :, t % 2 * BS : (t % 2 + 1) * BS]
                    dups.append(jnp.concatenate([x, x], axis=1))
                at = [table_ref[t, side * rb + jj] for t in range(4)]
                for p in range(*touched(side, tiles)):
                    total = None
                    for t in range(4):
                        keep = dups[t] * jnp.where(wants[p] == at[t], 1.0, 0.0).astype(BF)
                        total = keep if total is None else total + keep
                    o_ref[out_first + jq, p, d * BS : (d + 1) * BS] = total
            return carry

        lax.fori_loop(0, rb // 4, four, 0)

    if len(refs) == 2:
        fill(refs[0], 1, 0)
    else:
        first = refs[0]
        second = refs[1]

        @pl.when(core == 0)
        def _():
            fill(first, 0, 0)
            fill(second, 2, rb // 4)

        @pl.when(core == 1)
        def _():
            fill(second, 0, 0)
            fill(first, 2, rb // 4)


def right_factor(table, srcs, tiles, us):
    rb = table.shape[1] // 3
    return pl.pallas_call(
        functools.partial(right_kernel, rb, tiles),
        out_shape=jax.ShapeDtypeStruct((len(srcs) * rb // 4, tiles, 4 * BS, LANES), BF),
        in_specs=[SM] + [VM] * len(srcs),
        out_specs=VM,
        compiler_params=params(8),
        cost_estimate=cost(us),
        name="right_factor",
    )(table, *srcs)


def slot_places(a_cols, counts):
    rb, ka = a_cols.shape
    row = jnp.arange(rb, dtype=jnp.int32)[:, None]
    near = a_cols - (lax.axis_index("row") - 1) * rb - row // 4 * 4
    live = jnp.arange(ka, dtype=jnp.int32)[None, :] < counts[:, None]
    return jnp.where(live, near, 2 * (rb + 2))


def first_slots(shifts, ks):
    col = lax.axis_index("col")
    ny = lax.axis_size("col") // 2
    y, core = col // 2, lax.rem(col, 2)
    slots = []
    for s, flip in shifts:
        c = core if flip == 0 else 1 - core
        slots.append((lax.rem(y - s + ny, ny) * 2 + c) * ks)
    return slots


def lay(first, place_ref, srcs, slots, band, start):
    low = low_lanes(BS)
    zero = jnp.zeros((BS, LANES), BF)

    def group(g, carry):
        for t in range(band.shape[1]):
            band[g, t] = start(g, t)
        for src, slot in zip(srcs, slots):
            for k in range(src.shape[1]):
                for d0 in range(0, 4, 2):
                    cuts = []
                    for d in range(d0, d0 + 2):
                        x = src[4 * g + d, k]
                        r = jnp.concatenate([x[:, BS:], x[:, :BS]], axis=1)
                        cuts.append(
                            (
                                (jnp.where(low, x, zero), jnp.where(low, zero, r)),
                                (jnp.where(low, r, zero), jnp.where(low, zero, x)),
                            )
                        )
                    for e in range(2):
                        at = [place_ref[first + 4 * g + d0 + d, slot + 2 * k + e] for d in range(2)]
                        spots = [(g, a >> 1, slice((d0 + d) * BS, (d0 + d + 1) * BS)) for d, a in enumerate(at)]
                        old = [band[spot] for spot in spots]
                        for spot, a, x, cut in zip(spots, at, old, cuts):
                            band[spot] = x + jnp.where((a & 1) == 0, cut[e][0], cut[e][1])
        return carry

    lax.fori_loop(0, band.shape[0], group, 0)


def band_kernel(first, shifts, place_ref, *refs):
    srcs, band = refs[:-1], refs[-1]
    slots = first_slots(shifts, srcs[0].shape[1] * 2)
    lay(first, place_ref, srcs, slots, band, lambda g, t: jnp.zeros((4 * BS, LANES), BF))


def near_band(place, srcs, shifts, first):
    rows = srcs[0].shape[0]
    return pl.pallas_call(
        functools.partial(band_kernel, first, shifts),
        out_shape=jax.ShapeDtypeStruct((rows // 4, place.shape[0] + 3, 4 * BS, LANES), BF),
        in_specs=[SM] + [VM] * len(srcs),
        out_specs=VM,
        compiler_params=params(12),
        cost_estimate=cost(0.16 * rows),
        name="near_band",
    )(place, *srcs)


def product_kernel(first, rb, shifts, place_ref, own_ref, near_ref, start_ref, *refs):
    srcs = refs[: len(shifts)]
    o_ref, band, acc = refs[len(shifts) :]
    rows = o_ref.shape[0]
    tiles = own_ref.shape[1]
    wide = rb + 2
    slots = first_slots(shifts, srcs[0].shape[1] * 2)
    lay(first, place_ref, srcs, slots, band, lambda g, t: start_ref[g, t])
    quads = rb // 4
    for g in range(rows // 4):
        start = first // 4 + g
        acc[...] = jnp.zeros_like(acc)
        for side in range(3):
            k0, k1 = max(start, side * quads), min(start + wide // 2, (side + 1) * quads)
            if k0 >= k1:
                continue
            p0, p1 = touched(side, tiles)
            ref, base = (own_ref, quads) if side == 1 else (near_ref, 0 if side == 0 else quads)
            total = None
            for k in range(k0, k1):
                lhs = jnp.concatenate([band[g, 2 * (k - start)], band[g, 2 * (k - start) + 1]], axis=1)
                rhs = jnp.concatenate([ref[k - base, p] for p in range(p0, p1)], axis=1)
                part = dot(lhs, rhs)
                total = part if total is None else total + part
            acc[:, p0 * LANES : p1 * LANES] += total
        for d in range(4):
            o_ref[4 * g + d] = acc[d * BS : (d + 1) * BS].astype(BF)


def product(place, own, near, start, srcs, shifts, first, us):
    rows = srcs[0].shape[0]
    rb = place.shape[0]
    tiles = own.shape[1]
    return pl.pallas_call(
        functools.partial(product_kernel, first, rb, shifts),
        out_shape=jax.ShapeDtypeStruct((rows, BS, tiles * LANES), BF),
        in_specs=[SM] + [VM] * (3 + len(srcs)),
        out_specs=VM,
        scratch_shapes=[
            pltpu.VMEM(start.shape, BF),
            pltpu.VMEM((4 * BS, tiles * LANES), F32),
        ],
        compiler_params=params(16),
        cost_estimate=cost(us),
        name="product",
    )(place, own, near, start, *srcs)


def coarse_kernel(sets, a0, a1, left_ref, *refs):
    outs = refs[-1 - len(sets) : -1]
    aps = refs[: -1 - len(sets)]
    scr = refs[-1]
    ac = a1 - a0
    tiles = aps[0].shape[2] // LANES
    for out, (i0, i1) in zip(outs, sets):
        rows = i1 - i0
        low = low_lanes(rows)
        for p0 in range(0, tiles, 2):
            p1 = min(p0 + 2, tiles)
            acc = jnp.zeros((rows * ac, (p1 - p0) * LANES), F32)
            ip = 0
            for ap in aps:
                for g in range(0, ap.shape[0] // 2, 2):
                    lhs = [left_ref[ip + d, i0:i1, a0:a1].reshape(rows * ac, LANES) for d in range(2)]
                    rhs = ap[2 * g : 2 * g + 4, :, p0 * LANES : p1 * LANES].reshape(4 * BS, (p1 - p0) * LANES)
                    acc = acc + dot(jnp.concatenate(lhs, axis=1), rhs)
                    ip += 2
            for p in range(p0, p1):
                scr[p, 0 : rows * ac] = acc[:, (p - p0) * LANES : (p - p0 + 1) * LANES]
        for p in range(tiles):
            for a in range(0, ac, 2):
                x0 = scr[p, pl.ds(a, rows, stride=ac), :]
                x1 = scr[p, pl.ds(a + 1, rows, stride=ac), :]
                at = slice(a * BS, (a + 2) * BS)
                out[p, :, at] = jnp.where(low, x0, pltpu.roll(x1, BS, 1)).astype(out.dtype)
                out[tiles + p, :, at] = jnp.where(low, pltpu.roll(x0, BS, 1), x1).astype(out.dtype)


def coarse_rows(left, aps, sets, a0, a1, dtype, us):
    tiles = aps[0].shape[2] // LANES
    return pl.pallas_call(
        functools.partial(coarse_kernel, sets, a0, a1),
        out_shape=[jax.ShapeDtypeStruct((2 * tiles, i1 - i0, (a1 - a0) * BS), dtype) for i0, i1 in sets],
        in_specs=[VM] * (1 + len(aps)),
        out_specs=[VM] * len(sets),
        scratch_shapes=[pltpu.VMEM((tiles, max(i1 - i0 for i0, i1 in sets) * (a1 - a0), LANES), F32)],
        compiler_params=params(12),
        cost_estimate=cost(us),
        name="coarse",
    )(left, *aps)


def assemble_kernel(order_ref, *refs):
    out = refs[-1]
    srcs = refs[:-1] if len(refs) % 2 else refs[1:-1]
    x = jnp.concatenate([s[...].reshape(-1, s.shape[2]) for s in srcs], axis=0)
    res = dot(order_ref[...], x)
    wide = out.shape[1]
    for i in range(CB):
        out[i] = res[i * wide : (i + 1) * wide].astype(BF)


def assemble(order, srcs, a0, total, before):
    n, _, lanes = srcs[0].shape
    step = 512
    per = lanes // step
    wide = n * len(srcs)
    specs = [pl.BlockSpec(order.shape, lambda i: (0, 0))]
    args = [order]
    alias = {}
    if before is not None:
        specs.append(pl.BlockSpec(memory_space=pl.ANY))
        args.append(before)
        alias = {1: 0}
    specs += [pl.BlockSpec((n, CB, step), lambda i: (0, 0, i))] * len(srcs)
    return pl.pallas_call(
        assemble_kernel,
        grid=(per,),
        out_shape=jax.ShapeDtypeStruct((CB, wide, total), BF),
        in_specs=specs,
        out_specs=pl.BlockSpec((CB, wide, step), lambda i: (0, 0, a0 * BS // step + i)),
        input_output_aliases=alias,
        compiler_params=params(12),
        cost_estimate=cost(2.9),
        name="assemble",
    )(*args, *srcs)


def assembly_order(shifts, ncol, share):
    col = lax.axis_index("col")
    y, core = col // 2, col % 2
    groups = GROUPS + 2
    size = ncol * share * groups * CB
    out_row = lax.broadcasted_iota(jnp.int32, (size, size), 0)
    src_row = lax.broadcasted_iota(jnp.int32, (size, size), 1)
    per = share * groups * CB
    which, rest = src_row // per, src_row % per
    e, g, i = rest // (groups * CB), rest // CB % groups, rest % CB
    src_col = jnp.zeros_like(which)
    for z, (s, flip) in enumerate(shifts):
        c = (y - s) % (ncol // 2) * 2 + (core + flip) % 2
        src_col = jnp.where(which == z, c, src_col)
    return (out_row == i * (groups * CB) + g * CB + share * src_col + e).astype(BF)


def body(a_blocks, a_cols, counts, p_blocks, p_cols):
    rb, ks, _ = a_blocks.shape
    nrow, ncol = lax.axis_size("row"), lax.axis_size("col")
    ny = ncol // 2
    nfb = p_cols.shape[0]
    share = CB // ncol
    tiles = (GROUPS * share + 1) // 2
    parts = ((0, rb * 2 // 3), (rb * 2 // 3, rb // 3))
    chunks = ((0, 32), (32, 64))

    def outward(x):
        pairs = [(r * ncol + c, (r + 1 - 2 * (c % 2)) * ncol + c) for r in range(nrow) for c in range(ncol)]
        return lax.ppermute(x, ("row", "col"), [(a, b) for a, b in pairs if 0 <= b < nrow * ncol])

    def over_y(x, s):
        return lax.ppermute(x, "col", [(y * 2 + c, (y + s) % ny * 2 + c) for y in range(ny) for c in range(2)])

    def over_core(x):
        return lax.ppermute(x, "col", [(c, c ^ 1) for c in range(ncol)])

    def upward(x):
        return lax.ppermute(x, "row", [(i, i + 1) for i in range(nrow - 1)])

    def downward(x):
        return lax.ppermute(x, "row", [(i + 1, i) for i in range(nrow - 1)])

    shifts = tuple((s, f) for s in range(ny) for f in range(2))
    pct = p_cols.T

    own_a, side_a, far_a = [], [], []
    for h, (first, rows) in enumerate(parts):
        x = relayout(a_blocks, first, rows)
        own_a.append(x)
        far_a.append([over_y(x, s) for s in range(1, ny)])
        side_a.append(over_core(x))
        if h == 0:
            a_blocks, p_blocks, side_a[0] = lax.optimization_barrier((a_blocks, p_blocks, side_a[0]))
    p_own = relayout_rows(p_blocks)
    beside = outward(p_own)
    p_blocks, p_own, side_a[1] = lax.optimization_barrier((p_blocks, p_own, side_a[1]))
    table = column_table(pct, rb, share)
    left = left_factor(pct, relayout(p_blocks, 0, rb))
    own = right_factor(table, [p_own], tiles, 2.0)
    order = assembly_order(shifts, ncol, share)
    place = slot_places(a_cols, counts)
    bands = [near_band(place, [own_a[h], side_a[h]], shifts[:2], parts[h][0]) for h in range(2)]
    beside, far_a[0], left, own, order, bands = lax.optimization_barrier((beside, far_a[0], left, own, order, bands))
    near = right_factor(table, [beside, over_core(beside)], tiles, 3.0)
    aps = []
    for h in range(2):
        srcs = [z for g in far_a[h] for z in (g, over_core(g))]
        aps.append(product(place, own, near, bands[h], srcs, shifts[2:], parts[h][0], 0.3 * parts[h][1]))
        if h == 0:
            far_a[1], aps[0] = lax.optimization_barrier((far_a[1], aps[0]))
            early = downward(coarse_rows(left, aps, ((0, CB // 2),), 0, BS, BF, 1.0)[0])

    def columns(x, g):
        y = x[: GROUPS * share].reshape((share, GROUPS) + x.shape[1:])
        return jnp.pad(y.astype(F32), ((0, 0), (g, 2 - g), (0, 0), (0, 0)))

    late = downward(coarse_rows(left, aps, ((CB // 2, CB),), 0, BS, BF, 1.0)[0])
    highs = [coarse_rows(left, aps, ((2 * CB, 3 * CB),), a0, a1, BF, 1.0)[0] for a0, a1 in chunks]
    left, highs = lax.optimization_barrier((left, highs))
    highs[1], late = lax.optimization_barrier((highs[1], late))
    highs = [upward(x) for x in highs]
    mids = [coarse_rows(left, aps, ((CB, 2 * CB),), a0, a1, F32, 1.0)[0] for a0, a1 in chunks]
    early, mids = lax.optimization_barrier((early, mids))
    lower = jnp.concatenate([early, late], axis=1)
    totals, fars = [], []
    for (a0, a1), high, mid in zip(chunks, highs, mids):
        total = columns(high, 0) + columns(mid, 1) + columns(lower[:, :, a0 * BS : a1 * BS], 2)
        totals.append(total.astype(BF).reshape((share * (GROUPS + 2),) + total.shape[2:]))
        fars.append([over_y(totals[-1], s) for s in range(1, ny)])
    fars[0], totals[1] = lax.optimization_barrier((fars[0], totals[1]))
    out = None
    for (a0, a1), total, far in zip(chunks, totals, fars):
        if out is not None:
            far, out = lax.optimization_barrier((far, out))
        srcs = [z for g in [total] + far for z in (g, over_core(g))]
        out = assemble(order, srcs, a0, BS * BS, out)
    return out


def solution(mesh):
    return jax.shard_map(
        body,
        mesh=mesh,
        in_specs=(P("row", "col", None), P("row", None), P("row"), P("row", None, None), P()),
        out_specs=P("row", None, None),
        check_vma=False,
    )
```

```python
import functools

import jax
import jax.numpy as jnp
from jax import lax
from jax.experimental import pallas as pl
from jax.experimental.pallas import tpu as pltpu
from jax.sharding import PartitionSpec as P

BS = 64
CB = 8
GROUPS = 5
LANES = 128
BF = jnp.bfloat16
F32 = jnp.float32
MIB = 1 << 20

VM = pl.BlockSpec(memory_space=pltpu.VMEM)
SM = pl.BlockSpec(memory_space=pltpu.SMEM)


def params(mib):
    return pltpu.CompilerParams(vmem_limit_bytes=mib * MIB)


def cost(us):
    return pl.CostEstimate(flops=int(us * 1e8), bytes_accessed=int(us * 3.7e6), transcendentals=0)


def low_lanes(rows):
    return lax.broadcasted_iota(jnp.int32, (rows, LANES), 1) < BS


def dot(a, b):
    return lax.dot_general(a, b, (((1,), (0,)), ((), ())), preferred_element_type=F32)


def relayout_kernel(x_ref, o_ref, scr):
    rows, nb, _ = x_ref.shape
    low = low_lanes(32)
    for r in range(rows):
        for q in range(32):
            scr[r, pl.ds(q * 8, nb), :] = x_ref[r, :, q * LANES : (q + 1) * LANES].astype(F32)
        for k in range(0, nb, 2):
            x0 = scr[r, pl.ds(k, 32, stride=8), :]
            x1 = scr[r, pl.ds(k + 1, 32, stride=8), :]
            o_ref[r, k // 2, 0:32] = jnp.where(low, x0, pltpu.roll(x1, BS, 1)).astype(BF)
            o_ref[r, k // 2, 32:64] = jnp.where(low, pltpu.roll(x0, BS, 1), x1).astype(BF)


def relayout(x, first, rows):
    nb = x.shape[1]
    step = 4
    return pl.pallas_call(
        relayout_kernel,
        grid=(rows // step,),
        out_shape=jax.ShapeDtypeStruct((rows, nb // 2, BS, LANES), BF),
        in_specs=[pl.BlockSpec((step, nb, BS * BS), lambda i: (i + first // step, 0, 0))],
        out_specs=pl.BlockSpec((step, nb // 2, BS, LANES), lambda i: (i, 0, 0, 0)),
        scratch_shapes=[pltpu.VMEM((step, 256, LANES), F32)],
        compiler_params=params(4),
        cost_estimate=cost(0.6),
        name="relayout",
    )(x)


def relayout_rows_kernel(x_ref, o_ref, scr, mix):
    rows, nb, _ = x_ref.shape
    low = low_lanes(32)
    for r in range(rows):
        for q in range(32):
            scr[r, pl.ds(q * 8, nb), :] = x_ref[r, :, q * LANES : (q + 1) * LANES].astype(F32)
        for k in range(0, nb, 2):
            x0 = scr[r, pl.ds(k, 32, stride=8), :]
            x1 = scr[r, pl.ds(k + 1, 32, stride=8), :]
            mix[r, k // 2, pl.ds(0, 32, stride=2), :] = jnp.where(low, x0, pltpu.roll(x1, BS, 1))
            mix[r, k // 2, pl.ds(1, 32, stride=2), :] = jnp.where(low, pltpu.roll(x0, BS, 1), x1)
            o_ref[r, k // 2] = mix[r, k // 2].astype(BF)


def relayout_rows(x):
    rows, nb, _ = x.shape
    step = 4
    return pl.pallas_call(
        relayout_rows_kernel,
        grid=(rows // step,),
        out_shape=jax.ShapeDtypeStruct((rows, nb // 2, BS, LANES), BF),
        in_specs=[pl.BlockSpec((step, nb, BS * BS), lambda i: (i, 0, 0))],
        out_specs=pl.BlockSpec((step, nb // 2, BS, LANES), lambda i: (i, 0, 0, 0)),
        scratch_shapes=[pltpu.VMEM((step, 256, LANES), F32), pltpu.VMEM((step, nb // 2, BS, LANES), F32)],
        compiler_params=params(4),
        cost_estimate=cost(1.0),
        name="relayout_rows",
    )(x)


def left_kernel(rb, pct_ref, pl_ref, o_ref):
    slab = lax.axis_index("row")
    low = low_lanes(4 * BS)
    o_ref[...] = jnp.zeros_like(o_ref)

    def pair(ip, carry):
        for half in range(2):
            i = ip * 2 + half
            x = jnp.concatenate([pl_ref[i, 0], pl_ref[i, 1]], axis=1).astype(F32)
            xt = jnp.concatenate([x, x], axis=0).T
            keep = jnp.where(low if half == 0 else jnp.logical_not(low), xt, 0.0)
            for s in range(4):
                w = pct_ref[s, slab * rb + i] - (slab - 1) * CB
                o_ref[ip, w] = (o_ref[ip, w].astype(F32) + keep[s * BS : (s + 1) * BS]).astype(BF)
        return carry

    lax.fori_loop(0, rb // 2, pair, 0)


def left_factor(pct, p_own):
    rb = p_own.shape[0]
    return pl.pallas_call(
        functools.partial(left_kernel, rb),
        out_shape=jax.ShapeDtypeStruct((rb // 2, 3 * CB, BS, LANES), BF),
        in_specs=[SM, VM],
        out_specs=VM,
        compiler_params=params(12),
        cost_estimate=cost(2.9),
        name="left_factor",
    )(pct, p_own)


def column_table(pct, rb, share):
    slab = lax.axis_index("row")
    padded = jnp.pad(pct, ((0, 0), (rb, rb)), constant_values=-1000000)
    near = lax.dynamic_slice_in_dim(padded, slab * rb, 3 * rb, 1)
    w = near - (slab - 2) * CB
    e = (w & (CB - 1)) - share * lax.axis_index("col")
    return jnp.where((w >= 0) & (e >= 0) & (e < share), e * GROUPS + (w >> 3), -1)


def touched(side, tiles):
    return (side, side + 3) if tiles == GROUPS else (0, tiles)


def right_kernel(rb, tiles, table_ref, *refs):
    o_ref = refs[-1]
    core = lax.rem(lax.axis_index("col"), 2)
    low = lax.broadcasted_iota(jnp.int32, (1, LANES), 1) < BS
    wants = [jnp.where(low, p, tiles + p) for p in range(tiles)]

    def fill(src, side, out_first):
        def four(jq, carry):
            for d in range(4):
                jj = 4 * jq + d
                dups = []
                for t in range(4):
                    x = src[jj, t // 2, :, t % 2 * BS : (t % 2 + 1) * BS]
                    dups.append(jnp.concatenate([x, x], axis=1))
                at = [table_ref[t, side * rb + jj] for t in range(4)]
                for p in range(*touched(side, tiles)):
                    total = None
                    for t in range(4):
                        keep = dups[t] * jnp.where(wants[p] == at[t], 1.0, 0.0).astype(BF)
                        total = keep if total is None else total + keep
                    o_ref[out_first + jq, p, d * BS : (d + 1) * BS] = total
            return carry

        lax.fori_loop(0, rb // 4, four, 0)

    if len(refs) == 2:
        fill(refs[0], 1, 0)
    else:
        first = refs[0]
        second = refs[1]

        @pl.when(core == 0)
        def _():
            fill(first, 0, 0)
            fill(second, 2, rb // 4)

        @pl.when(core == 1)
        def _():
            fill(second, 0, 0)
            fill(first, 2, rb // 4)


def right_factor(table, srcs, tiles, us):
    rb = table.shape[1] // 3
    return pl.pallas_call(
        functools.partial(right_kernel, rb, tiles),
        out_shape=jax.ShapeDtypeStruct((len(srcs) * rb // 4, tiles, 4 * BS, LANES), BF),
        in_specs=[SM] + [VM] * len(srcs),
        out_specs=VM,
        compiler_params=params(8),
        cost_estimate=cost(us),
        name="right_factor",
    )(table, *srcs)


def slot_places(a_cols, counts):
    rb, ka = a_cols.shape
    row = jnp.arange(rb, dtype=jnp.int32)[:, None]
    near = a_cols - (lax.axis_index("row") - 1) * rb - row // 4 * 4
    live = jnp.arange(ka, dtype=jnp.int32)[None, :] < counts[:, None]
    return jnp.where(live, near, 2 * (rb + 2))


def first_slots(shifts, ks):
    col = lax.axis_index("col")
    ny = lax.axis_size("col") // 2
    y, core = col // 2, lax.rem(col, 2)
    slots = []
    for s, flip in shifts:
        c = core if flip == 0 else 1 - core
        slots.append((lax.rem(y - s + ny, ny) * 2 + c) * ks)
    return slots


def lay(first, place_ref, srcs, slots, band, start):
    low = low_lanes(BS)
    zero = jnp.zeros((BS, LANES), BF)

    def group(g, carry):
        for t in range(band.shape[1]):
            band[g, t] = start(g, t)
        for src, slot in zip(srcs, slots):
            for k in range(src.shape[1]):
                for d0 in range(0, 4, 2):
                    cuts = []
                    for d in range(d0, d0 + 2):
                        x = src[4 * g + d, k]
                        r = jnp.concatenate([x[:, BS:], x[:, :BS]], axis=1)
                        cuts.append(
                            (
                                (jnp.where(low, x, zero), jnp.where(low, zero, r)),
                                (jnp.where(low, r, zero), jnp.where(low, zero, x)),
                            )
                        )
                    for e in range(2):
                        at = [place_ref[first + 4 * g + d0 + d, slot + 2 * k + e] for d in range(2)]
                        spots = [(g, a >> 1, slice((d0 + d) * BS, (d0 + d + 1) * BS)) for d, a in enumerate(at)]
                        old = [band[spot] for spot in spots]
                        for spot, a, x, cut in zip(spots, at, old, cuts):
                            band[spot] = x + jnp.where((a & 1) == 0, cut[e][0], cut[e][1])
        return carry

    lax.fori_loop(0, band.shape[0], group, 0)


def band_kernel(first, shifts, place_ref, *refs):
    srcs, band = refs[:-1], refs[-1]
    slots = first_slots(shifts, srcs[0].shape[1] * 2)
    lay(first, place_ref, srcs, slots, band, lambda g, t: jnp.zeros((4 * BS, LANES), BF))


def near_band(place, srcs, shifts, first):
    rows = srcs[0].shape[0]
    return pl.pallas_call(
        functools.partial(band_kernel, first, shifts),
        out_shape=jax.ShapeDtypeStruct((rows // 4, place.shape[0] + 3, 4 * BS, LANES), BF),
        in_specs=[SM] + [VM] * len(srcs),
        out_specs=VM,
        compiler_params=params(12),
        cost_estimate=cost(0.16 * rows),
        name="near_band",
    )(place, *srcs)


def product_kernel(first, rb, shifts, place_ref, own_ref, near_ref, start_ref, *refs):
    srcs = refs[: len(shifts)]
    o_ref, band, acc = refs[len(shifts) :]
    rows = o_ref.shape[0]
    tiles = own_ref.shape[1]
    wide = rb + 2
    slots = first_slots(shifts, srcs[0].shape[1] * 2)
    lay(first, place_ref, srcs, slots, band, lambda g, t: start_ref[g, t])
    quads = rb // 4
    for g in range(rows // 4):
        start = first // 4 + g
        acc[...] = jnp.zeros_like(acc)
        for side in range(3):
            k0, k1 = max(start, side * quads), min(start + wide // 2, (side + 1) * quads)
            if k0 >= k1:
                continue
            p0, p1 = touched(side, tiles)
            ref, base = (own_ref, quads) if side == 1 else (near_ref, 0 if side == 0 else quads)
            total = None
            for k in range(k0, k1):
                lhs = jnp.concatenate([band[g, 2 * (k - start)], band[g, 2 * (k - start) + 1]], axis=1)
                rhs = jnp.concatenate([ref[k - base, p] for p in range(p0, p1)], axis=1)
                part = dot(lhs, rhs)
                total = part if total is None else total + part
            acc[:, p0 * LANES : p1 * LANES] += total
        for d in range(4):
            o_ref[4 * g + d] = acc[d * BS : (d + 1) * BS].astype(BF)


def product(place, own, near, start, srcs, shifts, first, us):
    rows = srcs[0].shape[0]
    rb = place.shape[0]
    tiles = own.shape[1]
    return pl.pallas_call(
        functools.partial(product_kernel, first, rb, shifts),
        out_shape=jax.ShapeDtypeStruct((rows, BS, tiles * LANES), BF),
        in_specs=[SM] + [VM] * (3 + len(srcs)),
        out_specs=VM,
        scratch_shapes=[
            pltpu.VMEM(start.shape, BF),
            pltpu.VMEM((4 * BS, tiles * LANES), F32),
        ],
        compiler_params=params(16),
        cost_estimate=cost(us),
        name="product",
    )(place, own, near, start, *srcs)


def coarse_kernel(sets, a0, a1, left_ref, *refs):
    outs = refs[-1 - len(sets) : -1]
    aps = refs[: -1 - len(sets)]
    scr = refs[-1]
    ac = a1 - a0
    tiles = aps[0].shape[2] // LANES
    for out, (i0, i1) in zip(outs, sets):
        rows = i1 - i0
        low = low_lanes(rows)
        for p0 in range(0, tiles, 2):
            p1 = min(p0 + 2, tiles)
            acc = jnp.zeros((rows * ac, (p1 - p0) * LANES), F32)
            ip = 0
            for ap in aps:
                for g in range(0, ap.shape[0] // 2, 2):
                    lhs = [left_ref[ip + d, i0:i1, a0:a1].reshape(rows * ac, LANES) for d in range(2)]
                    rhs = ap[2 * g : 2 * g + 4, :, p0 * LANES : p1 * LANES].reshape(4 * BS, (p1 - p0) * LANES)
                    acc = acc + dot(jnp.concatenate(lhs, axis=1), rhs)
                    ip += 2
            for p in range(p0, p1):
                scr[p, 0 : rows * ac] = acc[:, (p - p0) * LANES : (p - p0 + 1) * LANES]
        for p in range(tiles):
            for a in range(0, ac, 2):
                x0 = scr[p, pl.ds(a, rows, stride=ac), :]
                x1 = scr[p, pl.ds(a + 1, rows, stride=ac), :]
                at = slice(a * BS, (a + 2) * BS)
                out[p, :, at] = jnp.where(low, x0, pltpu.roll(x1, BS, 1)).astype(out.dtype)
                out[tiles + p, :, at] = jnp.where(low, pltpu.roll(x0, BS, 1), x1).astype(out.dtype)


def coarse_rows(left, aps, sets, a0, a1, dtype, us):
    tiles = aps[0].shape[2] // LANES
    return pl.pallas_call(
        functools.partial(coarse_kernel, sets, a0, a1),
        out_shape=[jax.ShapeDtypeStruct((2 * tiles, i1 - i0, (a1 - a0) * BS), dtype) for i0, i1 in sets],
        in_specs=[VM] * (1 + len(aps)),
        out_specs=[VM] * len(sets),
        scratch_shapes=[pltpu.VMEM((tiles, max(i1 - i0 for i0, i1 in sets) * (a1 - a0), LANES), F32)],
        compiler_params=params(12),
        cost_estimate=cost(us),
        name="coarse",
    )(left, *aps)


def assemble_kernel(order_ref, *refs):
    out = refs[-1]
    srcs = refs[:-1] if len(refs) % 2 else refs[1:-1]
    x = jnp.concatenate([s[...].reshape(-1, s.shape[2]) for s in srcs], axis=0)
    res = dot(order_ref[...], x)
    wide = out.shape[1]
    for i in range(CB):
        out[i] = res[i * wide : (i + 1) * wide].astype(BF)


def assemble(order, srcs, a0, total, before):
    n, _, lanes = srcs[0].shape
    step = 512
    per = lanes // step
    wide = n * len(srcs)
    specs = [pl.BlockSpec(order.shape, lambda i: (0, 0))]
    args = [order]
    alias = {}
    if before is not None:
        specs.append(pl.BlockSpec(memory_space=pl.ANY))
        args.append(before)
        alias = {1: 0}
    specs += [pl.BlockSpec((n, CB, step), lambda i: (0, 0, i))] * len(srcs)
    return pl.pallas_call(
        assemble_kernel,
        grid=(per,),
        out_shape=jax.ShapeDtypeStruct((CB, wide, total), BF),
        in_specs=specs,
        out_specs=pl.BlockSpec((CB, wide, step), lambda i: (0, 0, a0 * BS // step + i)),
        input_output_aliases=alias,
        compiler_params=params(12),
        cost_estimate=cost(2.9),
        name="assemble",
    )(*args, *srcs)


def assembly_order(shifts, ncol, share):
    col = lax.axis_index("col")
    y, core = col // 2, col % 2
    groups = GROUPS + 2
    size = ncol * share * groups * CB
    out_row = lax.broadcasted_iota(jnp.int32, (size, size), 0)
    src_row = lax.broadcasted_iota(jnp.int32, (size, size), 1)
    per = share * groups * CB
    which, rest = src_row // per, src_row % per
    e, g, i = rest // (groups * CB), rest // CB % groups, rest % CB
    src_col = jnp.zeros_like(which)
    for z, (s, flip) in enumerate(shifts):
        c = (y - s) % (ncol // 2) * 2 + (core + flip) % 2
        src_col = jnp.where(which == z, c, src_col)
    return (out_row == i * (groups * CB) + g * CB + share * src_col + e).astype(BF)


def body(a_blocks, a_cols, counts, p_blocks, p_cols):
    rb, ks, _ = a_blocks.shape
    nrow, ncol = lax.axis_size("row"), lax.axis_size("col")
    ny = ncol // 2
    nfb = p_cols.shape[0]
    share = CB // ncol
    tiles = (GROUPS * share + 1) // 2
    parts = ((0, rb * 2 // 3), (rb * 2 // 3, rb // 3))
    chunks = ((0, 32), (32, 64))

    def outward(x):
        pairs = [(r * ncol + c, (r + 1 - 2 * (c % 2)) * ncol + c) for r in range(nrow) for c in range(ncol)]
        return lax.ppermute(x, ("row", "col"), [(a, b) for a, b in pairs if 0 <= b < nrow * ncol])

    def over_y(x, s):
        return lax.ppermute(x, "col", [(y * 2 + c, (y + s) % ny * 2 + c) for y in range(ny) for c in range(2)])

    def over_core(x):
        return lax.ppermute(x, "col", [(c, c ^ 1) for c in range(ncol)])

    def upward(x):
        return lax.ppermute(x, "row", [(i, i + 1) for i in range(nrow - 1)])

    def downward(x):
        return lax.ppermute(x, "row", [(i + 1, i) for i in range(nrow - 1)])

    shifts = tuple((s, f) for s in range(ny) for f in range(2))
    pct = p_cols.T

    own_a, side_a, far_a = [], [], []
    for h, (first, rows) in enumerate(parts):
        x = relayout(a_blocks, first, rows)
        own_a.append(x)
        far_a.append([over_y(x, s) for s in range(1, ny)])
        side_a.append(over_core(x))
        if h == 0:
            a_blocks, p_blocks, side_a[0] = lax.optimization_barrier((a_blocks, p_blocks, side_a[0]))
    p_own = relayout_rows(p_blocks)
    beside = outward(p_own)
    p_blocks, p_own, side_a[1] = lax.optimization_barrier((p_blocks, p_own, side_a[1]))
    table = column_table(pct, rb, share)
    left = left_factor(pct, relayout(p_blocks, 0, rb))
    own = right_factor(table, [p_own], tiles, 2.0)
    order = assembly_order(shifts, ncol, share)
    place = slot_places(a_cols, counts)
    bands = [near_band(place, [own_a[h], side_a[h]], shifts[:2], parts[h][0]) for h in range(2)]
    beside, far_a[0], left, own, order, bands = lax.optimization_barrier((beside, far_a[0], left, own, order, bands))
    near = right_factor(table, [beside, over_core(beside)], tiles, 3.0)
    aps = []
    for h in range(2):
        srcs = [z for g in far_a[h] for z in (g, over_core(g))]
        aps.append(product(place, own, near, bands[h], srcs, shifts[2:], parts[h][0], 0.3 * parts[h][1]))
        if h == 0:
            far_a[1], aps[0] = lax.optimization_barrier((far_a[1], aps[0]))
            early = downward(coarse_rows(left, aps, ((0, CB // 2),), 0, BS, BF, 1.0)[0])

    def columns(x, g):
        y = x[: GROUPS * share].reshape((share, GROUPS) + x.shape[1:])
        return jnp.pad(y.astype(F32), ((0, 0), (g, 2 - g), (0, 0), (0, 0)))

    rims = []
    for a0, a1 in chunks:
        low = coarse_rows(left, aps, ((CB // 2, CB),), a0, a1, BF, 1.0)[0]
        high = coarse_rows(left, aps, ((2 * CB, 3 * CB),), a0, a1, BF, 1.0)[0]
        rims.append((downward(low), upward(high)))
    mids = [coarse_rows(left, aps, ((CB, 2 * CB),), a0, a1, F32, 1.0)[0] for a0, a1 in chunks]
    totals, fars = [], []
    for (a0, a1), (low, high), mid in zip(chunks, rims, mids):
        lower = jnp.concatenate([early[:, :, a0 * BS : a1 * BS], low], axis=1)
        total = columns(high, 0) + columns(mid, 1) + columns(lower, 2)
        totals.append(total.astype(BF).reshape((share * (GROUPS + 2),) + total.shape[2:]))
        fars.append([over_y(totals[-1], s) for s in range(1, ny)])
    fars[0], totals[1] = lax.optimization_barrier((fars[0], totals[1]))
    sides = [over_core(x) for x in totals]
    beyond = [over_core(x) for x in fars[0]]
    fars[1], beyond = lax.optimization_barrier((fars[1], beyond))
    beyond = [beyond, [over_core(x) for x in fars[1]]]
    out = None
    for z, (a0, a1) in enumerate(chunks):
        srcs = [totals[z], sides[z]] + [q for pair in zip(fars[z], beyond[z]) for q in pair]
        out = assemble(order, srcs, a0, BS * BS, out)
    return out


def solution(mesh):
    return jax.shard_map(
        body,
        mesh=mesh,
        in_specs=(P("row", "col", None), P("row", None), P("row"), P("row", None, None), P()),
        out_specs=P("row", None, None),
        check_vma=False,
    )
```

```python
import functools

import jax
import jax.numpy as jnp
from jax import lax
from jax.experimental import pallas as pl
from jax.experimental.pallas import tpu as pltpu
from jax.sharding import PartitionSpec as P

BS = 64
CB = 8
GROUPS = 5
LANES = 128
BF = jnp.bfloat16
F32 = jnp.float32
MIB = 1 << 20

VM = pl.BlockSpec(memory_space=pltpu.VMEM)
SM = pl.BlockSpec(memory_space=pltpu.SMEM)


def params(mib):
    return pltpu.CompilerParams(vmem_limit_bytes=mib * MIB)


def cost(us):
    return pl.CostEstimate(flops=int(us * 1e8), bytes_accessed=int(us * 3.7e6), transcendentals=0)


def low_lanes(rows):
    return lax.broadcasted_iota(jnp.int32, (rows, LANES), 1) < BS


def dot(a, b):
    return lax.dot_general(a, b, (((1,), (0,)), ((), ())), preferred_element_type=F32)


def relayout_kernel(x_ref, o_ref, scr):
    rows, nb, _ = x_ref.shape
    low = low_lanes(32)
    for r in range(rows):
        for q in range(32):
            scr[r, pl.ds(q * 8, nb), :] = x_ref[r, :, q * LANES : (q + 1) * LANES].astype(F32)
        for k in range(0, nb, 2):
            x0 = scr[r, pl.ds(k, 32, stride=8), :]
            x1 = scr[r, pl.ds(k + 1, 32, stride=8), :]
            o_ref[r, k // 2, 0:32] = jnp.where(low, x0, pltpu.roll(x1, BS, 1)).astype(BF)
            o_ref[r, k // 2, 32:64] = jnp.where(low, pltpu.roll(x0, BS, 1), x1).astype(BF)


def relayout(x, first, rows):
    nb = x.shape[1]
    step = 4
    return pl.pallas_call(
        relayout_kernel,
        grid=(rows // step,),
        out_shape=jax.ShapeDtypeStruct((rows, nb // 2, BS, LANES), BF),
        in_specs=[pl.BlockSpec((step, nb, BS * BS), lambda i: (i + first // step, 0, 0))],
        out_specs=pl.BlockSpec((step, nb // 2, BS, LANES), lambda i: (i, 0, 0, 0)),
        scratch_shapes=[pltpu.VMEM((step, 256, LANES), F32)],
        compiler_params=params(4),
        cost_estimate=cost(0.6),
        name="relayout",
    )(x)


def relayout_rows_kernel(x_ref, o_ref, scr, mix):
    rows, nb, _ = x_ref.shape
    low = low_lanes(32)
    for r in range(rows):
        for q in range(32):
            scr[r, pl.ds(q * 8, nb), :] = x_ref[r, :, q * LANES : (q + 1) * LANES].astype(F32)
        for k in range(0, nb, 2):
            x0 = scr[r, pl.ds(k, 32, stride=8), :]
            x1 = scr[r, pl.ds(k + 1, 32, stride=8), :]
            mix[r, k // 2, pl.ds(0, 32, stride=2), :] = jnp.where(low, x0, pltpu.roll(x1, BS, 1))
            mix[r, k // 2, pl.ds(1, 32, stride=2), :] = jnp.where(low, pltpu.roll(x0, BS, 1), x1)
            o_ref[r, k // 2] = mix[r, k // 2].astype(BF)


def relayout_rows(x):
    rows, nb, _ = x.shape
    step = 4
    return pl.pallas_call(
        relayout_rows_kernel,
        grid=(rows // step,),
        out_shape=jax.ShapeDtypeStruct((rows, nb // 2, BS, LANES), BF),
        in_specs=[pl.BlockSpec((step, nb, BS * BS), lambda i: (i, 0, 0))],
        out_specs=pl.BlockSpec((step, nb // 2, BS, LANES), lambda i: (i, 0, 0, 0)),
        scratch_shapes=[pltpu.VMEM((step, 256, LANES), F32), pltpu.VMEM((step, nb // 2, BS, LANES), F32)],
        compiler_params=params(4),
        cost_estimate=cost(1.0),
        name="relayout_rows",
    )(x)


def left_kernel(rb, pct_ref, pl_ref, o_ref):
    slab = lax.axis_index("row")
    low = low_lanes(4 * BS)
    o_ref[...] = jnp.zeros_like(o_ref)

    def pair(ip, carry):
        for half in range(2):
            i = ip * 2 + half
            x = jnp.concatenate([pl_ref[i, 0], pl_ref[i, 1]], axis=1).astype(F32)
            xt = jnp.concatenate([x, x], axis=0).T
            keep = jnp.where(low if half == 0 else jnp.logical_not(low), xt, 0.0)
            for s in range(4):
                w = pct_ref[s, slab * rb + i] - (slab - 1) * CB
                o_ref[ip, w] = (o_ref[ip, w].astype(F32) + keep[s * BS : (s + 1) * BS]).astype(BF)
        return carry

    lax.fori_loop(0, rb // 2, pair, 0)


def left_factor(pct, p_own):
    rb = p_own.shape[0]
    return pl.pallas_call(
        functools.partial(left_kernel, rb),
        out_shape=jax.ShapeDtypeStruct((rb // 2, 3 * CB, BS, LANES), BF),
        in_specs=[SM, VM],
        out_specs=VM,
        compiler_params=params(12),
        cost_estimate=cost(2.9),
        name="left_factor",
    )(pct, p_own)


def column_table(pct, rb, share):
    slab = lax.axis_index("row")
    padded = jnp.pad(pct, ((0, 0), (rb, rb)), constant_values=-1000000)
    near = lax.dynamic_slice_in_dim(padded, slab * rb, 3 * rb, 1)
    w = near - (slab - 2) * CB
    e = (w & (CB - 1)) - share * lax.axis_index("col")
    return jnp.where((w >= 0) & (e >= 0) & (e < share), e * GROUPS + (w >> 3), -1)


def touched(side, tiles):
    return (side, side + 3) if tiles == GROUPS else (0, tiles)


def right_kernel(rb, tiles, table_ref, *refs):
    o_ref = refs[-1]
    core = lax.rem(lax.axis_index("col"), 2)
    low = lax.broadcasted_iota(jnp.int32, (1, LANES), 1) < BS
    wants = [jnp.where(low, p, tiles + p) for p in range(tiles)]

    def fill(src, side, out_first):
        def four(jq, carry):
            for d in range(4):
                jj = 4 * jq + d
                dups = []
                for t in range(4):
                    x = src[jj, t // 2, :, t % 2 * BS : (t % 2 + 1) * BS]
                    dups.append(jnp.concatenate([x, x], axis=1))
                at = [table_ref[t, side * rb + jj] for t in range(4)]
                for p in range(*touched(side, tiles)):
                    total = None
                    for t in range(4):
                        keep = dups[t] * jnp.where(wants[p] == at[t], 1.0, 0.0).astype(BF)
                        total = keep if total is None else total + keep
                    o_ref[out_first + jq, p, d * BS : (d + 1) * BS] = total
            return carry

        lax.fori_loop(0, rb // 4, four, 0)

    if len(refs) == 2:
        fill(refs[0], 1, 0)
    else:
        first = refs[0]
        second = refs[1]

        @pl.when(core == 0)
        def _():
            fill(first, 0, 0)
            fill(second, 2, rb // 4)

        @pl.when(core == 1)
        def _():
            fill(second, 0, 0)
            fill(first, 2, rb // 4)


def right_factor(table, srcs, tiles, us):
    rb = table.shape[1] // 3
    return pl.pallas_call(
        functools.partial(right_kernel, rb, tiles),
        out_shape=jax.ShapeDtypeStruct((len(srcs) * rb // 4, tiles, 4 * BS, LANES), BF),
        in_specs=[SM] + [VM] * len(srcs),
        out_specs=VM,
        compiler_params=params(8),
        cost_estimate=cost(us),
        name="right_factor",
    )(table, *srcs)


def slot_places(a_cols, counts):
    rb, ka = a_cols.shape
    row = jnp.arange(rb, dtype=jnp.int32)[:, None]
    near = a_cols - (lax.axis_index("row") - 1) * rb - row // 4 * 4
    live = jnp.arange(ka, dtype=jnp.int32)[None, :] < counts[:, None]
    return jnp.where(live, near, 2 * (rb + 2))


def first_slots(shifts, ks):
    col = lax.axis_index("col")
    ny = lax.axis_size("col") // 2
    y, core = col // 2, lax.rem(col, 2)
    slots = []
    for s, flip in shifts:
        c = core if flip == 0 else 1 - core
        slots.append((lax.rem(y - s + ny, ny) * 2 + c) * ks)
    return slots


def lay(first, place_ref, srcs, slots, band, start):
    low = low_lanes(BS)
    zero = jnp.zeros((BS, LANES), BF)

    def group(g, carry):
        for t in range(band.shape[1]):
            band[g, t] = start(g, t)
        for src, slot in zip(srcs, slots):
            for k in range(src.shape[1]):
                for d0 in range(0, 4, 2):
                    cuts = []
                    for d in range(d0, d0 + 2):
                        x = src[4 * g + d, k]
                        r = jnp.concatenate([x[:, BS:], x[:, :BS]], axis=1)
                        cuts.append(
                            (
                                (jnp.where(low, x, zero), jnp.where(low, zero, r)),
                                (jnp.where(low, r, zero), jnp.where(low, zero, x)),
                            )
                        )
                    for e in range(2):
                        at = [place_ref[first + 4 * g + d0 + d, slot + 2 * k + e] for d in range(2)]
                        spots = [(g, a >> 1, slice((d0 + d) * BS, (d0 + d + 1) * BS)) for d, a in enumerate(at)]
                        old = [band[spot] for spot in spots]
                        for spot, a, x, cut in zip(spots, at, old, cuts):
                            band[spot] = x + jnp.where((a & 1) == 0, cut[e][0], cut[e][1])
        return carry

    lax.fori_loop(0, band.shape[0], group, 0)


def band_kernel(first, shifts, place_ref, *refs):
    srcs, band = refs[:-1], refs[-1]
    slots = first_slots(shifts, srcs[0].shape[1] * 2)
    lay(first, place_ref, srcs, slots, band, lambda g, t: jnp.zeros((4 * BS, LANES), BF))


def near_band(place, srcs, shifts, first):
    rows = srcs[0].shape[0]
    return pl.pallas_call(
        functools.partial(band_kernel, first, shifts),
        out_shape=jax.ShapeDtypeStruct((rows // 4, place.shape[0] + 3, 4 * BS, LANES), BF),
        in_specs=[SM] + [VM] * len(srcs),
        out_specs=VM,
        compiler_params=params(12),
        cost_estimate=cost(0.16 * rows),
        name="near_band",
    )(place, *srcs)


def product_kernel(first, rb, shifts, place_ref, own_ref, near_ref, start_ref, *refs):
    srcs = refs[: len(shifts)]
    o_ref, band, acc = refs[len(shifts) :]
    rows = o_ref.shape[0]
    tiles = own_ref.shape[1]
    wide = rb + 2
    slots = first_slots(shifts, srcs[0].shape[1] * 2)
    lay(first, place_ref, srcs, slots, band, lambda g, t: start_ref[g, t])
    quads = rb // 4
    for g in range(rows // 4):
        start = first // 4 + g
        acc[...] = jnp.zeros_like(acc)
        for side in range(3):
            k0, k1 = max(start, side * quads), min(start + wide // 2, (side + 1) * quads)
            if k0 >= k1:
                continue
            p0, p1 = touched(side, tiles)
            ref, base = (own_ref, quads) if side == 1 else (near_ref, 0 if side == 0 else quads)
            total = None
            for k in range(k0, k1):
                lhs = jnp.concatenate([band[g, 2 * (k - start)], band[g, 2 * (k - start) + 1]], axis=1)
                rhs = jnp.concatenate([ref[k - base, p] for p in range(p0, p1)], axis=1)
                part = dot(lhs, rhs)
                total = part if total is None else total + part
            acc[:, p0 * LANES : p1 * LANES] += total
        for d in range(4):
            o_ref[4 * g + d] = acc[d * BS : (d + 1) * BS].astype(BF)


def product(place, own, near, start, srcs, shifts, first, us):
    rows = srcs[0].shape[0]
    rb = place.shape[0]
    tiles = own.shape[1]
    return pl.pallas_call(
        functools.partial(product_kernel, first, rb, shifts),
        out_shape=jax.ShapeDtypeStruct((rows, BS, tiles * LANES), BF),
        in_specs=[SM] + [VM] * (3 + len(srcs)),
        out_specs=VM,
        scratch_shapes=[
            pltpu.VMEM(start.shape, BF),
            pltpu.VMEM((4 * BS, tiles * LANES), F32),
        ],
        compiler_params=params(16),
        cost_estimate=cost(us),
        name="product",
    )(place, own, near, start, *srcs)


def coarse_kernel(sets, a0, a1, left_ref, *refs):
    outs = refs[-1 - len(sets) : -1]
    aps = refs[: -1 - len(sets)]
    scr = refs[-1]
    ac = a1 - a0
    tiles = aps[0].shape[2] // LANES
    for out, (i0, i1) in zip(outs, sets):
        rows = i1 - i0
        low = low_lanes(rows)
        for p0 in range(0, tiles, 2):
            p1 = min(p0 + 2, tiles)
            acc = jnp.zeros((rows * ac, (p1 - p0) * LANES), F32)
            ip = 0
            for ap in aps:
                for g in range(0, ap.shape[0] // 2, 2):
                    lhs = [left_ref[ip + d, i0:i1, a0:a1].reshape(rows * ac, LANES) for d in range(2)]
                    rhs = ap[2 * g : 2 * g + 4, :, p0 * LANES : p1 * LANES].reshape(4 * BS, (p1 - p0) * LANES)
                    acc = acc + dot(jnp.concatenate(lhs, axis=1), rhs)
                    ip += 2
            for p in range(p0, p1):
                scr[p, 0 : rows * ac] = acc[:, (p - p0) * LANES : (p - p0 + 1) * LANES]
        for p in range(tiles):
            for a in range(0, ac, 2):
                x0 = scr[p, pl.ds(a, rows, stride=ac), :]
                x1 = scr[p, pl.ds(a + 1, rows, stride=ac), :]
                at = slice(a * BS, (a + 2) * BS)
                out[p, :, at] = jnp.where(low, x0, pltpu.roll(x1, BS, 1)).astype(out.dtype)
                out[tiles + p, :, at] = jnp.where(low, pltpu.roll(x0, BS, 1), x1).astype(out.dtype)


def coarse_rows(left, aps, sets, a0, a1, dtype, us):
    tiles = aps[0].shape[2] // LANES
    return pl.pallas_call(
        functools.partial(coarse_kernel, sets, a0, a1),
        out_shape=[jax.ShapeDtypeStruct((2 * tiles, i1 - i0, (a1 - a0) * BS), dtype) for i0, i1 in sets],
        in_specs=[VM] * (1 + len(aps)),
        out_specs=[VM] * len(sets),
        scratch_shapes=[pltpu.VMEM((tiles, max(i1 - i0 for i0, i1 in sets) * (a1 - a0), LANES), F32)],
        compiler_params=params(12),
        cost_estimate=cost(us),
        name="coarse",
    )(left, *aps)


def assemble_kernel(order_ref, *refs):
    out = refs[-1]
    srcs = refs[:-1] if len(refs) % 2 else refs[1:-1]
    x = jnp.concatenate([s[...].reshape(-1, s.shape[2]) for s in srcs], axis=0)
    res = dot(order_ref[...], x)
    wide = out.shape[1]
    for i in range(CB):
        out[i] = res[i * wide : (i + 1) * wide].astype(BF)


def assemble(order, srcs, a0, total, before):
    n, _, lanes = srcs[0].shape
    step = 512
    per = lanes // step
    wide = n * len(srcs)
    specs = [pl.BlockSpec(order.shape, lambda i: (0, 0))]
    args = [order]
    alias = {}
    if before is not None:
        specs.append(pl.BlockSpec(memory_space=pl.ANY))
        args.append(before)
        alias = {1: 0}
    specs += [pl.BlockSpec((n, CB, step), lambda i: (0, 0, i))] * len(srcs)
    return pl.pallas_call(
        assemble_kernel,
        grid=(per,),
        out_shape=jax.ShapeDtypeStruct((CB, wide, total), BF),
        in_specs=specs,
        out_specs=pl.BlockSpec((CB, wide, step), lambda i: (0, 0, a0 * BS // step + i)),
        input_output_aliases=alias,
        compiler_params=params(12),
        cost_estimate=cost(2.9),
        name="assemble",
    )(*args, *srcs)


def assembly_order(shifts, ncol, share):
    col = lax.axis_index("col")
    y, core = col // 2, col % 2
    groups = GROUPS + 2
    size = ncol * share * groups * CB
    out_row = lax.broadcasted_iota(jnp.int32, (size, size), 0)
    src_row = lax.broadcasted_iota(jnp.int32, (size, size), 1)
    per = share * groups * CB
    which, rest = src_row // per, src_row % per
    e, g, i = rest // (groups * CB), rest // CB % groups, rest % CB
    src_col = jnp.zeros_like(which)
    for z, (s, flip) in enumerate(shifts):
        c = (y - s) % (ncol // 2) * 2 + (core + flip) % 2
        src_col = jnp.where(which == z, c, src_col)
    return (out_row == i * (groups * CB) + g * CB + share * src_col + e).astype(BF)


def body(a_blocks, a_cols, counts, p_blocks, p_cols):
    rb, ks, _ = a_blocks.shape
    nrow, ncol = lax.axis_size("row"), lax.axis_size("col")
    ny = ncol // 2
    nfb = p_cols.shape[0]
    share = CB // ncol
    tiles = (GROUPS * share + 1) // 2
    parts = ((0, rb * 2 // 3), (rb * 2 // 3, rb // 3))
    chunks = ((0, 16), (16, 40), (40, 64))

    def outward(x):
        pairs = [(r * ncol + c, (r + 1 - 2 * (c % 2)) * ncol + c) for r in range(nrow) for c in range(ncol)]
        return lax.ppermute(x, ("row", "col"), [(a, b) for a, b in pairs if 0 <= b < nrow * ncol])

    def over_y(x, s):
        return lax.ppermute(x, "col", [(y * 2 + c, (y + s) % ny * 2 + c) for y in range(ny) for c in range(2)])

    def over_core(x):
        return lax.ppermute(x, "col", [(c, c ^ 1) for c in range(ncol)])

    def upward(x):
        return lax.ppermute(x, "row", [(i, i + 1) for i in range(nrow - 1)])

    def downward(x):
        return lax.ppermute(x, "row", [(i + 1, i) for i in range(nrow - 1)])

    shifts = tuple((s, f) for s in range(ny) for f in range(2))
    pct = p_cols.T

    own_a, side_a, far_a = [], [], []
    for h, (first, rows) in enumerate(parts):
        x = relayout(a_blocks, first, rows)
        own_a.append(x)
        far_a.append([over_y(x, s) for s in range(1, ny)])
        side_a.append(over_core(x))
        if h == 0:
            a_blocks, p_blocks, side_a[0] = lax.optimization_barrier((a_blocks, p_blocks, side_a[0]))
    p_own = relayout_rows(p_blocks)
    beside = outward(p_own)
    p_blocks, p_own, side_a[1] = lax.optimization_barrier((p_blocks, p_own, side_a[1]))
    table = column_table(pct, rb, share)
    left = left_factor(pct, relayout(p_blocks, 0, rb))
    own = right_factor(table, [p_own], tiles, 2.0)
    order = assembly_order(shifts, ncol, share)
    place = slot_places(a_cols, counts)
    bands = [near_band(place, [own_a[h], side_a[h]], shifts[:2], parts[h][0]) for h in range(2)]
    beside, far_a[0], left, own, order, bands = lax.optimization_barrier((beside, far_a[0], left, own, order, bands))
    near = right_factor(table, [beside, over_core(beside)], tiles, 3.0)
    aps = []
    for h in range(2):
        srcs = [z for g in far_a[h] for z in (g, over_core(g))]
        aps.append(product(place, own, near, bands[h], srcs, shifts[2:], parts[h][0], 0.3 * parts[h][1]))
        if h == 0:
            far_a[1], aps[0] = lax.optimization_barrier((far_a[1], aps[0]))
            early = downward(coarse_rows(left, aps, ((0, CB // 2),), 0, BS, BF, 1.0)[0])

    def columns(x, g):
        y = x[: GROUPS * share].reshape((share, GROUPS) + x.shape[1:])
        return jnp.pad(y.astype(F32), ((0, 0), (g, 2 - g), (0, 0), (0, 0)))

    late = downward(coarse_rows(left, aps, ((CB // 2, CB),), 0, BS, BF, 1.0)[0])
    highs = [upward(coarse_rows(left, aps, ((2 * CB, 3 * CB),), a0, a1, BF, 1.0)[0]) for a0, a1 in chunks]
    mids = [coarse_rows(left, aps, ((CB, 2 * CB),), a0, a1, F32, 1.0)[0] for a0, a1 in chunks]
    lower = jnp.concatenate([early, late], axis=1)
    totals, sides, fars, beyond = [], [], [], []
    for z, (a0, a1) in enumerate(chunks):
        total = columns(highs[z], 0) + columns(mids[z], 1) + columns(lower[:, :, a0 * BS : a1 * BS], 2)
        total = total.astype(BF).reshape((share * (GROUPS + 2),) + total.shape[2:])
        if z > 0:
            fars[-1], total = lax.optimization_barrier((fars[-1], total))
            beyond.append([over_core(x) for x in fars[-1]])
        totals.append(total)
        sides.append(over_core(total))
        fars.append([over_y(total, s) for s in range(1, ny)])
    out = None
    for z, (a0, a1) in enumerate(chunks):
        if z == len(chunks) - 1:
            fars[z], out = lax.optimization_barrier((fars[z], out))
            beyond.append([over_core(x) for x in fars[z]])
        srcs = [totals[z], sides[z]] + [q for pair in zip(fars[z], beyond[z]) for q in pair]
        out = assemble(order, srcs, a0, BS * BS, out)
    return out


def solution(mesh):
    return jax.shard_map(
        body,
        mesh=mesh,
        in_specs=(P("row", "col", None), P("row", None), P("row"), P("row", None, None), P()),
        out_specs=P("row", None, None),
        check_vma=False,
    )
```

```python
import functools

import jax
import jax.numpy as jnp
from jax import lax
from jax.experimental import pallas as pl
from jax.experimental.pallas import tpu as pltpu
from jax.sharding import PartitionSpec as P

BS = 64
CB = 8
GROUPS = 5
LANES = 128
BF = jnp.bfloat16
F32 = jnp.float32
MIB = 1 << 20

VM = pl.BlockSpec(memory_space=pltpu.VMEM)
SM = pl.BlockSpec(memory_space=pltpu.SMEM)


def params(mib):
    return pltpu.CompilerParams(vmem_limit_bytes=mib * MIB)


def cost(us):
    return pl.CostEstimate(flops=int(us * 1e8), bytes_accessed=int(us * 3.7e6), transcendentals=0)


def low_lanes(rows):
    return lax.broadcasted_iota(jnp.int32, (rows, LANES), 1) < BS


def dot(a, b):
    return lax.dot_general(a, b, (((1,), (0,)), ((), ())), preferred_element_type=F32)


def relayout_kernel(x_ref, o_ref, scr):
    rows, nb, _ = x_ref.shape
    low = low_lanes(32)
    for r in range(rows):
        for q in range(32):
            scr[r, pl.ds(q * 8, nb), :] = x_ref[r, :, q * LANES : (q + 1) * LANES].astype(F32)
        for k in range(0, nb, 2):
            x0 = scr[r, pl.ds(k, 32, stride=8), :]
            x1 = scr[r, pl.ds(k + 1, 32, stride=8), :]
            o_ref[r, k // 2, 0:32] = jnp.where(low, x0, pltpu.roll(x1, BS, 1)).astype(BF)
            o_ref[r, k // 2, 32:64] = jnp.where(low, pltpu.roll(x0, BS, 1), x1).astype(BF)


def relayout(x, first, rows):
    nb = x.shape[1]
    step = 4
    return pl.pallas_call(
        relayout_kernel,
        grid=(rows // step,),
        out_shape=jax.ShapeDtypeStruct((rows, nb // 2, BS, LANES), BF),
        in_specs=[pl.BlockSpec((step, nb, BS * BS), lambda i: (i + first // step, 0, 0))],
        out_specs=pl.BlockSpec((step, nb // 2, BS, LANES), lambda i: (i, 0, 0, 0)),
        scratch_shapes=[pltpu.VMEM((step, 256, LANES), F32)],
        compiler_params=params(4),
        cost_estimate=cost(0.6),
        name="relayout",
    )(x)


def relayout_rows_kernel(x_ref, o_ref, scr, mix):
    rows, nb, _ = x_ref.shape
    low = low_lanes(32)
    for r in range(rows):
        for q in range(32):
            scr[r, pl.ds(q * 8, nb), :] = x_ref[r, :, q * LANES : (q + 1) * LANES].astype(F32)
        for k in range(0, nb, 2):
            x0 = scr[r, pl.ds(k, 32, stride=8), :]
            x1 = scr[r, pl.ds(k + 1, 32, stride=8), :]
            mix[r, k // 2, pl.ds(0, 32, stride=2), :] = jnp.where(low, x0, pltpu.roll(x1, BS, 1))
            mix[r, k // 2, pl.ds(1, 32, stride=2), :] = jnp.where(low, pltpu.roll(x0, BS, 1), x1)
            o_ref[r, k // 2] = mix[r, k // 2].astype(BF)


def relayout_rows(x):
    rows, nb, _ = x.shape
    step = 4
    return pl.pallas_call(
        relayout_rows_kernel,
        grid=(rows // step,),
        out_shape=jax.ShapeDtypeStruct((rows, nb // 2, BS, LANES), BF),
        in_specs=[pl.BlockSpec((step, nb, BS * BS), lambda i: (i, 0, 0))],
        out_specs=pl.BlockSpec((step, nb // 2, BS, LANES), lambda i: (i, 0, 0, 0)),
        scratch_shapes=[pltpu.VMEM((step, 256, LANES), F32), pltpu.VMEM((step, nb // 2, BS, LANES), F32)],
        compiler_params=params(4),
        cost_estimate=cost(1.0),
        name="relayout_rows",
    )(x)


def left_kernel(rb, pct_ref, pl_ref, o_ref):
    slab = lax.axis_index("row")
    low = low_lanes(4 * BS)
    o_ref[...] = jnp.zeros_like(o_ref)

    def pair(ip, carry):
        for half in range(2):
            i = ip * 2 + half
            x = jnp.concatenate([pl_ref[i, 0], pl_ref[i, 1]], axis=1).astype(F32)
            xt = jnp.concatenate([x, x], axis=0).T
            keep = jnp.where(low if half == 0 else jnp.logical_not(low), xt, 0.0)
            for s in range(4):
                w = pct_ref[s, slab * rb + i] - (slab - 1) * CB
                o_ref[ip, w] = (o_ref[ip, w].astype(F32) + keep[s * BS : (s + 1) * BS]).astype(BF)
        return carry

    lax.fori_loop(0, rb // 2, pair, 0)


def left_factor(pct, p_own):
    rb = p_own.shape[0]
    return pl.pallas_call(
        functools.partial(left_kernel, rb),
        out_shape=jax.ShapeDtypeStruct((rb // 2, 3 * CB, BS, LANES), BF),
        in_specs=[SM, VM],
        out_specs=VM,
        compiler_params=params(12),
        cost_estimate=cost(2.9),
        name="left_factor",
    )(pct, p_own)


def column_table(pct, rb, share):
    slab = lax.axis_index("row")
    padded = jnp.pad(pct, ((0, 0), (rb, rb)), constant_values=-1000000)
    near = lax.dynamic_slice_in_dim(padded, slab * rb, 3 * rb, 1)
    w = near - (slab - 2) * CB
    e = (w & (CB - 1)) - share * lax.axis_index("col")
    return jnp.where((w >= 0) & (e >= 0) & (e < share), e * GROUPS + (w >> 3), -1)


def touched(side, tiles):
    return (side, side + 3) if tiles == GROUPS else (0, tiles)


def right_kernel(rb, tiles, table_ref, *refs):
    o_ref = refs[-1]
    core = lax.rem(lax.axis_index("col"), 2)
    low = lax.broadcasted_iota(jnp.int32, (1, LANES), 1) < BS
    wants = [jnp.where(low, p, tiles + p) for p in range(tiles)]

    def fill(src, side, out_first):
        def four(jq, carry):
            for d in range(4):
                jj = 4 * jq + d
                dups = []
                for t in range(4):
                    x = src[jj, t // 2, :, t % 2 * BS : (t % 2 + 1) * BS]
                    dups.append(jnp.concatenate([x, x], axis=1))
                at = [table_ref[t, side * rb + jj] for t in range(4)]
                for p in range(*touched(side, tiles)):
                    total = None
                    for t in range(4):
                        keep = dups[t] * jnp.where(wants[p] == at[t], 1.0, 0.0).astype(BF)
                        total = keep if total is None else total + keep
                    o_ref[out_first + jq, p, d * BS : (d + 1) * BS] = total
            return carry

        lax.fori_loop(0, rb // 4, four, 0)

    if len(refs) == 2:
        fill(refs[0], 1, 0)
    else:
        first = refs[0]
        second = refs[1]

        @pl.when(core == 0)
        def _():
            fill(first, 0, 0)
            fill(second, 2, rb // 4)

        @pl.when(core == 1)
        def _():
            fill(second, 0, 0)
            fill(first, 2, rb // 4)


def right_factor(table, srcs, tiles, us):
    rb = table.shape[1] // 3
    return pl.pallas_call(
        functools.partial(right_kernel, rb, tiles),
        out_shape=jax.ShapeDtypeStruct((len(srcs) * rb // 4, tiles, 4 * BS, LANES), BF),
        in_specs=[SM] + [VM] * len(srcs),
        out_specs=VM,
        compiler_params=params(8),
        cost_estimate=cost(us),
        name="right_factor",
    )(table, *srcs)


def slot_places(a_cols, counts):
    rb, ka = a_cols.shape
    row = jnp.arange(rb, dtype=jnp.int32)[:, None]
    near = a_cols - (lax.axis_index("row") - 1) * rb - row // 4 * 4
    live = jnp.arange(ka, dtype=jnp.int32)[None, :] < counts[:, None]
    return jnp.where(live, near, 2 * (rb + 2))


def first_slots(shifts, ks):
    col = lax.axis_index("col")
    ny = lax.axis_size("col") // 2
    y, core = col // 2, lax.rem(col, 2)
    slots = []
    for s, flip in shifts:
        c = core if flip == 0 else 1 - core
        slots.append((lax.rem(y - s + ny, ny) * 2 + c) * ks)
    return slots


def lay(first, place_ref, srcs, slots, band, start):
    low = low_lanes(BS)
    zero = jnp.zeros((BS, LANES), BF)

    def group(g, carry):
        for t in range(band.shape[1]):
            band[g, t] = start(g, t)
        for src, slot in zip(srcs, slots):
            for k in range(src.shape[1]):
                for d0 in range(0, 4, 2):
                    cuts = []
                    for d in range(d0, d0 + 2):
                        x = src[4 * g + d, k]
                        r = jnp.concatenate([x[:, BS:], x[:, :BS]], axis=1)
                        cuts.append(
                            (
                                (jnp.where(low, x, zero), jnp.where(low, zero, r)),
                                (jnp.where(low, r, zero), jnp.where(low, zero, x)),
                            )
                        )
                    for e in range(2):
                        at = [place_ref[first + 4 * g + d0 + d, slot + 2 * k + e] for d in range(2)]
                        spots = [(g, a >> 1, slice((d0 + d) * BS, (d0 + d + 1) * BS)) for d, a in enumerate(at)]
                        old = [band[spot] for spot in spots]
                        for spot, a, x, cut in zip(spots, at, old, cuts):
                            band[spot] = x + jnp.where((a & 1) == 0, cut[e][0], cut[e][1])
        return carry

    lax.fori_loop(0, band.shape[0], group, 0)


def band_kernel(first, shifts, place_ref, *refs):
    srcs, band = refs[:-1], refs[-1]
    slots = first_slots(shifts, srcs[0].shape[1] * 2)
    lay(first, place_ref, srcs, slots, band, lambda g, t: jnp.zeros((4 * BS, LANES), BF))


def near_band(place, srcs, shifts, first):
    rows = srcs[0].shape[0]
    return pl.pallas_call(
        functools.partial(band_kernel, first, shifts),
        out_shape=jax.ShapeDtypeStruct((rows // 4, place.shape[0] + 3, 4 * BS, LANES), BF),
        in_specs=[SM] + [VM] * len(srcs),
        out_specs=VM,
        compiler_params=params(12),
        cost_estimate=cost(0.16 * rows),
        name="near_band",
    )(place, *srcs)


def product_kernel(first, rb, shifts, place_ref, own_ref, near_ref, start_ref, *refs):
    srcs = refs[: len(shifts)]
    o_ref, band, acc = refs[len(shifts) :]
    rows = o_ref.shape[0]
    tiles = own_ref.shape[1]
    wide = rb + 2
    slots = first_slots(shifts, srcs[0].shape[1] * 2)
    lay(first, place_ref, srcs, slots, band, lambda g, t: start_ref[g, t])
    quads = rb // 4
    for g in range(rows // 4):
        start = first // 4 + g
        acc[...] = jnp.zeros_like(acc)
        for side in range(3):
            k0, k1 = max(start, side * quads), min(start + wide // 2, (side + 1) * quads)
            if k0 >= k1:
                continue
            p0, p1 = touched(side, tiles)
            ref, base = (own_ref, quads) if side == 1 else (near_ref, 0 if side == 0 else quads)
            total = None
            for k in range(k0, k1):
                lhs = jnp.concatenate([band[g, 2 * (k - start)], band[g, 2 * (k - start) + 1]], axis=1)
                rhs = jnp.concatenate([ref[k - base, p] for p in range(p0, p1)], axis=1)
                part = dot(lhs, rhs)
                total = part if total is None else total + part
            acc[:, p0 * LANES : p1 * LANES] += total
        for d in range(4):
            o_ref[4 * g + d] = acc[d * BS : (d + 1) * BS].astype(BF)


def product(place, own, near, start, srcs, shifts, first, us):
    rows = srcs[0].shape[0]
    rb = place.shape[0]
    tiles = own.shape[1]
    return pl.pallas_call(
        functools.partial(product_kernel, first, rb, shifts),
        out_shape=jax.ShapeDtypeStruct((rows, BS, tiles * LANES), BF),
        in_specs=[SM] + [VM] * (3 + len(srcs)),
        out_specs=VM,
        scratch_shapes=[
            pltpu.VMEM(start.shape, BF),
            pltpu.VMEM((4 * BS, tiles * LANES), F32),
        ],
        compiler_params=params(16),
        cost_estimate=cost(us),
        name="product",
    )(place, own, near, start, *srcs)


def coarse_kernel(sets, a0, a1, left_ref, *refs):
    outs = refs[-1 - len(sets) : -1]
    aps = refs[: -1 - len(sets)]
    scr = refs[-1]
    ac = a1 - a0
    tiles = aps[0].shape[2] // LANES
    for out, (i0, i1) in zip(outs, sets):
        rows = i1 - i0
        low = low_lanes(rows)
        for p0 in range(0, tiles, 2):
            p1 = min(p0 + 2, tiles)
            acc = jnp.zeros((rows * ac, (p1 - p0) * LANES), F32)
            ip = 0
            for ap in aps:
                for g in range(0, ap.shape[0] // 2, 2):
                    lhs = [left_ref[ip + d, i0:i1, a0:a1].reshape(rows * ac, LANES) for d in range(2)]
                    rhs = ap[2 * g : 2 * g + 4, :, p0 * LANES : p1 * LANES].reshape(4 * BS, (p1 - p0) * LANES)
                    acc = acc + dot(jnp.concatenate(lhs, axis=1), rhs)
                    ip += 2
            for p in range(p0, p1):
                scr[p, 0 : rows * ac] = acc[:, (p - p0) * LANES : (p - p0 + 1) * LANES]
        for p in range(tiles):
            for a in range(0, ac, 2):
                x0 = scr[p, pl.ds(a, rows, stride=ac), :]
                x1 = scr[p, pl.ds(a + 1, rows, stride=ac), :]
                at = slice(a * BS, (a + 2) * BS)
                out[p, :, at] = jnp.where(low, x0, pltpu.roll(x1, BS, 1)).astype(out.dtype)
                out[tiles + p, :, at] = jnp.where(low, pltpu.roll(x0, BS, 1), x1).astype(out.dtype)


def coarse_rows(left, aps, sets, a0, a1, dtype, us):
    tiles = aps[0].shape[2] // LANES
    return pl.pallas_call(
        functools.partial(coarse_kernel, sets, a0, a1),
        out_shape=[jax.ShapeDtypeStruct((2 * tiles, i1 - i0, (a1 - a0) * BS), dtype) for i0, i1 in sets],
        in_specs=[VM] * (1 + len(aps)),
        out_specs=[VM] * len(sets),
        scratch_shapes=[pltpu.VMEM((tiles, max(i1 - i0 for i0, i1 in sets) * (a1 - a0), LANES), F32)],
        compiler_params=params(12),
        cost_estimate=cost(us),
        name="coarse",
    )(left, *aps)


def assemble_kernel(order_ref, *refs):
    out = refs[-1]
    srcs = refs[:-1] if len(refs) % 2 else refs[1:-1]
    x = jnp.concatenate([s[...].reshape(-1, s.shape[2]) for s in srcs], axis=0)
    res = dot(order_ref[...], x)
    wide = out.shape[1]
    for i in range(CB):
        out[i] = res[i * wide : (i + 1) * wide].astype(BF)


def assemble(order, srcs, a0, total, before):
    n, _, lanes = srcs[0].shape
    step = 512
    per = lanes // step
    wide = n * len(srcs)
    specs = [pl.BlockSpec(order.shape, lambda i: (0, 0))]
    args = [order]
    alias = {}
    if before is not None:
        specs.append(pl.BlockSpec(memory_space=pl.ANY))
        args.append(before)
        alias = {1: 0}
    specs += [pl.BlockSpec((n, CB, step), lambda i: (0, 0, i))] * len(srcs)
    return pl.pallas_call(
        assemble_kernel,
        grid=(per,),
        out_shape=jax.ShapeDtypeStruct((CB, wide, total), BF),
        in_specs=specs,
        out_specs=pl.BlockSpec((CB, wide, step), lambda i: (0, 0, a0 * BS // step + i)),
        input_output_aliases=alias,
        compiler_params=params(12),
        cost_estimate=cost(2.9),
        name="assemble",
    )(*args, *srcs)


def assembly_order(shifts, ncol, share):
    col = lax.axis_index("col")
    y, core = col // 2, col % 2
    groups = GROUPS + 2
    size = ncol * share * groups * CB
    out_row = lax.broadcasted_iota(jnp.int32, (size, size), 0)
    src_row = lax.broadcasted_iota(jnp.int32, (size, size), 1)
    per = share * groups * CB
    which, rest = src_row // per, src_row % per
    e, g, i = rest // (groups * CB), rest // CB % groups, rest % CB
    src_col = jnp.zeros_like(which)
    for z, (s, flip) in enumerate(shifts):
        c = (y - s) % (ncol // 2) * 2 + (core + flip) % 2
        src_col = jnp.where(which == z, c, src_col)
    return (out_row == i * (groups * CB) + g * CB + share * src_col + e).astype(BF)


def body(a_blocks, a_cols, counts, p_blocks, p_cols):
    rb, ks, _ = a_blocks.shape
    nrow, ncol = lax.axis_size("row"), lax.axis_size("col")
    ny = ncol // 2
    nfb = p_cols.shape[0]
    share = CB // ncol
    tiles = (GROUPS * share + 1) // 2
    parts = ((0, rb * 2 // 3), (rb * 2 // 3, rb // 3))
    chunks = ((0, 16), (16, 40), (40, 64))

    def outward(x):
        pairs = [(r * ncol + c, (r + 1 - 2 * (c % 2)) * ncol + c) for r in range(nrow) for c in range(ncol)]
        return lax.ppermute(x, ("row", "col"), [(a, b) for a, b in pairs if 0 <= b < nrow * ncol])

    def over_y(x, s):
        return lax.ppermute(x, "col", [(y * 2 + c, (y + s) % ny * 2 + c) for y in range(ny) for c in range(2)])

    def over_core(x):
        return lax.ppermute(x, "col", [(c, c ^ 1) for c in range(ncol)])

    def upward(x):
        return lax.ppermute(x, "row", [(i, i + 1) for i in range(nrow - 1)])

    def downward(x):
        return lax.ppermute(x, "row", [(i + 1, i) for i in range(nrow - 1)])

    shifts = tuple((s, f) for s in range(ny) for f in range(2))
    pct = p_cols.T

    own_a, side_a, far_a = [], [], []
    for h, (first, rows) in enumerate(parts):
        x = relayout(a_blocks, first, rows)
        own_a.append(x)
        far_a.append([over_y(x, s) for s in range(1, ny)])
        side_a.append(over_core(x))
        if h == 0:
            a_blocks, p_blocks, side_a[0] = lax.optimization_barrier((a_blocks, p_blocks, side_a[0]))
    p_own = relayout_rows(p_blocks)
    beside = outward(p_own)
    p_blocks, p_own, side_a[1] = lax.optimization_barrier((p_blocks, p_own, side_a[1]))
    table = column_table(pct, rb, share)
    left = left_factor(pct, relayout(p_blocks, 0, rb))
    own = right_factor(table, [p_own], tiles, 2.0)
    order = assembly_order(shifts, ncol, share)
    place = slot_places(a_cols, counts)
    bands = [near_band(place, [own_a[h], side_a[h]], shifts[:2], parts[h][0]) for h in range(2)]
    beside, far_a[0], left, own, order, bands = lax.optimization_barrier((beside, far_a[0], left, own, order, bands))
    near = right_factor(table, [beside, over_core(beside)], tiles, 3.0)
    aps = []
    for h in range(2):
        srcs = [z for g in far_a[h] for z in (g, over_core(g))]
        aps.append(product(place, own, near, bands[h], srcs, shifts[2:], parts[h][0], 0.3 * parts[h][1]))
        if h == 0:
            far_a[1], aps[0] = lax.optimization_barrier((far_a[1], aps[0]))
            early = downward(coarse_rows(left, aps, ((0, CB // 2),), 0, BS, BF, 1.0)[0])

    def columns(x, g):
        y = x[: GROUPS * share].reshape((share, GROUPS) + x.shape[1:])
        return jnp.pad(y.astype(F32), ((0, 0), (g, 2 - g), (0, 0), (0, 0)))

    late = downward(coarse_rows(left, aps, ((CB // 2, CB),), 0, BS, BF, 1.0)[0])
    raw = [coarse_rows(left, aps, ((2 * CB, 3 * CB),), a0, a1, BF, 1.0)[0] for a0, a1 in chunks]
    early, raw[0] = lax.optimization_barrier((early, raw[0]))
    highs = [upward(raw[0])]
    highs[0], raw[1] = lax.optimization_barrier((highs[0], raw[1]))
    highs.append(upward(raw[1]))
    late, raw[2] = lax.optimization_barrier((late, raw[2]))
    highs.append(upward(raw[2]))
    mids = [coarse_rows(left, aps, ((CB, 2 * CB),), a0, a1, F32, 1.0)[0] for a0, a1 in chunks]
    lower = jnp.concatenate([early, late], axis=1)
    totals, sides, fars, beyond = [], [], [], []
    for z, (a0, a1) in enumerate(chunks):
        total = columns(highs[z], 0) + columns(mids[z], 1) + columns(lower[:, :, a0 * BS : a1 * BS], 2)
        total = total.astype(BF).reshape((share * (GROUPS + 2),) + total.shape[2:])
        if z > 0:
            fars[-1], total = lax.optimization_barrier((fars[-1], total))
            beyond.append([over_core(x) for x in fars[-1]])
        totals.append(total)
        sides.append(over_core(total))
        fars.append([over_y(total, s) for s in range(1, ny)])
    out = None
    for z, (a0, a1) in enumerate(chunks):
        if z == len(chunks) - 1:
            fars[z], out = lax.optimization_barrier((fars[z], out))
            beyond.append([over_core(x) for x in fars[z]])
        srcs = [totals[z], sides[z]] + [q for pair in zip(fars[z], beyond[z]) for q in pair]
        out = assemble(order, srcs, a0, BS * BS, out)
    return out


def solution(mesh):
    return jax.shard_map(
        body,
        mesh=mesh,
        in_specs=(P("row", "col", None), P("row", None), P("row"), P("row", None, None), P()),
        out_specs=P("row", None, None),
        check_vma=False,
    )
```

```python
import functools

import jax
import jax.numpy as jnp
from jax import lax
from jax.experimental import pallas as pl
from jax.experimental.pallas import tpu as pltpu
from jax.sharding import PartitionSpec as P

BS = 64
CB = 8
GROUPS = 5
LANES = 128
BF = jnp.bfloat16
F32 = jnp.float32
MIB = 1 << 20

VM = pl.BlockSpec(memory_space=pltpu.VMEM)
SM = pl.BlockSpec(memory_space=pltpu.SMEM)


def params(mib):
    return pltpu.CompilerParams(vmem_limit_bytes=mib * MIB)


def cost(us):
    return pl.CostEstimate(flops=int(us * 1e8), bytes_accessed=int(us * 3.7e6), transcendentals=0)


def low_lanes(rows):
    return lax.broadcasted_iota(jnp.int32, (rows, LANES), 1) < BS


def dot(a, b):
    return lax.dot_general(a, b, (((1,), (0,)), ((), ())), preferred_element_type=F32)


def relayout_kernel(x_ref, o_ref, scr):
    rows, nb, _ = x_ref.shape
    low = low_lanes(32)
    for r in range(rows):
        for q in range(32):
            scr[r, pl.ds(q * 8, nb), :] = x_ref[r, :, q * LANES : (q + 1) * LANES].astype(F32)
        for k in range(0, nb, 2):
            x0 = scr[r, pl.ds(k, 32, stride=8), :]
            x1 = scr[r, pl.ds(k + 1, 32, stride=8), :]
            o_ref[r, k // 2, 0:32] = jnp.where(low, x0, pltpu.roll(x1, BS, 1)).astype(BF)
            o_ref[r, k // 2, 32:64] = jnp.where(low, pltpu.roll(x0, BS, 1), x1).astype(BF)


def relayout(x, first, rows):
    nb = x.shape[1]
    step = 4
    return pl.pallas_call(
        relayout_kernel,
        grid=(rows // step,),
        out_shape=jax.ShapeDtypeStruct((rows, nb // 2, BS, LANES), BF),
        in_specs=[pl.BlockSpec((step, nb, BS * BS), lambda i: (i + first // step, 0, 0))],
        out_specs=pl.BlockSpec((step, nb // 2, BS, LANES), lambda i: (i, 0, 0, 0)),
        scratch_shapes=[pltpu.VMEM((step, 256, LANES), F32)],
        compiler_params=params(4),
        cost_estimate=cost(0.6),
        name="relayout",
    )(x)


def relayout_rows_kernel(x_ref, o_ref, scr, mix):
    rows, nb, _ = x_ref.shape
    low = low_lanes(32)
    for r in range(rows):
        for q in range(32):
            scr[r, pl.ds(q * 8, nb), :] = x_ref[r, :, q * LANES : (q + 1) * LANES].astype(F32)
        for k in range(0, nb, 2):
            x0 = scr[r, pl.ds(k, 32, stride=8), :]
            x1 = scr[r, pl.ds(k + 1, 32, stride=8), :]
            mix[r, k // 2, pl.ds(0, 32, stride=2), :] = jnp.where(low, x0, pltpu.roll(x1, BS, 1))
            mix[r, k // 2, pl.ds(1, 32, stride=2), :] = jnp.where(low, pltpu.roll(x0, BS, 1), x1)
            o_ref[r, k // 2] = mix[r, k // 2].astype(BF)


def relayout_rows(x):
    rows, nb, _ = x.shape
    step = 4
    return pl.pallas_call(
        relayout_rows_kernel,
        grid=(rows // step,),
        out_shape=jax.ShapeDtypeStruct((rows, nb // 2, BS, LANES), BF),
        in_specs=[pl.BlockSpec((step, nb, BS * BS), lambda i: (i, 0, 0))],
        out_specs=pl.BlockSpec((step, nb // 2, BS, LANES), lambda i: (i, 0, 0, 0)),
        scratch_shapes=[pltpu.VMEM((step, 256, LANES), F32), pltpu.VMEM((step, nb // 2, BS, LANES), F32)],
        compiler_params=params(4),
        cost_estimate=cost(1.0),
        name="relayout_rows",
    )(x)


def left_kernel(rb, pct_ref, pl_ref, o_ref):
    slab = lax.axis_index("row")
    low = low_lanes(4 * BS)
    o_ref[...] = jnp.zeros_like(o_ref)

    def pair(ip, carry):
        for half in range(2):
            i = ip * 2 + half
            x = jnp.concatenate([pl_ref[i, 0], pl_ref[i, 1]], axis=1).astype(F32)
            xt = jnp.concatenate([x, x], axis=0).T
            keep = jnp.where(low if half == 0 else jnp.logical_not(low), xt, 0.0)
            for s in range(4):
                w = pct_ref[s, slab * rb + i] - (slab - 1) * CB
                o_ref[ip, w] = (o_ref[ip, w].astype(F32) + keep[s * BS : (s + 1) * BS]).astype(BF)
        return carry

    lax.fori_loop(0, rb // 2, pair, 0)


def left_factor(pct, p_own):
    rb = p_own.shape[0]
    return pl.pallas_call(
        functools.partial(left_kernel, rb),
        out_shape=jax.ShapeDtypeStruct((rb // 2, 3 * CB, BS, LANES), BF),
        in_specs=[SM, VM],
        out_specs=VM,
        compiler_params=params(12),
        cost_estimate=cost(2.9),
        name="left_factor",
    )(pct, p_own)


def column_table(pct, rb, share):
    slab = lax.axis_index("row")
    padded = jnp.pad(pct, ((0, 0), (rb, rb)), constant_values=-1000000)
    near = lax.dynamic_slice_in_dim(padded, slab * rb, 3 * rb, 1)
    w = near - (slab - 2) * CB
    e = (w & (CB - 1)) - share * lax.axis_index("col")
    return jnp.where((w >= 0) & (e >= 0) & (e < share), e * GROUPS + (w >> 3), -1)


def touched(side, tiles):
    return (side, side + 3) if tiles == GROUPS else (0, tiles)


def right_kernel(rb, tiles, table_ref, *refs):
    o_ref = refs[-1]
    core = lax.rem(lax.axis_index("col"), 2)
    low = lax.broadcasted_iota(jnp.int32, (1, LANES), 1) < BS
    wants = [jnp.where(low, p, tiles + p) for p in range(tiles)]

    def fill(src, side, out_first):
        def four(jq, carry):
            for d in range(4):
                jj = 4 * jq + d
                dups = []
                for t in range(4):
                    x = src[jj, t // 2, :, t % 2 * BS : (t % 2 + 1) * BS]
                    dups.append(jnp.concatenate([x, x], axis=1))
                at = [table_ref[t, side * rb + jj] for t in range(4)]
                for p in range(*touched(side, tiles)):
                    total = None
                    for t in range(4):
                        keep = dups[t] * jnp.where(wants[p] == at[t], 1.0, 0.0).astype(BF)
                        total = keep if total is None else total + keep
                    o_ref[out_first + jq, p, d * BS : (d + 1) * BS] = total
            return carry

        lax.fori_loop(0, rb // 4, four, 0)

    if len(refs) == 2:
        fill(refs[0], 1, 0)
    else:
        first = refs[0]
        second = refs[1]

        @pl.when(core == 0)
        def _():
            fill(first, 0, 0)
            fill(second, 2, rb // 4)

        @pl.when(core == 1)
        def _():
            fill(second, 0, 0)
            fill(first, 2, rb // 4)


def right_factor(table, srcs, tiles, us):
    rb = table.shape[1] // 3
    return pl.pallas_call(
        functools.partial(right_kernel, rb, tiles),
        out_shape=jax.ShapeDtypeStruct((len(srcs) * rb // 4, tiles, 4 * BS, LANES), BF),
        in_specs=[SM] + [VM] * len(srcs),
        out_specs=VM,
        compiler_params=params(8),
        cost_estimate=cost(us),
        name="right_factor",
    )(table, *srcs)


def slot_places(a_cols, counts):
    rb, ka = a_cols.shape
    row = jnp.arange(rb, dtype=jnp.int32)[:, None]
    near = a_cols - (lax.axis_index("row") - 1) * rb - row // 4 * 4
    live = jnp.arange(ka, dtype=jnp.int32)[None, :] < counts[:, None]
    return jnp.where(live, near, 2 * (rb + 2))


def first_slots(shifts, ks):
    col = lax.axis_index("col")
    ny = lax.axis_size("col") // 2
    y, core = col // 2, lax.rem(col, 2)
    slots = []
    for s, flip in shifts:
        c = core if flip == 0 else 1 - core
        slots.append((lax.rem(y - s + ny, ny) * 2 + c) * ks)
    return slots


def lay(first, place_ref, srcs, slots, band, start):
    low = low_lanes(BS)
    zero = jnp.zeros((BS, LANES), BF)

    def group(g, carry):
        for t in range(band.shape[1]):
            band[g, t] = start(g, t)
        for src, slot in zip(srcs, slots):
            for k in range(src.shape[1]):
                for d0 in range(0, 4, 2):
                    cuts = []
                    for d in range(d0, d0 + 2):
                        x = src[4 * g + d, k]
                        r = jnp.concatenate([x[:, BS:], x[:, :BS]], axis=1)
                        cuts.append(
                            (
                                (jnp.where(low, x, zero), jnp.where(low, zero, r)),
                                (jnp.where(low, r, zero), jnp.where(low, zero, x)),
                            )
                        )
                    for e in range(2):
                        at = [place_ref[first + 4 * g + d0 + d, slot + 2 * k + e] for d in range(2)]
                        spots = [(g, a >> 1, slice((d0 + d) * BS, (d0 + d + 1) * BS)) for d, a in enumerate(at)]
                        old = [band[spot] for spot in spots]
                        for spot, a, x, cut in zip(spots, at, old, cuts):
                            band[spot] = x + jnp.where((a & 1) == 0, cut[e][0], cut[e][1])
        return carry

    lax.fori_loop(0, band.shape[0], group, 0)


def band_kernel(first, shifts, place_ref, *refs):
    srcs, band = refs[:-1], refs[-1]
    slots = first_slots(shifts, srcs[0].shape[1] * 2)
    lay(first, place_ref, srcs, slots, band, lambda g, t: jnp.zeros((4 * BS, LANES), BF))


def near_band(place, srcs, shifts, first):
    rows = srcs[0].shape[0]
    return pl.pallas_call(
        functools.partial(band_kernel, first, shifts),
        out_shape=jax.ShapeDtypeStruct((rows // 4, place.shape[0] + 3, 4 * BS, LANES), BF),
        in_specs=[SM] + [VM] * len(srcs),
        out_specs=VM,
        compiler_params=params(12),
        cost_estimate=cost(0.16 * rows),
        name="near_band",
    )(place, *srcs)


def product_kernel(first, rb, shifts, place_ref, own_ref, near_ref, start_ref, *refs):
    srcs = refs[: len(shifts)]
    o_ref, band, acc = refs[len(shifts) :]
    rows = o_ref.shape[0]
    tiles = own_ref.shape[1]
    wide = rb + 2
    slots = first_slots(shifts, srcs[0].shape[1] * 2)
    lay(first, place_ref, srcs, slots, band, lambda g, t: start_ref[g, t])
    quads = rb // 4
    for g in range(rows // 4):
        start = first // 4 + g
        acc[...] = jnp.zeros_like(acc)
        for side in range(3):
            k0, k1 = max(start, side * quads), min(start + wide // 2, (side + 1) * quads)
            if k0 >= k1:
                continue
            p0, p1 = touched(side, tiles)
            ref, base = (own_ref, quads) if side == 1 else (near_ref, 0 if side == 0 else quads)
            total = None
            for k in range(k0, k1):
                lhs = jnp.concatenate([band[g, 2 * (k - start)], band[g, 2 * (k - start) + 1]], axis=1)
                rhs = jnp.concatenate([ref[k - base, p] for p in range(p0, p1)], axis=1)
                part = dot(lhs, rhs)
                total = part if total is None else total + part
            acc[:, p0 * LANES : p1 * LANES] += total
        for d in range(4):
            o_ref[4 * g + d] = acc[d * BS : (d + 1) * BS].astype(BF)


def product(place, own, near, start, srcs, shifts, first, us):
    rows = srcs[0].shape[0]
    rb = place.shape[0]
    tiles = own.shape[1]
    return pl.pallas_call(
        functools.partial(product_kernel, first, rb, shifts),
        out_shape=jax.ShapeDtypeStruct((rows, BS, tiles * LANES), BF),
        in_specs=[SM] + [VM] * (3 + len(srcs)),
        out_specs=VM,
        scratch_shapes=[
            pltpu.VMEM(start.shape, BF),
            pltpu.VMEM((4 * BS, tiles * LANES), F32),
        ],
        compiler_params=params(16),
        cost_estimate=cost(us),
        name="product",
    )(place, own, near, start, *srcs)


def coarse_kernel(sets, a0, a1, left_ref, *refs):
    outs = refs[-1 - len(sets) : -1]
    aps = refs[: -1 - len(sets)]
    scr = refs[-1]
    ac = a1 - a0
    tiles = aps[0].shape[2] // LANES
    for out, (i0, i1) in zip(outs, sets):
        rows = i1 - i0
        low = low_lanes(rows)
        for p0 in range(0, tiles, 2):
            p1 = min(p0 + 2, tiles)
            acc = jnp.zeros((rows * ac, (p1 - p0) * LANES), F32)
            ip = 0
            for ap in aps:
                for g in range(0, ap.shape[0] // 2, 2):
                    lhs = [left_ref[ip + d, i0:i1, a0:a1].reshape(rows * ac, LANES) for d in range(2)]
                    rhs = ap[2 * g : 2 * g + 4, :, p0 * LANES : p1 * LANES].reshape(4 * BS, (p1 - p0) * LANES)
                    acc = acc + dot(jnp.concatenate(lhs, axis=1), rhs)
                    ip += 2
            for p in range(p0, p1):
                scr[p, 0 : rows * ac] = acc[:, (p - p0) * LANES : (p - p0 + 1) * LANES]
        for p in range(tiles):
            for a in range(0, ac, 2):
                x0 = scr[p, pl.ds(a, rows, stride=ac), :]
                x1 = scr[p, pl.ds(a + 1, rows, stride=ac), :]
                at = slice(a * BS, (a + 2) * BS)
                out[p, :, at] = jnp.where(low, x0, pltpu.roll(x1, BS, 1)).astype(out.dtype)
                out[tiles + p, :, at] = jnp.where(low, pltpu.roll(x0, BS, 1), x1).astype(out.dtype)


def coarse_rows(left, aps, sets, a0, a1, dtype, us):
    tiles = aps[0].shape[2] // LANES
    return pl.pallas_call(
        functools.partial(coarse_kernel, sets, a0, a1),
        out_shape=[jax.ShapeDtypeStruct((2 * tiles, i1 - i0, (a1 - a0) * BS), dtype) for i0, i1 in sets],
        in_specs=[VM] * (1 + len(aps)),
        out_specs=[VM] * len(sets),
        scratch_shapes=[pltpu.VMEM((tiles, max(i1 - i0 for i0, i1 in sets) * (a1 - a0), LANES), F32)],
        compiler_params=params(12),
        cost_estimate=cost(us),
        name="coarse",
    )(left, *aps)


def assemble_kernel(order_ref, *refs):
    out = refs[-1]
    srcs = refs[:-1] if len(refs) % 2 else refs[1:-1]
    x = jnp.concatenate([s[...].reshape(-1, s.shape[2]) for s in srcs], axis=0)
    res = dot(order_ref[...], x)
    wide = out.shape[1]
    for i in range(CB):
        out[i] = res[i * wide : (i + 1) * wide].astype(BF)


def assemble(order, srcs, a0, total, before):
    n, _, lanes = srcs[0].shape
    step = 512
    per = lanes // step
    wide = n * len(srcs)
    specs = [pl.BlockSpec(order.shape, lambda i: (0, 0))]
    args = [order]
    alias = {}
    if before is not None:
        specs.append(pl.BlockSpec(memory_space=pl.ANY))
        args.append(before)
        alias = {1: 0}
    specs += [pl.BlockSpec((n, CB, step), lambda i: (0, 0, i))] * len(srcs)
    return pl.pallas_call(
        assemble_kernel,
        grid=(per,),
        out_shape=jax.ShapeDtypeStruct((CB, wide, total), BF),
        in_specs=specs,
        out_specs=pl.BlockSpec((CB, wide, step), lambda i: (0, 0, a0 * BS // step + i)),
        input_output_aliases=alias,
        compiler_params=params(12),
        cost_estimate=cost(2.9),
        name="assemble",
    )(*args, *srcs)


def assembly_order(shifts, ncol, share):
    col = lax.axis_index("col")
    y, core = col // 2, col % 2
    groups = GROUPS + 2
    size = ncol * share * groups * CB
    out_row = lax.broadcasted_iota(jnp.int32, (size, size), 0)
    src_row = lax.broadcasted_iota(jnp.int32, (size, size), 1)
    per = share * groups * CB
    which, rest = src_row // per, src_row % per
    e, g, i = rest // (groups * CB), rest // CB % groups, rest % CB
    src_col = jnp.zeros_like(which)
    for z, (s, flip) in enumerate(shifts):
        c = (y - s) % (ncol // 2) * 2 + (core + flip) % 2
        src_col = jnp.where(which == z, c, src_col)
    return (out_row == i * (groups * CB) + g * CB + share * src_col + e).astype(BF)


def body(a_blocks, a_cols, counts, p_blocks, p_cols):
    rb, ks, _ = a_blocks.shape
    nrow, ncol = lax.axis_size("row"), lax.axis_size("col")
    ny = ncol // 2
    nfb = p_cols.shape[0]
    share = CB // ncol
    tiles = (GROUPS * share + 1) // 2
    parts = ((0, rb * 2 // 3), (rb * 2 // 3, rb // 3))
    chunks = ((0, 16), (16, 40), (40, 64))

    def outward(x):
        pairs = [(r * ncol + c, (r + 1 - 2 * (c % 2)) * ncol + c) for r in range(nrow) for c in range(ncol)]
        return lax.ppermute(x, ("row", "col"), [(a, b) for a, b in pairs if 0 <= b < nrow * ncol])

    def over_y(x, s):
        return lax.ppermute(x, "col", [(y * 2 + c, (y + s) % ny * 2 + c) for y in range(ny) for c in range(2)])

    def over_core(x):
        return lax.ppermute(x, "col", [(c, c ^ 1) for c in range(ncol)])

    def upward(x):
        return lax.ppermute(x, "row", [(i, i + 1) for i in range(nrow - 1)])

    def downward(x):
        return lax.ppermute(x, "row", [(i + 1, i) for i in range(nrow - 1)])

    shifts = tuple((s, f) for s in range(ny) for f in range(2))
    pct = p_cols.T

    own_a, side_a, far_a = [], [], []
    for h, (first, rows) in enumerate(parts):
        x = relayout(a_blocks, first, rows)
        own_a.append(x)
        far_a.append([over_y(x, s) for s in range(1, ny)])
        side_a.append(over_core(x))
        if h == 0:
            p_own = relayout_rows(p_blocks)
            a_blocks, p_own, side_a[0] = lax.optimization_barrier((a_blocks, p_own, side_a[0]))
    beside = outward(p_own)
    p_blocks, p_own, side_a[1] = lax.optimization_barrier((p_blocks, p_own, side_a[1]))
    table = column_table(pct, rb, share)
    left = left_factor(pct, relayout(p_blocks, 0, rb))
    own = right_factor(table, [p_own], tiles, 2.0)
    order = assembly_order(shifts, ncol, share)
    place = slot_places(a_cols, counts)
    bands = [near_band(place, [own_a[h], side_a[h]], shifts[:2], parts[h][0]) for h in range(2)]
    beside, far_a[0], left, own, order, bands = lax.optimization_barrier((beside, far_a[0], left, own, order, bands))
    near = right_factor(table, [beside, over_core(beside)], tiles, 3.0)
    aps = []
    for h in range(2):
        srcs = [z for g in far_a[h] for z in (g, over_core(g))]
        aps.append(product(place, own, near, bands[h], srcs, shifts[2:], parts[h][0], 0.3 * parts[h][1]))
        if h == 0:
            far_a[1], aps[0] = lax.optimization_barrier((far_a[1], aps[0]))
            early = downward(coarse_rows(left, aps, ((0, CB // 2),), 0, BS, BF, 1.0)[0])

    def columns(x, g):
        y = x[: GROUPS * share].reshape((share, GROUPS) + x.shape[1:])
        return jnp.pad(y.astype(F32), ((0, 0), (g, 2 - g), (0, 0), (0, 0)))

    late = downward(coarse_rows(left, aps, ((CB // 2, CB),), 0, BS, BF, 1.0)[0])
    raw = [coarse_rows(left, aps, ((2 * CB, 3 * CB),), a0, a1, BF, 1.0)[0] for a0, a1 in chunks]
    early, raw[0] = lax.optimization_barrier((early, raw[0]))
    highs = [upward(raw[0])]
    highs[0], raw[1] = lax.optimization_barrier((highs[0], raw[1]))
    highs.append(upward(raw[1]))
    late, raw[2] = lax.optimization_barrier((late, raw[2]))
    highs.append(upward(raw[2]))
    mids = [coarse_rows(left, aps, ((CB, 2 * CB),), a0, a1, F32, 1.0)[0] for a0, a1 in chunks]
    lower = jnp.concatenate([early, late], axis=1)
    totals, sides, fars = [], [], []
    for z, (a0, a1) in enumerate(chunks):
        total = columns(highs[z], 0) + columns(mids[z], 1) + columns(lower[:, :, a0 * BS : a1 * BS], 2)
        total = total.astype(BF).reshape((share * (GROUPS + 2),) + total.shape[2:])
        totals.append(total)
        sides.append(over_core(total))
        fars.append([over_y(total, s) for s in range(1, ny)])
    for z in range(len(chunks) - 1):
        fars[z], _ = lax.optimization_barrier((fars[z], totals[z + 1]))
    out = None
    for z, (a0, a1) in enumerate(chunks):
        if z == 1:
            fars[1:], out = lax.optimization_barrier((fars[1:], out))
        srcs = [totals[z], sides[z]] + [q for x in fars[z] for q in (x, over_core(x))]
        out = assemble(order, srcs, a0, BS * BS, out)
    return out


def solution(mesh):
    return jax.shard_map(
        body,
        mesh=mesh,
        in_specs=(P("row", "col", None), P("row", None), P("row"), P("row", None, None), P()),
        out_specs=P("row", None, None),
        check_vma=False,
    )
```

```python
import functools

import jax
import jax.numpy as jnp
from jax import lax
from jax.experimental import pallas as pl
from jax.experimental.pallas import tpu as pltpu
from jax.sharding import PartitionSpec as P

BS = 64
CB = 8
GROUPS = 5
LANES = 128
BF = jnp.bfloat16
F32 = jnp.float32
MIB = 1 << 20

VM = pl.BlockSpec(memory_space=pltpu.VMEM)
SM = pl.BlockSpec(memory_space=pltpu.SMEM)


def params(mib):
    return pltpu.CompilerParams(vmem_limit_bytes=mib * MIB)


def cost(us):
    return pl.CostEstimate(flops=int(us * 1e8), bytes_accessed=int(us * 3.7e6), transcendentals=0)


def low_lanes(rows):
    return lax.broadcasted_iota(jnp.int32, (rows, LANES), 1) < BS


def dot(a, b):
    return lax.dot_general(a, b, (((1,), (0,)), ((), ())), preferred_element_type=F32)


def relayout_kernel(x_ref, o_ref, scr):
    rows, nb, _ = x_ref.shape
    low = low_lanes(32)
    for r in range(rows):
        for q in range(32):
            scr[r, pl.ds(q * 8, nb), :] = x_ref[r, :, q * LANES : (q + 1) * LANES].astype(F32)
        for k in range(0, nb, 2):
            x0 = scr[r, pl.ds(k, 32, stride=8), :]
            x1 = scr[r, pl.ds(k + 1, 32, stride=8), :]
            o_ref[r, k // 2, 0:32] = jnp.where(low, x0, pltpu.roll(x1, BS, 1)).astype(BF)
            o_ref[r, k // 2, 32:64] = jnp.where(low, pltpu.roll(x0, BS, 1), x1).astype(BF)


def relayout(x, first, rows):
    nb = x.shape[1]
    step = 4
    return pl.pallas_call(
        relayout_kernel,
        grid=(rows // step,),
        out_shape=jax.ShapeDtypeStruct((rows, nb // 2, BS, LANES), BF),
        in_specs=[pl.BlockSpec((step, nb, BS * BS), lambda i: (i + first // step, 0, 0))],
        out_specs=pl.BlockSpec((step, nb // 2, BS, LANES), lambda i: (i, 0, 0, 0)),
        scratch_shapes=[pltpu.VMEM((step, 256, LANES), F32)],
        compiler_params=params(4),
        cost_estimate=cost(0.6),
        name="relayout",
    )(x)


def relayout_rows_kernel(x_ref, o_ref, scr, mix):
    rows, nb, _ = x_ref.shape
    low = low_lanes(32)
    for r in range(rows):
        for q in range(32):
            scr[r, pl.ds(q * 8, nb), :] = x_ref[r, :, q * LANES : (q + 1) * LANES].astype(F32)
        for k in range(0, nb, 2):
            x0 = scr[r, pl.ds(k, 32, stride=8), :]
            x1 = scr[r, pl.ds(k + 1, 32, stride=8), :]
            mix[r, k // 2, pl.ds(0, 32, stride=2), :] = jnp.where(low, x0, pltpu.roll(x1, BS, 1))
            mix[r, k // 2, pl.ds(1, 32, stride=2), :] = jnp.where(low, pltpu.roll(x0, BS, 1), x1)
            o_ref[r, k // 2] = mix[r, k // 2].astype(BF)


def relayout_rows(x):
    rows, nb, _ = x.shape
    step = 4
    return pl.pallas_call(
        relayout_rows_kernel,
        grid=(rows // step,),
        out_shape=jax.ShapeDtypeStruct((rows, nb // 2, BS, LANES), BF),
        in_specs=[pl.BlockSpec((step, nb, BS * BS), lambda i: (i, 0, 0))],
        out_specs=pl.BlockSpec((step, nb // 2, BS, LANES), lambda i: (i, 0, 0, 0)),
        scratch_shapes=[pltpu.VMEM((step, 256, LANES), F32), pltpu.VMEM((step, nb // 2, BS, LANES), F32)],
        compiler_params=params(4),
        cost_estimate=cost(1.0),
        name="relayout_rows",
    )(x)


def left_kernel(rb, pct_ref, pl_ref, o_ref):
    slab = lax.axis_index("row")
    low = low_lanes(4 * BS)
    o_ref[...] = jnp.zeros_like(o_ref)

    def pair(ip, carry):
        for half in range(2):
            i = ip * 2 + half
            x = jnp.concatenate([pl_ref[i, 0], pl_ref[i, 1]], axis=1).astype(F32)
            xt = jnp.concatenate([x, x], axis=0).T
            keep = jnp.where(low if half == 0 else jnp.logical_not(low), xt, 0.0)
            for s in range(4):
                w = pct_ref[s, slab * rb + i] - (slab - 1) * CB
                o_ref[ip, w] = (o_ref[ip, w].astype(F32) + keep[s * BS : (s + 1) * BS]).astype(BF)
        return carry

    lax.fori_loop(0, rb // 2, pair, 0)


def left_factor(pct, p_own):
    rb = p_own.shape[0]
    return pl.pallas_call(
        functools.partial(left_kernel, rb),
        out_shape=jax.ShapeDtypeStruct((rb // 2, 3 * CB, BS, LANES), BF),
        in_specs=[SM, VM],
        out_specs=VM,
        compiler_params=params(12),
        cost_estimate=cost(2.9),
        name="left_factor",
    )(pct, p_own)


def column_table(pct, rb, share):
    slab = lax.axis_index("row")
    padded = jnp.pad(pct, ((0, 0), (rb, rb)), constant_values=-1000000)
    near = lax.dynamic_slice_in_dim(padded, slab * rb, 3 * rb, 1)
    w = near - (slab - 2) * CB
    e = (w & (CB - 1)) - share * lax.axis_index("col")
    return jnp.where((w >= 0) & (e >= 0) & (e < share), e * GROUPS + (w >> 3), -1)


def touched(side, tiles):
    return (side, side + 3) if tiles == GROUPS else (0, tiles)


def right_kernel(rb, tiles, table_ref, *refs):
    o_ref = refs[-1]
    core = lax.rem(lax.axis_index("col"), 2)
    low = lax.broadcasted_iota(jnp.int32, (1, LANES), 1) < BS
    wants = [jnp.where(low, p, tiles + p) for p in range(tiles)]

    def fill(src, side, out_first):
        def four(jq, carry):
            for d in range(4):
                jj = 4 * jq + d
                dups = []
                for t in range(4):
                    x = src[jj, t // 2, :, t % 2 * BS : (t % 2 + 1) * BS]
                    dups.append(jnp.concatenate([x, x], axis=1))
                at = [table_ref[t, side * rb + jj] for t in range(4)]
                for p in range(*touched(side, tiles)):
                    total = None
                    for t in range(4):
                        keep = dups[t] * jnp.where(wants[p] == at[t], 1.0, 0.0).astype(BF)
                        total = keep if total is None else total + keep
                    o_ref[out_first + jq, p, d * BS : (d + 1) * BS] = total
            return carry

        lax.fori_loop(0, rb // 4, four, 0)

    if len(refs) == 2:
        fill(refs[0], 1, 0)
    else:
        first = refs[0]
        second = refs[1]

        @pl.when(core == 0)
        def _():
            fill(first, 0, 0)
            fill(second, 2, rb // 4)

        @pl.when(core == 1)
        def _():
            fill(second, 0, 0)
            fill(first, 2, rb // 4)


def right_factor(table, srcs, tiles, us):
    rb = table.shape[1] // 3
    return pl.pallas_call(
        functools.partial(right_kernel, rb, tiles),
        out_shape=jax.ShapeDtypeStruct((len(srcs) * rb // 4, tiles, 4 * BS, LANES), BF),
        in_specs=[SM] + [VM] * len(srcs),
        out_specs=VM,
        compiler_params=params(8),
        cost_estimate=cost(us),
        name="right_factor",
    )(table, *srcs)


def slot_places(a_cols, counts):
    rb, ka = a_cols.shape
    row = jnp.arange(rb, dtype=jnp.int32)[:, None]
    near = a_cols - (lax.axis_index("row") - 1) * rb - row // 4 * 4
    live = jnp.arange(ka, dtype=jnp.int32)[None, :] < counts[:, None]
    return jnp.where(live, near, 2 * (rb + 2))


def first_slots(shifts, ks):
    col = lax.axis_index("col")
    ny = lax.axis_size("col") // 2
    y, core = col // 2, lax.rem(col, 2)
    slots = []
    for s, flip in shifts:
        c = core if flip == 0 else 1 - core
        slots.append((lax.rem(y - s + ny, ny) * 2 + c) * ks)
    return slots


def lay(first, place_ref, srcs, slots, band, start):
    low = low_lanes(BS)
    zero = jnp.zeros((BS, LANES), BF)

    def group(g, carry):
        for t in range(band.shape[1]):
            band[g, t] = start(g, t)
        for src, slot in zip(srcs, slots):
            for k in range(src.shape[1]):
                for d0 in range(0, 4, 2):
                    cuts = []
                    for d in range(d0, d0 + 2):
                        x = src[4 * g + d, k]
                        r = jnp.concatenate([x[:, BS:], x[:, :BS]], axis=1)
                        cuts.append(
                            (
                                (jnp.where(low, x, zero), jnp.where(low, zero, r)),
                                (jnp.where(low, r, zero), jnp.where(low, zero, x)),
                            )
                        )
                    for e in range(2):
                        at = [place_ref[first + 4 * g + d0 + d, slot + 2 * k + e] for d in range(2)]
                        spots = [(g, a >> 1, slice((d0 + d) * BS, (d0 + d + 1) * BS)) for d, a in enumerate(at)]
                        old = [band[spot] for spot in spots]
                        for spot, a, x, cut in zip(spots, at, old, cuts):
                            band[spot] = x + jnp.where((a & 1) == 0, cut[e][0], cut[e][1])
        return carry

    lax.fori_loop(0, band.shape[0], group, 0)


def band_kernel(first, shifts, place_ref, *refs):
    srcs, band = refs[:-1], refs[-1]
    slots = first_slots(shifts, srcs[0].shape[1] * 2)
    lay(first, place_ref, srcs, slots, band, lambda g, t: jnp.zeros((4 * BS, LANES), BF))


def near_band(place, srcs, shifts, first):
    rows = srcs[0].shape[0]
    return pl.pallas_call(
        functools.partial(band_kernel, first, shifts),
        out_shape=jax.ShapeDtypeStruct((rows // 4, place.shape[0] + 3, 4 * BS, LANES), BF),
        in_specs=[SM] + [VM] * len(srcs),
        out_specs=VM,
        compiler_params=params(12),
        cost_estimate=cost(0.16 * rows),
        name="near_band",
    )(place, *srcs)


def product_kernel(first, rb, shifts, place_ref, own_ref, near_ref, start_ref, *refs):
    srcs = refs[: len(shifts)]
    o_ref, band, acc = refs[len(shifts) :]
    rows = o_ref.shape[0]
    tiles = own_ref.shape[1]
    wide = rb + 2
    slots = first_slots(shifts, srcs[0].shape[1] * 2)
    lay(first, place_ref, srcs, slots, band, lambda g, t: start_ref[g, t])
    quads = rb // 4
    for g in range(rows // 4):
        start = first // 4 + g
        acc[...] = jnp.zeros_like(acc)
        for side in range(3):
            k0, k1 = max(start, side * quads), min(start + wide // 2, (side + 1) * quads)
            if k0 >= k1:
                continue
            p0, p1 = touched(side, tiles)
            ref, base = (own_ref, quads) if side == 1 else (near_ref, 0 if side == 0 else quads)
            total = None
            for k in range(k0, k1):
                lhs = jnp.concatenate([band[g, 2 * (k - start)], band[g, 2 * (k - start) + 1]], axis=1)
                rhs = jnp.concatenate([ref[k - base, p] for p in range(p0, p1)], axis=1)
                part = dot(lhs, rhs)
                total = part if total is None else total + part
            acc[:, p0 * LANES : p1 * LANES] += total
        for d in range(4):
            o_ref[4 * g + d] = acc[d * BS : (d + 1) * BS].astype(BF)


def product(place, own, near, start, srcs, shifts, first, us):
    rows = srcs[0].shape[0]
    rb = place.shape[0]
    tiles = own.shape[1]
    return pl.pallas_call(
        functools.partial(product_kernel, first, rb, shifts),
        out_shape=jax.ShapeDtypeStruct((rows, BS, tiles * LANES), BF),
        in_specs=[SM] + [VM] * (3 + len(srcs)),
        out_specs=VM,
        scratch_shapes=[
            pltpu.VMEM(start.shape, BF),
            pltpu.VMEM((4 * BS, tiles * LANES), F32),
        ],
        compiler_params=params(16),
        cost_estimate=cost(us),
        name="product",
    )(place, own, near, start, *srcs)


def coarse_kernel(sets, a0, a1, left_ref, *refs):
    outs = refs[-1 - len(sets) : -1]
    aps = refs[: -1 - len(sets)]
    scr = refs[-1]
    ac = a1 - a0
    tiles = aps[0].shape[2] // LANES
    for out, (i0, i1) in zip(outs, sets):
        rows = i1 - i0
        low = low_lanes(rows)
        for p0 in range(0, tiles, 2):
            p1 = min(p0 + 2, tiles)
            acc = jnp.zeros((rows * ac, (p1 - p0) * LANES), F32)
            ip = 0
            for ap in aps:
                for g in range(0, ap.shape[0] // 2, 2):
                    lhs = [left_ref[ip + d, i0:i1, a0:a1].reshape(rows * ac, LANES) for d in range(2)]
                    rhs = ap[2 * g : 2 * g + 4, :, p0 * LANES : p1 * LANES].reshape(4 * BS, (p1 - p0) * LANES)
                    acc = acc + dot(jnp.concatenate(lhs, axis=1), rhs)
                    ip += 2
            for p in range(p0, p1):
                scr[p, 0 : rows * ac] = acc[:, (p - p0) * LANES : (p - p0 + 1) * LANES]
        for p in range(tiles):
            for a in range(0, ac, 2):
                x0 = scr[p, pl.ds(a, rows, stride=ac), :]
                x1 = scr[p, pl.ds(a + 1, rows, stride=ac), :]
                at = slice(a * BS, (a + 2) * BS)
                out[p, :, at] = jnp.where(low, x0, pltpu.roll(x1, BS, 1)).astype(out.dtype)
                out[tiles + p, :, at] = jnp.where(low, pltpu.roll(x0, BS, 1), x1).astype(out.dtype)


def coarse_rows(left, aps, sets, a0, a1, dtype, us):
    tiles = aps[0].shape[2] // LANES
    return pl.pallas_call(
        functools.partial(coarse_kernel, sets, a0, a1),
        out_shape=[jax.ShapeDtypeStruct((2 * tiles, i1 - i0, (a1 - a0) * BS), dtype) for i0, i1 in sets],
        in_specs=[VM] * (1 + len(aps)),
        out_specs=[VM] * len(sets),
        scratch_shapes=[pltpu.VMEM((tiles, max(i1 - i0 for i0, i1 in sets) * (a1 - a0), LANES), F32)],
        compiler_params=params(12),
        cost_estimate=cost(us),
        name="coarse",
    )(left, *aps)


def assemble_kernel(order_ref, *refs):
    out = refs[-1]
    srcs = refs[:-1] if len(refs) % 2 else refs[1:-1]
    x = jnp.concatenate([s[...].reshape(-1, s.shape[2]) for s in srcs], axis=0)
    res = dot(order_ref[...], x)
    wide = out.shape[1]
    for i in range(CB):
        out[i] = res[i * wide : (i + 1) * wide].astype(BF)


def assemble(order, srcs, a0, total, before):
    n, _, lanes = srcs[0].shape
    step = 512
    per = lanes // step
    wide = n * len(srcs)
    specs = [pl.BlockSpec(order.shape, lambda i: (0, 0))]
    args = [order]
    alias = {}
    if before is not None:
        specs.append(pl.BlockSpec(memory_space=pl.ANY))
        args.append(before)
        alias = {1: 0}
    specs += [pl.BlockSpec((n, CB, step), lambda i: (0, 0, i))] * len(srcs)
    return pl.pallas_call(
        assemble_kernel,
        grid=(per,),
        out_shape=jax.ShapeDtypeStruct((CB, wide, total), BF),
        in_specs=specs,
        out_specs=pl.BlockSpec((CB, wide, step), lambda i: (0, 0, a0 * BS // step + i)),
        input_output_aliases=alias,
        compiler_params=params(12),
        cost_estimate=cost(2.9),
        name="assemble",
    )(*args, *srcs)


def assembly_order(shifts, ncol, share):
    col = lax.axis_index("col")
    y, core = col // 2, col % 2
    groups = GROUPS + 2
    size = ncol * share * groups * CB
    out_row = lax.broadcasted_iota(jnp.int32, (size, size), 0)
    src_row = lax.broadcasted_iota(jnp.int32, (size, size), 1)
    per = share * groups * CB
    which, rest = src_row // per, src_row % per
    e, g, i = rest // (groups * CB), rest // CB % groups, rest % CB
    src_col = jnp.zeros_like(which)
    for z, (s, flip) in enumerate(shifts):
        c = (y - s) % (ncol // 2) * 2 + (core + flip) % 2
        src_col = jnp.where(which == z, c, src_col)
    return (out_row == i * (groups * CB) + g * CB + share * src_col + e).astype(BF)


def body(a_blocks, a_cols, counts, p_blocks, p_cols):
    rb, ks, _ = a_blocks.shape
    nrow, ncol = lax.axis_size("row"), lax.axis_size("col")
    ny = ncol // 2
    nfb = p_cols.shape[0]
    share = CB // ncol
    tiles = (GROUPS * share + 1) // 2
    parts = ((0, rb * 2 // 3), (rb * 2 // 3, rb // 3))
    chunks = ((0, 24), (24, 48), (48, 64))

    def outward(x):
        pairs = [(r * ncol + c, (r + 1 - 2 * (c % 2)) * ncol + c) for r in range(nrow) for c in range(ncol)]
        return lax.ppermute(x, ("row", "col"), [(a, b) for a, b in pairs if 0 <= b < nrow * ncol])

    def over_y(x, s):
        return lax.ppermute(x, "col", [(y * 2 + c, (y + s) % ny * 2 + c) for y in range(ny) for c in range(2)])

    def over_core(x):
        return lax.ppermute(x, "col", [(c, c ^ 1) for c in range(ncol)])

    def upward(x):
        return lax.ppermute(x, "row", [(i, i + 1) for i in range(nrow - 1)])

    def downward(x):
        return lax.ppermute(x, "row", [(i + 1, i) for i in range(nrow - 1)])

    shifts = tuple((s, f) for s in range(ny) for f in range(2))
    pct = p_cols.T

    own_a, side_a, far_a = [], [], []
    for h, (first, rows) in enumerate(parts):
        x = relayout(a_blocks, first, rows)
        own_a.append(x)
        far_a.append([over_y(x, s) for s in range(1, ny)])
        side_a.append(over_core(x))
        if h == 0:
            p_own = relayout_rows(p_blocks)
            a_blocks, p_own, side_a[0] = lax.optimization_barrier((a_blocks, p_own, side_a[0]))
    beside = outward(p_own)
    p_blocks, p_own, side_a[1] = lax.optimization_barrier((p_blocks, p_own, side_a[1]))
    table = column_table(pct, rb, share)
    left = left_factor(pct, relayout(p_blocks, 0, rb))
    own = right_factor(table, [p_own], tiles, 2.0)
    order = assembly_order(shifts, ncol, share)
    place = slot_places(a_cols, counts)
    bands = [near_band(place, [own_a[h], side_a[h]], shifts[:2], parts[h][0]) for h in range(2)]
    beside, far_a[0], left, own, order, bands = lax.optimization_barrier((beside, far_a[0], left, own, order, bands))
    near = right_factor(table, [beside, over_core(beside)], tiles, 3.0)
    aps = []
    for h in range(2):
        srcs = [z for g in far_a[h] for z in (g, over_core(g))]
        aps.append(product(place, own, near, bands[h], srcs, shifts[2:], parts[h][0], 0.3 * parts[h][1]))
        if h == 0:
            far_a[1], aps[0] = lax.optimization_barrier((far_a[1], aps[0]))
            early = downward(coarse_rows(left, aps, ((0, CB // 2),), 0, BS, BF, 1.0)[0])

    def columns(x, g):
        y = x[: GROUPS * share].reshape((share, GROUPS) + x.shape[1:])
        return jnp.pad(y.astype(F32), ((0, 0), (g, 2 - g), (0, 0), (0, 0)))

    cut = chunks[0][1]
    lows = [coarse_rows(left, aps, ((CB // 2, CB),), a0, a1, BF, 1.0)[0] for a0, a1 in ((0, cut), (cut, BS))]
    raw = [coarse_rows(left, aps, ((2 * CB, 3 * CB),), a0, a1, BF, 1.0)[0] for a0, a1 in chunks]
    late = [downward(lows[0])]
    early, raw[0] = lax.optimization_barrier((early, raw[0]))
    highs = [upward(raw[0])]
    late[0], lows[1] = lax.optimization_barrier((late[0], lows[1]))
    late.append(downward(lows[1]))
    highs[0], raw[1] = lax.optimization_barrier((highs[0], raw[1]))
    highs.append(upward(raw[1]))
    late[1], raw[2] = lax.optimization_barrier((late[1], raw[2]))
    highs.append(upward(raw[2]))
    mids = [coarse_rows(left, aps, ((CB, 2 * CB),), a0, a1, F32, 1.0)[0] for a0, a1 in chunks]
    lower = [
        jnp.concatenate([early[:, :, : cut * BS], late[0]], axis=1),
        jnp.concatenate([early[:, :, cut * BS :], late[1]], axis=1),
    ]
    totals, sides, fars = [], [], []
    for z, (a0, a1) in enumerate(chunks):
        low = lower[0] if z == 0 else lower[1][:, :, (a0 - cut) * BS : (a1 - cut) * BS]
        total = columns(highs[z], 0) + columns(mids[z], 1) + columns(low, 2)
        total = total.astype(BF).reshape((share * (GROUPS + 2),) + total.shape[2:])
        totals.append(total)
        sides.append(over_core(total))
        fars.append([over_y(total, s) for s in range(1, ny)])
    for z in range(len(chunks) - 1):
        fars[z], _ = lax.optimization_barrier((fars[z], totals[z + 1]))
    out = None
    for z, (a0, a1) in enumerate(chunks):
        if z == 1:
            fars[1:], out = lax.optimization_barrier((fars[1:], out))
        srcs = [totals[z], sides[z]] + [q for x in fars[z] for q in (x, over_core(x))]
        out = assemble(order, srcs, a0, BS * BS, out)
    return out


def solution(mesh):
    return jax.shard_map(
        body,
        mesh=mesh,
        in_specs=(P("row", "col", None), P("row", None), P("row"), P("row", None, None), P()),
        out_specs=P("row", None, None),
        check_vma=False,
    )
```

```python
import functools

import jax
import jax.numpy as jnp
from jax import lax
from jax.experimental import pallas as pl
from jax.experimental.pallas import tpu as pltpu
from jax.sharding import PartitionSpec as P

BS = 64
CB = 8
GROUPS = 5
LANES = 128
BF = jnp.bfloat16
F32 = jnp.float32
MIB = 1 << 20

VM = pl.BlockSpec(memory_space=pltpu.VMEM)
SM = pl.BlockSpec(memory_space=pltpu.SMEM)


def params(mib):
    return pltpu.CompilerParams(vmem_limit_bytes=mib * MIB)


def cost(us):
    return pl.CostEstimate(flops=int(us * 1e8), bytes_accessed=int(us * 3.7e6), transcendentals=0)


def low_lanes(rows):
    return lax.broadcasted_iota(jnp.int32, (rows, LANES), 1) < BS


def dot(a, b):
    return lax.dot_general(a, b, (((1,), (0,)), ((), ())), preferred_element_type=F32)


def relayout_kernel(first, natural, x_ref, o_ref, buf, sems, scr, mix):
    parts, step, nb, _ = buf.shape
    low = low_lanes(32)

    def fetch(g):
        return pltpu.make_async_copy(x_ref.at[pl.ds(first + g * step, step)], buf.at[g], sems.at[g])

    for g in range(parts):
        fetch(g).start()

    def part(g, carry):
        fetch(g).wait()
        for r in range(step):
            for q in range(32):
                scr[r, pl.ds(q * 8, nb), :] = buf[g, r, :, q * LANES : (q + 1) * LANES].astype(F32)
            for k in range(0, nb, 2):
                x0 = scr[r, pl.ds(k, 32, stride=8), :]
                x1 = scr[r, pl.ds(k + 1, 32, stride=8), :]
                even = jnp.where(low, x0, pltpu.roll(x1, BS, 1))
                odd = jnp.where(low, pltpu.roll(x0, BS, 1), x1)
                if natural:
                    mix[r, k // 2, pl.ds(0, 32, stride=2), :] = even
                    mix[r, k // 2, pl.ds(1, 32, stride=2), :] = odd
                    o_ref[g * step + r, k // 2] = mix[r, k // 2].astype(BF)
                else:
                    o_ref[g * step + r, k // 2, 0:32] = even.astype(BF)
                    o_ref[g * step + r, k // 2, 32:64] = odd.astype(BF)
        return carry

    lax.fori_loop(0, parts, part, 0)


def relayout(x, first, rows, natural=False):
    nb = x.shape[1]
    step = 4
    return pl.pallas_call(
        functools.partial(relayout_kernel, first, natural),
        out_shape=jax.ShapeDtypeStruct((rows, nb // 2, BS, LANES), BF),
        in_specs=[pl.BlockSpec(memory_space=pltpu.HBM)],
        out_specs=VM,
        scratch_shapes=[
            pltpu.VMEM((rows // step, step, nb, BS * BS), BF),
            pltpu.SemaphoreType.DMA((rows // step,)),
            pltpu.VMEM((step, 256, LANES), F32),
            pltpu.VMEM((step, nb // 2, BS, LANES), F32),
        ],
        compiler_params=params(8),
        cost_estimate=cost(1.0),
        name="relayout",
    )(x)


def left_kernel(rb, pct_ref, pl_ref, o_ref):
    slab = lax.axis_index("row")
    low = low_lanes(4 * BS)
    o_ref[...] = jnp.zeros_like(o_ref)

    def pair(ip, carry):
        for half in range(2):
            i = ip * 2 + half
            x = jnp.concatenate([pl_ref[i, 0], pl_ref[i, 1]], axis=1).astype(F32)
            xt = jnp.concatenate([x, x], axis=0).T
            keep = jnp.where(low if half == 0 else jnp.logical_not(low), xt, 0.0)
            for s in range(4):
                w = pct_ref[s, slab * rb + i] - (slab - 1) * CB
                o_ref[ip, w] = (o_ref[ip, w].astype(F32) + keep[s * BS : (s + 1) * BS]).astype(BF)
        return carry

    lax.fori_loop(0, rb // 2, pair, 0)


def left_factor(pct, p_own):
    rb = p_own.shape[0]
    return pl.pallas_call(
        functools.partial(left_kernel, rb),
        out_shape=jax.ShapeDtypeStruct((rb // 2, 3 * CB, BS, LANES), BF),
        in_specs=[SM, VM],
        out_specs=VM,
        compiler_params=params(12),
        cost_estimate=cost(2.9),
        name="left_factor",
    )(pct, p_own)


def column_table(pct, rb, share):
    slab = lax.axis_index("row")
    padded = jnp.pad(pct, ((0, 0), (rb, rb)), constant_values=-1000000)
    near = lax.dynamic_slice_in_dim(padded, slab * rb, 3 * rb, 1)
    w = near - (slab - 2) * CB
    e = (w & (CB - 1)) - share * lax.axis_index("col")
    return jnp.where((w >= 0) & (e >= 0) & (e < share), e * GROUPS + (w >> 3), -1)


def touched(side, tiles):
    return (side, side + 3) if tiles == GROUPS else (0, tiles)


def right_kernel(kind, rb, tiles, table_ref, *refs):
    o_ref = refs[-1]
    core = lax.rem(lax.axis_index("col"), 2)
    low = lax.broadcasted_iota(jnp.int32, (1, LANES), 1) < BS
    wants = [jnp.where(low, p, tiles + p) for p in range(tiles)]

    def fill(src, side, out_first):
        def four(jq, carry):
            for d in range(4):
                jj = 4 * jq + d
                dups = []
                for t in range(4):
                    x = src[jj, t // 2, :, t % 2 * BS : (t % 2 + 1) * BS]
                    dups.append(jnp.concatenate([x, x], axis=1))
                at = [table_ref[t, side * rb + jj] for t in range(4)]
                for p in range(*touched(side, tiles)):
                    total = None
                    for t in range(4):
                        keep = dups[t] * jnp.where(wants[p] == at[t], 1.0, 0.0).astype(BF)
                        total = keep if total is None else total + keep
                    o_ref[out_first + jq, p, d * BS : (d + 1) * BS] = total
            return carry

        lax.fori_loop(0, rb // 4, four, 0)

    quads = rb // 4
    if kind == 0:
        fill(refs[0], 1, 0)
    elif kind == 1:

        @pl.when(core == 0)
        def _():
            fill(refs[0], 0, 0)

        @pl.when(core == 1)
        def _():
            fill(refs[0], 2, 0)
    else:

        def keep(side, out_first):
            def one(jq, carry):
                for p in range(*touched(side, tiles)):
                    o_ref[out_first + jq, p] = refs[0][jq, p]
                return carry

            lax.fori_loop(0, quads, one, 0)

        @pl.when(core == 0)
        def _():
            keep(0, 0)
            fill(refs[1], 2, quads)

        @pl.when(core == 1)
        def _():
            fill(refs[1], 0, 0)
            keep(2, quads)


def right_factor(kind, table, srcs, tiles, us):
    rb = table.shape[1] // 3
    quads = rb // 4 * (2 if kind == 2 else 1)
    return pl.pallas_call(
        functools.partial(right_kernel, kind, rb, tiles),
        out_shape=jax.ShapeDtypeStruct((quads, tiles, 4 * BS, LANES), BF),
        in_specs=[SM] + [VM] * len(srcs),
        out_specs=VM,
        compiler_params=params(8),
        cost_estimate=cost(us),
        name="right_factor",
    )(table, *srcs)


def slot_places(a_cols, counts):
    rb, ka = a_cols.shape
    row = jnp.arange(rb, dtype=jnp.int32)[:, None]
    near = a_cols - (lax.axis_index("row") - 1) * rb - row // 4 * 4
    live = jnp.arange(ka, dtype=jnp.int32)[None, :] < counts[:, None]
    return jnp.where(live, near, 2 * (rb + 2))


def first_slots(shifts, ks):
    col = lax.axis_index("col")
    ny = lax.axis_size("col") // 2
    y, core = col // 2, lax.rem(col, 2)
    slots = []
    for s, flip in shifts:
        c = core if flip == 0 else 1 - core
        slots.append((lax.rem(y - s + ny, ny) * 2 + c) * ks)
    return slots


def lay(first, place_ref, srcs, slots, band, start):
    low = low_lanes(BS)
    zero = jnp.zeros((BS, LANES), BF)

    def group(g, carry):
        for t in range(band.shape[1]):
            band[g, t] = start(g, t)
        for src, slot in zip(srcs, slots):
            for k in range(src.shape[1]):
                for d0 in range(0, 4, 2):
                    cuts = []
                    for d in range(d0, d0 + 2):
                        x = src[4 * g + d, k]
                        r = jnp.concatenate([x[:, BS:], x[:, :BS]], axis=1)
                        cuts.append(
                            (
                                (jnp.where(low, x, zero), jnp.where(low, zero, r)),
                                (jnp.where(low, r, zero), jnp.where(low, zero, x)),
                            )
                        )
                    for e in range(2):
                        at = [place_ref[first + 4 * g + d0 + d, slot + 2 * k + e] for d in range(2)]
                        spots = [(g, a >> 1, slice((d0 + d) * BS, (d0 + d + 1) * BS)) for d, a in enumerate(at)]
                        old = [band[spot] for spot in spots]
                        for spot, a, x, cut in zip(spots, at, old, cuts):
                            band[spot] = x + jnp.where((a & 1) == 0, cut[e][0], cut[e][1])
        return carry

    lax.fori_loop(0, band.shape[0], group, 0)


def band_kernel(first, shifts, place_ref, *refs):
    srcs, band = refs[:-1], refs[-1]
    slots = first_slots(shifts, srcs[0].shape[1] * 2)
    lay(first, place_ref, srcs, slots, band, lambda g, t: jnp.zeros((4 * BS, LANES), BF))


def near_band(place, srcs, shifts, first):
    rows = srcs[0].shape[0]
    return pl.pallas_call(
        functools.partial(band_kernel, first, shifts),
        out_shape=jax.ShapeDtypeStruct((rows // 4, place.shape[0] + 3, 4 * BS, LANES), BF),
        in_specs=[SM] + [VM] * len(srcs),
        out_specs=VM,
        compiler_params=params(12),
        cost_estimate=cost(0.16 * rows),
        name="near_band",
    )(place, *srcs)


def product_kernel(first, rb, shifts, place_ref, own_ref, near_ref, start_ref, *refs):
    srcs = refs[: len(shifts)]
    o_ref, band, acc = refs[len(shifts) :]
    rows = o_ref.shape[0]
    tiles = own_ref.shape[1]
    wide = rb + 2
    slots = first_slots(shifts, srcs[0].shape[1] * 2)
    lay(first, place_ref, srcs, slots, band, lambda g, t: start_ref[g, t])
    quads = rb // 4
    for g in range(rows // 4):
        start = first // 4 + g
        acc[...] = jnp.zeros_like(acc)
        for side in range(3):
            k0, k1 = max(start, side * quads), min(start + wide // 2, (side + 1) * quads)
            if k0 >= k1:
                continue
            p0, p1 = touched(side, tiles)
            ref, base = (own_ref, quads) if side == 1 else (near_ref, 0 if side == 0 else quads)
            total = None
            for k in range(k0, k1):
                lhs = jnp.concatenate([band[g, 2 * (k - start)], band[g, 2 * (k - start) + 1]], axis=1)
                rhs = jnp.concatenate([ref[k - base, p] for p in range(p0, p1)], axis=1)
                part = dot(lhs, rhs)
                total = part if total is None else total + part
            acc[:, p0 * LANES : p1 * LANES] += total
        for d in range(4):
            o_ref[4 * g + d] = acc[d * BS : (d + 1) * BS].astype(BF)


def product(place, own, near, start, srcs, shifts, first, us):
    rows = srcs[0].shape[0]
    rb = place.shape[0]
    tiles = own.shape[1]
    return pl.pallas_call(
        functools.partial(product_kernel, first, rb, shifts),
        out_shape=jax.ShapeDtypeStruct((rows, BS, tiles * LANES), BF),
        in_specs=[SM] + [VM] * (3 + len(srcs)),
        out_specs=VM,
        scratch_shapes=[
            pltpu.VMEM(start.shape, BF),
            pltpu.VMEM((4 * BS, tiles * LANES), F32),
        ],
        compiler_params=params(16),
        cost_estimate=cost(us),
        name="product",
    )(place, own, near, start, *srcs)


def coarse_kernel(sets, a0, a1, left_ref, *refs):
    outs = refs[-1 - len(sets) : -1]
    aps = refs[: -1 - len(sets)]
    scr = refs[-1]
    ac = a1 - a0
    tiles = aps[0].shape[2] // LANES
    for out, (i0, i1) in zip(outs, sets):
        rows = i1 - i0
        low = low_lanes(rows)
        for p0 in range(0, tiles, 2):
            p1 = min(p0 + 2, tiles)
            acc = jnp.zeros((rows * ac, (p1 - p0) * LANES), F32)
            ip = 0
            for ap in aps:
                for g in range(0, ap.shape[0] // 2, 2):
                    lhs = [left_ref[ip + d, i0:i1, a0:a1].reshape(rows * ac, LANES) for d in range(2)]
                    rhs = ap[2 * g : 2 * g + 4, :, p0 * LANES : p1 * LANES].reshape(4 * BS, (p1 - p0) * LANES)
                    acc = acc + dot(jnp.concatenate(lhs, axis=1), rhs)
                    ip += 2
            for p in range(p0, p1):
                scr[p, 0 : rows * ac] = acc[:, (p - p0) * LANES : (p - p0 + 1) * LANES]
        for p in range(tiles):
            for a in range(0, ac, 2):
                x0 = scr[p, pl.ds(a, rows, stride=ac), :]
                x1 = scr[p, pl.ds(a + 1, rows, stride=ac), :]
                at = slice(a * BS, (a + 2) * BS)
                out[p, :, at] = jnp.where(low, x0, pltpu.roll(x1, BS, 1)).astype(out.dtype)
                out[tiles + p, :, at] = jnp.where(low, pltpu.roll(x0, BS, 1), x1).astype(out.dtype)


def coarse_rows(left, aps, sets, a0, a1, dtype, us):
    tiles = aps[0].shape[2] // LANES
    return pl.pallas_call(
        functools.partial(coarse_kernel, sets, a0, a1),
        out_shape=[jax.ShapeDtypeStruct((2 * tiles, i1 - i0, (a1 - a0) * BS), dtype) for i0, i1 in sets],
        in_specs=[VM] * (1 + len(aps)),
        out_specs=[VM] * len(sets),
        scratch_shapes=[pltpu.VMEM((tiles, max(i1 - i0 for i0, i1 in sets) * (a1 - a0), LANES), F32)],
        compiler_params=params(12),
        cost_estimate=cost(us),
        name="coarse",
    )(left, *aps)


def assemble_kernel(order_ref, *refs):
    out = refs[-1]
    srcs = refs[:-1] if len(refs) % 2 else refs[1:-1]
    x = jnp.concatenate([s[...].reshape(-1, s.shape[2]) for s in srcs], axis=0)
    res = dot(order_ref[...], x)
    wide = out.shape[1]
    for i in range(CB):
        out[i] = res[i * wide : (i + 1) * wide].astype(BF)


def assemble(order, srcs, a0, total, before):
    n, _, lanes = srcs[0].shape
    step = lanes
    per = lanes // step
    wide = n * len(srcs)
    specs = [pl.BlockSpec(order.shape, lambda i: (0, 0))]
    args = [order]
    alias = {}
    if before is not None:
        specs.append(pl.BlockSpec(memory_space=pl.ANY))
        args.append(before)
        alias = {1: 0}
    specs += [pl.BlockSpec((n, CB, step), lambda i: (0, 0, i))] * len(srcs)
    return pl.pallas_call(
        assemble_kernel,
        grid=(per,),
        out_shape=jax.ShapeDtypeStruct((CB, wide, total), BF),
        in_specs=specs,
        out_specs=pl.BlockSpec((CB, wide, step), lambda i: (0, 0, a0 * BS // step + i)),
        input_output_aliases=alias,
        compiler_params=params(12),
        cost_estimate=cost(2.9),
        name="assemble",
    )(*args, *srcs)


def assembly_order(shifts, ncol, share):
    col = lax.axis_index("col")
    y, core = col // 2, col % 2
    groups = GROUPS + 2
    size = ncol * share * groups * CB
    out_row = lax.broadcasted_iota(jnp.int32, (size, size), 0)
    src_row = lax.broadcasted_iota(jnp.int32, (size, size), 1)
    per = share * groups * CB
    which, rest = src_row // per, src_row % per
    e, g, i = rest // (groups * CB), rest // CB % groups, rest % CB
    src_col = jnp.zeros_like(which)
    for z, (s, flip) in enumerate(shifts):
        c = (y - s) % (ncol // 2) * 2 + (core + flip) % 2
        src_col = jnp.where(which == z, c, src_col)
    return (out_row == i * (groups * CB) + g * CB + share * src_col + e).astype(BF)


def body(a_blocks, a_cols, counts, p_blocks, p_cols):
    rb, ks, _ = a_blocks.shape
    nrow, ncol = lax.axis_size("row"), lax.axis_size("col")
    ny = ncol // 2
    nfb = p_cols.shape[0]
    share = CB // ncol
    tiles = (GROUPS * share + 1) // 2
    parts = ((0, rb * 2 // 3), (rb * 2 // 3, rb // 3))
    chunks = ((0, 24), (24, 48), (48, 64))

    def outward(x):
        pairs = [(r * ncol + c, (r + 1 - 2 * (c % 2)) * ncol + c) for r in range(nrow) for c in range(ncol)]
        return lax.ppermute(x, ("row", "col"), [(a, b) for a, b in pairs if 0 <= b < nrow * ncol])

    def over_y(x, s):
        return lax.ppermute(x, "col", [(y * 2 + c, (y + s) % ny * 2 + c) for y in range(ny) for c in range(2)])

    def over_core(x):
        return lax.ppermute(x, "col", [(c, c ^ 1) for c in range(ncol)])

    def upward(x):
        return lax.ppermute(x, "row", [(i, i + 1) for i in range(nrow - 1)])

    def downward(x):
        return lax.ppermute(x, "row", [(i + 1, i) for i in range(nrow - 1)])

    shifts = tuple((s, f) for s in range(ny) for f in range(2))
    pct = p_cols.T

    own_a, side_a, far_a = [], [], []
    for h, (first, rows) in enumerate(parts):
        x = relayout(a_blocks, first, rows)
        own_a.append(x)
        far_a.append([over_y(x, s) for s in range(1, ny)])
        side_a.append(over_core(x))
        if h == 0:
            p_own = relayout(p_blocks, 0, rb, True)
            a_blocks, p_own, side_a[0] = lax.optimization_barrier((a_blocks, p_own, side_a[0]))
    beside = outward(p_own)
    p_blocks, p_own, side_a[1] = lax.optimization_barrier((p_blocks, p_own, side_a[1]))
    table = column_table(pct, rb, share)
    left = left_factor(pct, relayout(p_blocks, 0, rb))
    own = right_factor(0, table, [p_own], tiles, 1.4)
    order = assembly_order(shifts, ncol, share)
    place = slot_places(a_cols, counts)
    bands = [near_band(place, [own_a[h], side_a[h]], shifts[:2], parts[h][0]) for h in range(2)]
    beside, far_a[0], left, own, order, bands = lax.optimization_barrier((beside, far_a[0], left, own, order, bands))
    near = right_factor(1, table, [beside], tiles, 1.2)
    near = right_factor(2, table, [near, over_core(beside)], tiles, 1.4)
    aps = []
    for h in range(2):
        srcs = [z for g in far_a[h] for z in (g, over_core(g))]
        aps.append(product(place, own, near, bands[h], srcs, shifts[2:], parts[h][0], 0.3 * parts[h][1]))
        if h == 0:
            far_a[1], aps[0] = lax.optimization_barrier((far_a[1], aps[0]))
            early = downward(coarse_rows(left, aps, ((0, CB // 2),), 0, BS, BF, 1.0)[0])

    def columns(x, g):
        y = x[: GROUPS * share].reshape((share, GROUPS) + x.shape[1:])
        return jnp.pad(y.astype(F32), ((0, 0), (g, 2 - g), (0, 0), (0, 0)))

    cut = chunks[0][1]
    lows = [coarse_rows(left, aps, ((CB // 2, CB),), a0, a1, BF, 1.0)[0] for a0, a1 in ((0, cut), (cut, BS))]
    raw = [coarse_rows(left, aps, ((2 * CB, 3 * CB),), a0, a1, BF, 1.0)[0] for a0, a1 in chunks]
    late = [downward(lows[0])]
    early, raw[0] = lax.optimization_barrier((early, raw[0]))
    highs = [upward(raw[0])]
    late[0], lows[1] = lax.optimization_barrier((late[0], lows[1]))
    late.append(downward(lows[1]))
    highs[0], raw[1] = lax.optimization_barrier((highs[0], raw[1]))
    highs.append(upward(raw[1]))
    late[1], raw[2] = lax.optimization_barrier((late[1], raw[2]))
    highs.append(upward(raw[2]))
    mids = [coarse_rows(left, aps, ((CB, 2 * CB),), a0, a1, F32, 1.0)[0] for a0, a1 in chunks]
    lower = [
        jnp.concatenate([early[:, :, : cut * BS], late[0]], axis=1),
        jnp.concatenate([early[:, :, cut * BS :], late[1]], axis=1),
    ]
    totals, sides, fars = [], [], []
    for z, (a0, a1) in enumerate(chunks):
        low = lower[0] if z == 0 else lower[1][:, :, (a0 - cut) * BS : (a1 - cut) * BS]
        total = columns(highs[z], 0) + columns(mids[z], 1) + columns(low, 2)
        total = total.astype(BF).reshape((share * (GROUPS + 2),) + total.shape[2:])
        totals.append(total)
        sides.append(over_core(total))
        fars.append([over_y(total, s) for s in range(1, ny)])
    for z in range(len(chunks) - 1):
        fars[z], _ = lax.optimization_barrier((fars[z], totals[z + 1]))
    out = None
    for z, (a0, a1) in enumerate(chunks):
        if z == 1:
            fars[1:], out = lax.optimization_barrier((fars[1:], out))
        srcs = [totals[z], sides[z]] + [q for x in fars[z] for q in (x, over_core(x))]
        out = assemble(order, srcs, a0, BS * BS, out)
    return out


def solution(mesh):
    return jax.shard_map(
        body,
        mesh=mesh,
        in_specs=(P("row", "col", None), P("row", None), P("row"), P("row", None, None), P()),
        out_specs=P("row", None, None),
        check_vma=False,
    )
```

```python
import functools

import jax
import jax.numpy as jnp
from jax import lax
from jax.experimental import pallas as pl
from jax.experimental.pallas import tpu as pltpu
from jax.sharding import PartitionSpec as P

BS = 64
CB = 8
GROUPS = 5
LANES = 128
BF = jnp.bfloat16
F32 = jnp.float32
MIB = 1 << 20

VM = pl.BlockSpec(memory_space=pltpu.VMEM)
SM = pl.BlockSpec(memory_space=pltpu.SMEM)


def params(mib):
    return pltpu.CompilerParams(vmem_limit_bytes=mib * MIB)


def cost(us):
    return pl.CostEstimate(flops=int(us * 1e8), bytes_accessed=int(us * 3.7e6), transcendentals=0)


def low_lanes(rows):
    return lax.broadcasted_iota(jnp.int32, (rows, LANES), 1) < BS


def dot(a, b):
    return lax.dot_general(a, b, (((1,), (0,)), ((), ())), preferred_element_type=F32)


def relayout_kernel(x_ref, o_ref, scr):
    rows, nb, _ = x_ref.shape
    low = low_lanes(32)
    for r in range(rows):
        for q in range(32):
            scr[r, pl.ds(q * 8, nb), :] = x_ref[r, :, q * LANES : (q + 1) * LANES].astype(F32)
        for k in range(0, nb, 2):
            x0 = scr[r, pl.ds(k, 32, stride=8), :]
            x1 = scr[r, pl.ds(k + 1, 32, stride=8), :]
            o_ref[r, k // 2, 0:32] = jnp.where(low, x0, pltpu.roll(x1, BS, 1)).astype(BF)
            o_ref[r, k // 2, 32:64] = jnp.where(low, pltpu.roll(x0, BS, 1), x1).astype(BF)


def relayout(x, first, rows):
    nb = x.shape[1]
    step = 4
    return pl.pallas_call(
        relayout_kernel,
        grid=(rows // step,),
        out_shape=jax.ShapeDtypeStruct((rows, nb // 2, BS, LANES), BF),
        in_specs=[pl.BlockSpec((step, nb, BS * BS), lambda i: (i + first // step, 0, 0))],
        out_specs=pl.BlockSpec((step, nb // 2, BS, LANES), lambda i: (i, 0, 0, 0)),
        scratch_shapes=[pltpu.VMEM((step, 256, LANES), F32)],
        compiler_params=params(4),
        cost_estimate=cost(0.6),
        name="relayout",
    )(x)


def relayout_rows_kernel(x_ref, o_ref, scr, mix):
    rows, nb, _ = x_ref.shape
    low = low_lanes(32)
    for r in range(rows):
        for q in range(32):
            scr[r, pl.ds(q * 8, nb), :] = x_ref[r, :, q * LANES : (q + 1) * LANES].astype(F32)
        for k in range(0, nb, 2):
            x0 = scr[r, pl.ds(k, 32, stride=8), :]
            x1 = scr[r, pl.ds(k + 1, 32, stride=8), :]
            mix[r, k // 2, pl.ds(0, 32, stride=2), :] = jnp.where(low, x0, pltpu.roll(x1, BS, 1))
            mix[r, k // 2, pl.ds(1, 32, stride=2), :] = jnp.where(low, pltpu.roll(x0, BS, 1), x1)
            o_ref[r, k // 2] = mix[r, k // 2].astype(BF)


def relayout_rows(x):
    rows, nb, _ = x.shape
    step = 4
    return pl.pallas_call(
        relayout_rows_kernel,
        grid=(rows // step,),
        out_shape=jax.ShapeDtypeStruct((rows, nb // 2, BS, LANES), BF),
        in_specs=[pl.BlockSpec((step, nb, BS * BS), lambda i: (i, 0, 0))],
        out_specs=pl.BlockSpec((step, nb // 2, BS, LANES), lambda i: (i, 0, 0, 0)),
        scratch_shapes=[pltpu.VMEM((step, 256, LANES), F32), pltpu.VMEM((step, nb // 2, BS, LANES), F32)],
        compiler_params=params(4),
        cost_estimate=cost(1.0),
        name="relayout_rows",
    )(x)


def left_kernel(rb, pct_ref, pl_ref, o_ref):
    slab = lax.axis_index("row")
    low = low_lanes(4 * BS)
    o_ref[...] = jnp.zeros_like(o_ref)

    def pair(ip, carry):
        for half in range(2):
            i = ip * 2 + half
            x = jnp.concatenate([pl_ref[i, 0], pl_ref[i, 1]], axis=1).astype(F32)
            xt = jnp.concatenate([x, x], axis=0).T
            keep = jnp.where(low if half == 0 else jnp.logical_not(low), xt, 0.0)
            for s in range(4):
                w = pct_ref[s, slab * rb + i] - (slab - 1) * CB
                o_ref[ip, w] = (o_ref[ip, w].astype(F32) + keep[s * BS : (s + 1) * BS]).astype(BF)
        return carry

    lax.fori_loop(0, rb // 2, pair, 0)


def left_factor(pct, p_own):
    rb = p_own.shape[0]
    return pl.pallas_call(
        functools.partial(left_kernel, rb),
        out_shape=jax.ShapeDtypeStruct((rb // 2, 3 * CB, BS, LANES), BF),
        in_specs=[SM, VM],
        out_specs=VM,
        compiler_params=params(12),
        cost_estimate=cost(2.9),
        name="left_factor",
    )(pct, p_own)


def column_table(pct, rb, share):
    slab = lax.axis_index("row")
    padded = jnp.pad(pct, ((0, 0), (rb, rb)), constant_values=-1000000)
    near = lax.dynamic_slice_in_dim(padded, slab * rb, 3 * rb, 1)
    w = near - (slab - 2) * CB
    e = (w & (CB - 1)) - share * lax.axis_index("col")
    return jnp.where((w >= 0) & (e >= 0) & (e < share), e * GROUPS + (w >> 3), -1)


def touched(side, tiles):
    return (side, side + 3) if tiles == GROUPS else (0, tiles)


def right_kernel(kind, rb, tiles, table_ref, *refs):
    o_ref = refs[-1]
    core = lax.rem(lax.axis_index("col"), 2)
    low = lax.broadcasted_iota(jnp.int32, (1, LANES), 1) < BS
    wants = [jnp.where(low, p, tiles + p) for p in range(tiles)]

    def fill(src, side, out_first):
        def four(jq, carry):
            for d in range(4):
                jj = 4 * jq + d
                dups = []
                for t in range(4):
                    x = src[jj, t // 2, :, t % 2 * BS : (t % 2 + 1) * BS]
                    dups.append(jnp.concatenate([x, x], axis=1))
                at = [table_ref[t, side * rb + jj] for t in range(4)]
                for p in range(*touched(side, tiles)):
                    total = None
                    for t in range(4):
                        keep = dups[t] * jnp.where(wants[p] == at[t], 1.0, 0.0).astype(BF)
                        total = keep if total is None else total + keep
                    o_ref[out_first + jq, p, d * BS : (d + 1) * BS] = total
            return carry

        lax.fori_loop(0, rb // 4, four, 0)

    quads = rb // 4
    if kind == 0:
        fill(refs[0], 1, 0)
    elif kind == 1:

        @pl.when(core == 0)
        def _():
            fill(refs[0], 0, 0)

        @pl.when(core == 1)
        def _():
            fill(refs[0], 2, 0)
    else:

        def keep(side, out_first):
            def one(jq, carry):
                for p in range(*touched(side, tiles)):
                    o_ref[out_first + jq, p] = refs[0][jq, p]
                return carry

            lax.fori_loop(0, quads, one, 0)

        @pl.when(core == 0)
        def _():
            keep(0, 0)
            fill(refs[1], 2, quads)

        @pl.when(core == 1)
        def _():
            fill(refs[1], 0, 0)
            keep(2, quads)


def right_factor(kind, table, srcs, tiles, us):
    rb = table.shape[1] // 3
    quads = rb // 4 * (2 if kind == 2 else 1)
    return pl.pallas_call(
        functools.partial(right_kernel, kind, rb, tiles),
        out_shape=jax.ShapeDtypeStruct((quads, tiles, 4 * BS, LANES), BF),
        in_specs=[SM] + [VM] * len(srcs),
        out_specs=VM,
        compiler_params=params(8),
        cost_estimate=cost(us),
        name="right_factor",
    )(table, *srcs)


def slot_places(a_cols, counts):
    rb, ka = a_cols.shape
    row = jnp.arange(rb, dtype=jnp.int32)[:, None]
    near = a_cols - (lax.axis_index("row") - 1) * rb - row // 4 * 4
    live = jnp.arange(ka, dtype=jnp.int32)[None, :] < counts[:, None]
    return jnp.where(live, near, 2 * (rb + 2))


def first_slots(shifts, ks):
    col = lax.axis_index("col")
    ny = lax.axis_size("col") // 2
    y, core = col // 2, lax.rem(col, 2)
    slots = []
    for s, flip in shifts:
        c = core if flip == 0 else 1 - core
        slots.append((lax.rem(y - s + ny, ny) * 2 + c) * ks)
    return slots


def lay(first, place_ref, srcs, slots, band, start):
    low = low_lanes(BS)
    zero = jnp.zeros((BS, LANES), BF)

    def group(g, carry):
        for t in range(band.shape[1]):
            band[g, t] = start(g, t)
        for src, slot in zip(srcs, slots):
            for k in range(src.shape[1]):
                for d0 in range(0, 4, 2):
                    cuts = []
                    for d in range(d0, d0 + 2):
                        x = src[4 * g + d, k]
                        r = jnp.concatenate([x[:, BS:], x[:, :BS]], axis=1)
                        cuts.append(
                            (
                                (jnp.where(low, x, zero), jnp.where(low, zero, r)),
                                (jnp.where(low, r, zero), jnp.where(low, zero, x)),
                            )
                        )
                    for e in range(2):
                        at = [place_ref[first + 4 * g + d0 + d, slot + 2 * k + e] for d in range(2)]
                        spots = [(g, a >> 1, slice((d0 + d) * BS, (d0 + d + 1) * BS)) for d, a in enumerate(at)]
                        old = [band[spot] for spot in spots]
                        for spot, a, x, cut in zip(spots, at, old, cuts):
                            band[spot] = x + jnp.where((a & 1) == 0, cut[e][0], cut[e][1])
        return carry

    lax.fori_loop(0, band.shape[0], group, 0)


def band_kernel(first, shifts, place_ref, *refs):
    srcs, band = refs[:-1], refs[-1]
    slots = first_slots(shifts, srcs[0].shape[1] * 2)
    lay(first, place_ref, srcs, slots, band, lambda g, t: jnp.zeros((4 * BS, LANES), BF))


def near_band(place, srcs, shifts, first):
    rows = srcs[0].shape[0]
    return pl.pallas_call(
        functools.partial(band_kernel, first, shifts),
        out_shape=jax.ShapeDtypeStruct((rows // 4, place.shape[0] + 3, 4 * BS, LANES), BF),
        in_specs=[SM] + [VM] * len(srcs),
        out_specs=VM,
        compiler_params=params(12),
        cost_estimate=cost(0.16 * rows),
        name="near_band",
    )(place, *srcs)


def product_kernel(first, rb, shifts, place_ref, own_ref, near_ref, start_ref, *refs):
    srcs = refs[: len(shifts)]
    o_ref, band, acc = refs[len(shifts) :]
    rows = o_ref.shape[0]
    tiles = own_ref.shape[1]
    wide = rb + 2
    slots = first_slots(shifts, srcs[0].shape[1] * 2)
    lay(first, place_ref, srcs, slots, band, lambda g, t: start_ref[g, t])
    quads = rb // 4
    for g in range(rows // 4):
        start = first // 4 + g
        acc[...] = jnp.zeros_like(acc)
        for side in range(3):
            k0, k1 = max(start, side * quads), min(start + wide // 2, (side + 1) * quads)
            if k0 >= k1:
                continue
            p0, p1 = touched(side, tiles)
            ref, base = (own_ref, quads) if side == 1 else (near_ref, 0 if side == 0 else quads)
            total = None
            for k in range(k0, k1):
                lhs = jnp.concatenate([band[g, 2 * (k - start)], band[g, 2 * (k - start) + 1]], axis=1)
                rhs = jnp.concatenate([ref[k - base, p] for p in range(p0, p1)], axis=1)
                part = dot(lhs, rhs)
                total = part if total is None else total + part
            acc[:, p0 * LANES : p1 * LANES] += total
        for d in range(4):
            o_ref[4 * g + d] = acc[d * BS : (d + 1) * BS].astype(BF)


def product(place, own, near, start, srcs, shifts, first, us):
    rows = srcs[0].shape[0]
    rb = place.shape[0]
    tiles = own.shape[1]
    return pl.pallas_call(
        functools.partial(product_kernel, first, rb, shifts),
        out_shape=jax.ShapeDtypeStruct((rows, BS, tiles * LANES), BF),
        in_specs=[SM] + [VM] * (3 + len(srcs)),
        out_specs=VM,
        scratch_shapes=[
            pltpu.VMEM(start.shape, BF),
            pltpu.VMEM((4 * BS, tiles * LANES), F32),
        ],
        compiler_params=params(16),
        cost_estimate=cost(us),
        name="product",
    )(place, own, near, start, *srcs)


def coarse_kernel(sets, a0, a1, left_ref, *refs):
    outs = refs[-1 - len(sets) : -1]
    aps = refs[: -1 - len(sets)]
    scr = refs[-1]
    ac = a1 - a0
    tiles = aps[0].shape[2] // LANES
    for out, (i0, i1) in zip(outs, sets):
        rows = i1 - i0
        low = low_lanes(rows)
        for p0 in range(0, tiles, 2):
            p1 = min(p0 + 2, tiles)
            acc = jnp.zeros((rows * ac, (p1 - p0) * LANES), F32)
            ip = 0
            for ap in aps:
                for g in range(0, ap.shape[0] // 2, 2):
                    lhs = [left_ref[ip + d, i0:i1, a0:a1].reshape(rows * ac, LANES) for d in range(2)]
                    rhs = ap[2 * g : 2 * g + 4, :, p0 * LANES : p1 * LANES].reshape(4 * BS, (p1 - p0) * LANES)
                    acc = acc + dot(jnp.concatenate(lhs, axis=1), rhs)
                    ip += 2
            for p in range(p0, p1):
                scr[p, 0 : rows * ac] = acc[:, (p - p0) * LANES : (p - p0 + 1) * LANES]
        for p in range(tiles):
            for a in range(0, ac, 2):
                x0 = scr[p, pl.ds(a, rows, stride=ac), :]
                x1 = scr[p, pl.ds(a + 1, rows, stride=ac), :]
                at = slice(a * BS, (a + 2) * BS)
                out[p, :, at] = jnp.where(low, x0, pltpu.roll(x1, BS, 1)).astype(out.dtype)
                out[tiles + p, :, at] = jnp.where(low, pltpu.roll(x0, BS, 1), x1).astype(out.dtype)


def coarse_rows(left, aps, sets, a0, a1, dtype, us):
    tiles = aps[0].shape[2] // LANES
    return pl.pallas_call(
        functools.partial(coarse_kernel, sets, a0, a1),
        out_shape=[jax.ShapeDtypeStruct((2 * tiles, i1 - i0, (a1 - a0) * BS), dtype) for i0, i1 in sets],
        in_specs=[VM] * (1 + len(aps)),
        out_specs=[VM] * len(sets),
        scratch_shapes=[pltpu.VMEM((tiles, max(i1 - i0 for i0, i1 in sets) * (a1 - a0), LANES), F32)],
        compiler_params=params(12),
        cost_estimate=cost(us),
        name="coarse",
    )(left, *aps)


def assemble_kernel(order_ref, *refs):
    out = refs[-1]
    srcs = refs[:-1] if len(refs) % 2 else refs[1:-1]
    x = jnp.concatenate([s[...].reshape(-1, s.shape[2]) for s in srcs], axis=0)
    res = dot(order_ref[...], x)
    wide = out.shape[1]
    for i in range(CB):
        out[i] = res[i * wide : (i + 1) * wide].astype(BF)


def assemble(order, srcs, a0, total, before):
    n, _, lanes = srcs[0].shape
    step = lanes
    per = lanes // step
    wide = n * len(srcs)
    specs = [pl.BlockSpec(order.shape, lambda i: (0, 0))]
    args = [order]
    alias = {}
    if before is not None:
        specs.append(pl.BlockSpec(memory_space=pl.ANY))
        args.append(before)
        alias = {1: 0}
    specs += [pl.BlockSpec((n, CB, step), lambda i: (0, 0, i))] * len(srcs)
    return pl.pallas_call(
        assemble_kernel,
        grid=(per,),
        out_shape=jax.ShapeDtypeStruct((CB, wide, total), BF),
        in_specs=specs,
        out_specs=pl.BlockSpec((CB, wide, step), lambda i: (0, 0, a0 * BS // step + i)),
        input_output_aliases=alias,
        compiler_params=params(12),
        cost_estimate=cost(2.9),
        name="assemble",
    )(*args, *srcs)


def assembly_order(shifts, ncol, share):
    col = lax.axis_index("col")
    y, core = col // 2, col % 2
    groups = GROUPS + 2
    size = ncol * share * groups * CB
    out_row = lax.broadcasted_iota(jnp.int32, (size, size), 0)
    src_row = lax.broadcasted_iota(jnp.int32, (size, size), 1)
    per = share * groups * CB
    which, rest = src_row // per, src_row % per
    e, g, i = rest // (groups * CB), rest // CB % groups, rest % CB
    src_col = jnp.zeros_like(which)
    for z, (s, flip) in enumerate(shifts):
        c = (y - s) % (ncol // 2) * 2 + (core + flip) % 2
        src_col = jnp.where(which == z, c, src_col)
    return (out_row == i * (groups * CB) + g * CB + share * src_col + e).astype(BF)


def body(a_blocks, a_cols, counts, p_blocks, p_cols):
    rb, ks, _ = a_blocks.shape
    nrow, ncol = lax.axis_size("row"), lax.axis_size("col")
    ny = ncol // 2
    nfb = p_cols.shape[0]
    share = CB // ncol
    tiles = (GROUPS * share + 1) // 2
    parts = ((0, rb * 2 // 3), (rb * 2 // 3, rb // 3))
    chunks = ((0, 32), (32, 64))

    def outward(x):
        pairs = [(r * ncol + c, (r + 1 - 2 * (c % 2)) * ncol + c) for r in range(nrow) for c in range(ncol)]
        return lax.ppermute(x, ("row", "col"), [(a, b) for a, b in pairs if 0 <= b < nrow * ncol])

    def over_y(x, s):
        return lax.ppermute(x, "col", [(y * 2 + c, (y + s) % ny * 2 + c) for y in range(ny) for c in range(2)])

    def over_core(x):
        return lax.ppermute(x, "col", [(c, c ^ 1) for c in range(ncol)])

    def upward(x):
        return lax.ppermute(x, "row", [(i, i + 1) for i in range(nrow - 1)])

    def downward(x):
        return lax.ppermute(x, "row", [(i + 1, i) for i in range(nrow - 1)])

    shifts = tuple((s, f) for s in range(ny) for f in range(2))
    pct = p_cols.T

    own_a, side_a, far_a = [], [], []
    for h, (first, rows) in enumerate(parts):
        x = relayout(a_blocks, first, rows)
        own_a.append(x)
        far_a.append([over_y(x, s) for s in range(1, ny)])
        side_a.append(over_core(x))
        if h == 0:
            p_own = relayout_rows(p_blocks)
            a_blocks, p_own, side_a[0] = lax.optimization_barrier((a_blocks, p_own, side_a[0]))
    beside = outward(p_own)
    p_blocks, p_own, side_a[1] = lax.optimization_barrier((p_blocks, p_own, side_a[1]))
    table = column_table(pct, rb, share)
    left = left_factor(pct, relayout(p_blocks, 0, rb))
    own = right_factor(0, table, [p_own], tiles, 1.4)
    order = assembly_order(shifts, ncol, share)
    place = slot_places(a_cols, counts)
    bands = [near_band(place, [own_a[h], side_a[h]], shifts[:2], parts[h][0]) for h in range(2)]
    beside, far_a[0], left, own, order, bands = lax.optimization_barrier((beside, far_a[0], left, own, order, bands))
    near = right_factor(1, table, [beside], tiles, 1.2)
    near = right_factor(2, table, [near, over_core(beside)], tiles, 1.4)
    aps = []
    for h in range(2):
        srcs = [z for g in far_a[h] for z in (g, over_core(g))]
        aps.append(product(place, own, near, bands[h], srcs, shifts[2:], parts[h][0], 0.3 * parts[h][1]))
        if h == 0:
            far_a[1], aps[0] = lax.optimization_barrier((far_a[1], aps[0]))
            early = downward(coarse_rows(left, aps, ((0, CB // 2),), 0, BS, BF, 1.0)[0])

    def columns(x, g):
        y = x[: GROUPS * share].reshape((share, GROUPS) + x.shape[1:])
        return jnp.pad(y.astype(F32), ((0, 0), (g, 2 - g), (0, 0), (0, 0)))

    cut = chunks[0][1]
    lows = [coarse_rows(left, aps, ((CB // 2, CB),), a0, a1, BF, 1.0)[0] for a0, a1 in ((0, cut), (cut, BS))]
    raw = [coarse_rows(left, aps, ((2 * CB, 3 * CB),), a0, a1, BF, 1.0)[0] for a0, a1 in chunks]
    late = [downward(lows[0])]
    early, raw[0] = lax.optimization_barrier((early, raw[0]))
    highs = [upward(raw[0])]
    late[0], lows[1] = lax.optimization_barrier((late[0], lows[1]))
    late.append(downward(lows[1]))
    highs[0], raw[1] = lax.optimization_barrier((highs[0], raw[1]))
    highs.append(upward(raw[1]))
    mids = [coarse_rows(left, aps, ((CB, 2 * CB),), a0, a1, F32, 1.0)[0] for a0, a1 in chunks]
    lower = [
        jnp.concatenate([early[:, :, : cut * BS], late[0]], axis=1),
        jnp.concatenate([early[:, :, cut * BS :], late[1]], axis=1),
    ]
    totals, fars = [], []
    for z, (a0, a1) in enumerate(chunks):
        low = lower[0] if z == 0 else lower[1][:, :, (a0 - cut) * BS : (a1 - cut) * BS]
        total = columns(highs[z], 0) + columns(mids[z], 1) + columns(low, 2)
        total = total.astype(BF).reshape((share * (GROUPS + 2),) + total.shape[2:])
        totals.append(total)
        fars.append([over_y(total, s) for s in range(1, ny)])
    totals, fars[:-1] = lax.optimization_barrier((totals, fars[:-1]))
    sides = [over_core(x) for x in totals]
    out = None
    for z, (a0, a1) in enumerate(chunks):
        if z == 1:
            fars[1], sides[0] = lax.optimization_barrier((fars[1], sides[0]))
        srcs = [totals[z], sides[z]] + [q for x in fars[z] for q in (x, over_core(x))]
        out = assemble(order, srcs, a0, BS * BS, out)
    return out


def solution(mesh):
    return jax.shard_map(
        body,
        mesh=mesh,
        in_specs=(P("row", "col", None), P("row", None), P("row"), P("row", None, None), P()),
        out_specs=P("row", None, None),
        check_vma=False,
    )
```

```python
import functools

import jax
import jax.numpy as jnp
from jax import lax
from jax.experimental import pallas as pl
from jax.experimental.pallas import tpu as pltpu
from jax.sharding import PartitionSpec as P

BS = 64
CB = 8
GROUPS = 5
LANES = 128
BF = jnp.bfloat16
F32 = jnp.float32
MIB = 1 << 20

VM = pl.BlockSpec(memory_space=pltpu.VMEM)
SM = pl.BlockSpec(memory_space=pltpu.SMEM)


def params(mib):
    return pltpu.CompilerParams(vmem_limit_bytes=mib * MIB)


def cost(us):
    return pl.CostEstimate(flops=int(us * 1e8), bytes_accessed=int(us * 3.7e6), transcendentals=0)


def low_lanes(rows):
    return lax.broadcasted_iota(jnp.int32, (rows, LANES), 1) < BS


def dot(a, b):
    return lax.dot_general(a, b, (((1,), (0,)), ((), ())), preferred_element_type=F32)


def relayout_kernel(x_ref, o_ref, scr):
    rows, nb, _ = x_ref.shape
    low = low_lanes(32)
    for r in range(rows):
        for q in range(32):
            scr[r, pl.ds(q * 8, nb), :] = x_ref[r, :, q * LANES : (q + 1) * LANES].astype(F32)
        for k in range(0, nb, 2):
            x0 = scr[r, pl.ds(k, 32, stride=8), :]
            x1 = scr[r, pl.ds(k + 1, 32, stride=8), :]
            o_ref[r, k // 2, 0:32] = jnp.where(low, x0, pltpu.roll(x1, BS, 1)).astype(BF)
            o_ref[r, k // 2, 32:64] = jnp.where(low, pltpu.roll(x0, BS, 1), x1).astype(BF)


def relayout(x, first, rows):
    nb = x.shape[1]
    step = 4
    return pl.pallas_call(
        relayout_kernel,
        grid=(rows // step,),
        out_shape=jax.ShapeDtypeStruct((rows, nb // 2, BS, LANES), BF),
        in_specs=[pl.BlockSpec((step, nb, BS * BS), lambda i: (i + first // step, 0, 0))],
        out_specs=pl.BlockSpec((step, nb // 2, BS, LANES), lambda i: (i, 0, 0, 0)),
        scratch_shapes=[pltpu.VMEM((step, 256, LANES), F32)],
        compiler_params=params(4),
        cost_estimate=cost(0.6),
        name="relayout",
    )(x)


def relayout_rows_kernel(x_ref, o_ref, scr, mix):
    rows, nb, _ = x_ref.shape
    low = low_lanes(32)
    for r in range(rows):
        for q in range(32):
            scr[r, pl.ds(q * 8, nb), :] = x_ref[r, :, q * LANES : (q + 1) * LANES].astype(F32)
        for k in range(0, nb, 2):
            x0 = scr[r, pl.ds(k, 32, stride=8), :]
            x1 = scr[r, pl.ds(k + 1, 32, stride=8), :]
            mix[r, k // 2, pl.ds(0, 32, stride=2), :] = jnp.where(low, x0, pltpu.roll(x1, BS, 1))
            mix[r, k // 2, pl.ds(1, 32, stride=2), :] = jnp.where(low, pltpu.roll(x0, BS, 1), x1)
            o_ref[r, k // 2] = mix[r, k // 2].astype(BF)


def relayout_rows(x):
    rows, nb, _ = x.shape
    step = 4
    return pl.pallas_call(
        relayout_rows_kernel,
        grid=(rows // step,),
        out_shape=jax.ShapeDtypeStruct((rows, nb // 2, BS, LANES), BF),
        in_specs=[pl.BlockSpec((step, nb, BS * BS), lambda i: (i, 0, 0))],
        out_specs=pl.BlockSpec((step, nb // 2, BS, LANES), lambda i: (i, 0, 0, 0)),
        scratch_shapes=[pltpu.VMEM((step, 256, LANES), F32), pltpu.VMEM((step, nb // 2, BS, LANES), F32)],
        compiler_params=params(4),
        cost_estimate=cost(1.0),
        name="relayout_rows",
    )(x)


def left_kernel(rb, pct_ref, pl_ref, o_ref):
    slab = lax.axis_index("row")
    low = low_lanes(4 * BS)
    o_ref[...] = jnp.zeros_like(o_ref)

    def pair(ip, carry):
        for half in range(2):
            i = ip * 2 + half
            x = jnp.concatenate([pl_ref[i, 0], pl_ref[i, 1]], axis=1).astype(F32)
            xt = jnp.concatenate([x, x], axis=0).T
            keep = jnp.where(low if half == 0 else jnp.logical_not(low), xt, 0.0)
            for s in range(4):
                w = pct_ref[s, slab * rb + i] - (slab - 1) * CB
                o_ref[ip, w] = (o_ref[ip, w].astype(F32) + keep[s * BS : (s + 1) * BS]).astype(BF)
        return carry

    lax.fori_loop(0, rb // 2, pair, 0)


def left_factor(pct, p_own):
    rb = p_own.shape[0]
    return pl.pallas_call(
        functools.partial(left_kernel, rb),
        out_shape=jax.ShapeDtypeStruct((rb // 2, 3 * CB, BS, LANES), BF),
        in_specs=[SM, VM],
        out_specs=VM,
        compiler_params=params(12),
        cost_estimate=cost(2.9),
        name="left_factor",
    )(pct, p_own)


def column_table(pct, rb, share):
    slab = lax.axis_index("row")
    padded = jnp.pad(pct, ((0, 0), (rb, rb)), constant_values=-1000000)
    near = lax.dynamic_slice_in_dim(padded, slab * rb, 3 * rb, 1)
    w = near - (slab - 2) * CB
    e = (w & (CB - 1)) - share * lax.axis_index("col")
    return jnp.where((w >= 0) & (e >= 0) & (e < share), e * GROUPS + (w >> 3), -1)


def touched(side, tiles):
    return (side, side + 3) if tiles == GROUPS else (0, tiles)


def right_kernel(kind, rb, tiles, table_ref, *refs):
    o_ref = refs[-1]
    core = lax.rem(lax.axis_index("col"), 2)
    low = lax.broadcasted_iota(jnp.int32, (1, LANES), 1) < BS
    wants = [jnp.where(low, p, tiles + p) for p in range(tiles)]

    def fill(src, side, out_first):
        def four(jq, carry):
            for d in range(4):
                jj = 4 * jq + d
                dups = []
                for t in range(4):
                    x = src[jj, t // 2, :, t % 2 * BS : (t % 2 + 1) * BS]
                    dups.append(jnp.concatenate([x, x], axis=1))
                at = [table_ref[t, side * rb + jj] for t in range(4)]
                for p in range(*touched(side, tiles)):
                    total = None
                    for t in range(4):
                        keep = dups[t] * jnp.where(wants[p] == at[t], 1.0, 0.0).astype(BF)
                        total = keep if total is None else total + keep
                    o_ref[out_first + jq, p, d * BS : (d + 1) * BS] = total
            return carry

        lax.fori_loop(0, rb // 4, four, 0)

    quads = rb // 4
    if kind == 0:
        fill(refs[0], 1, 0)
    elif kind == 1:

        @pl.when(core == 0)
        def _():
            fill(refs[0], 0, 0)

        @pl.when(core == 1)
        def _():
            fill(refs[0], 2, 0)
    else:

        def keep(side, out_first):
            def one(jq, carry):
                for p in range(*touched(side, tiles)):
                    o_ref[out_first + jq, p] = refs[0][jq, p]
                return carry

            lax.fori_loop(0, quads, one, 0)

        @pl.when(core == 0)
        def _():
            keep(0, 0)
            fill(refs[1], 2, quads)

        @pl.when(core == 1)
        def _():
            fill(refs[1], 0, 0)
            keep(2, quads)


def right_factor(kind, table, srcs, tiles, us):
    rb = table.shape[1] // 3
    quads = rb // 4 * (2 if kind == 2 else 1)
    return pl.pallas_call(
        functools.partial(right_kernel, kind, rb, tiles),
        out_shape=jax.ShapeDtypeStruct((quads, tiles, 4 * BS, LANES), BF),
        in_specs=[SM] + [VM] * len(srcs),
        out_specs=VM,
        compiler_params=params(8),
        cost_estimate=cost(us),
        name="right_factor",
    )(table, *srcs)


def slot_places(a_cols, counts):
    rb, ka = a_cols.shape
    row = jnp.arange(rb, dtype=jnp.int32)[:, None]
    near = a_cols - (lax.axis_index("row") - 1) * rb - row // 4 * 4
    live = jnp.arange(ka, dtype=jnp.int32)[None, :] < counts[:, None]
    return jnp.where(live, near, 2 * (rb + 2))


def first_slots(shifts, ks):
    col = lax.axis_index("col")
    ny = lax.axis_size("col") // 2
    y, core = col // 2, lax.rem(col, 2)
    slots = []
    for s, flip in shifts:
        c = core if flip == 0 else 1 - core
        slots.append((lax.rem(y - s + ny, ny) * 2 + c) * ks)
    return slots


def lay(first, place_ref, srcs, slots, band, start):
    low = low_lanes(BS)
    zero = jnp.zeros((BS, LANES), BF)

    def group(g, carry):
        for t in range(band.shape[1]):
            band[g, t] = start(g, t)
        for src, slot in zip(srcs, slots):
            for k in range(src.shape[1]):
                for d0 in range(0, 4, 2):
                    cuts = []
                    for d in range(d0, d0 + 2):
                        x = src[4 * g + d, k]
                        r = jnp.concatenate([x[:, BS:], x[:, :BS]], axis=1)
                        cuts.append(
                            (
                                (jnp.where(low, x, zero), jnp.where(low, zero, r)),
                                (jnp.where(low, r, zero), jnp.where(low, zero, x)),
                            )
                        )
                    for e in range(2):
                        at = [place_ref[first + 4 * g + d0 + d, slot + 2 * k + e] for d in range(2)]
                        spots = [(g, a >> 1, slice((d0 + d) * BS, (d0 + d + 1) * BS)) for d, a in enumerate(at)]
                        old = [band[spot] for spot in spots]
                        for spot, a, x, cut in zip(spots, at, old, cuts):
                            band[spot] = x + jnp.where((a & 1) == 0, cut[e][0], cut[e][1])
        return carry

    lax.fori_loop(0, band.shape[0], group, 0)


def band_kernel(first, shifts, place_ref, *refs):
    srcs, band = refs[:-1], refs[-1]
    slots = first_slots(shifts, srcs[0].shape[1] * 2)
    lay(first, place_ref, srcs, slots, band, lambda g, t: jnp.zeros((4 * BS, LANES), BF))


def near_band(place, srcs, shifts, first):
    rows = srcs[0].shape[0]
    return pl.pallas_call(
        functools.partial(band_kernel, first, shifts),
        out_shape=jax.ShapeDtypeStruct((rows // 4, place.shape[0] + 3, 4 * BS, LANES), BF),
        in_specs=[SM] + [VM] * len(srcs),
        out_specs=VM,
        compiler_params=params(12),
        cost_estimate=cost(0.16 * rows),
        name="near_band",
    )(place, *srcs)


def product_kernel(first, rb, shifts, place_ref, own_ref, near_ref, start_ref, *refs):
    srcs = refs[: len(shifts)]
    o_ref, band, acc = refs[len(shifts) :]
    rows = o_ref.shape[0]
    tiles = own_ref.shape[1]
    wide = rb + 2
    slots = first_slots(shifts, srcs[0].shape[1] * 2)
    lay(first, place_ref, srcs, slots, band, lambda g, t: start_ref[g, t])
    quads = rb // 4
    for g in range(rows // 4):
        start = first // 4 + g
        acc[...] = jnp.zeros_like(acc)
        for side in range(3):
            k0, k1 = max(start, side * quads), min(start + wide // 2, (side + 1) * quads)
            if k0 >= k1:
                continue
            p0, p1 = touched(side, tiles)
            ref, base = (own_ref, quads) if side == 1 else (near_ref, 0 if side == 0 else quads)
            total = None
            for k in range(k0, k1):
                lhs = jnp.concatenate([band[g, 2 * (k - start)], band[g, 2 * (k - start) + 1]], axis=1)
                rhs = jnp.concatenate([ref[k - base, p] for p in range(p0, p1)], axis=1)
                part = dot(lhs, rhs)
                total = part if total is None else total + part
            acc[:, p0 * LANES : p1 * LANES] += total
        for d in range(4):
            o_ref[4 * g + d] = acc[d * BS : (d + 1) * BS].astype(BF)


def product(place, own, near, start, srcs, shifts, first, us):
    rows = srcs[0].shape[0]
    rb = place.shape[0]
    tiles = own.shape[1]
    return pl.pallas_call(
        functools.partial(product_kernel, first, rb, shifts),
        out_shape=jax.ShapeDtypeStruct((rows, BS, tiles * LANES), BF),
        in_specs=[SM] + [VM] * (3 + len(srcs)),
        out_specs=VM,
        scratch_shapes=[
            pltpu.VMEM(start.shape, BF),
            pltpu.VMEM((4 * BS, tiles * LANES), F32),
        ],
        compiler_params=params(16),
        cost_estimate=cost(us),
        name="product",
    )(place, own, near, start, *srcs)


def coarse_kernel(sets, a0, a1, left_ref, *refs):
    outs = refs[-1 - len(sets) : -1]
    aps = refs[: -1 - len(sets)]
    scr = refs[-1]
    ac = a1 - a0
    tiles = aps[0].shape[2] // LANES
    for out, (i0, i1) in zip(outs, sets):
        rows = i1 - i0
        low = low_lanes(rows)
        for p0 in range(0, tiles, 2):
            p1 = min(p0 + 2, tiles)
            acc = jnp.zeros((rows * ac, (p1 - p0) * LANES), F32)
            ip = 0
            for ap in aps:
                for g in range(0, ap.shape[0] // 2, 2):
                    lhs = [left_ref[ip + d, i0:i1, a0:a1].reshape(rows * ac, LANES) for d in range(2)]
                    rhs = ap[2 * g : 2 * g + 4, :, p0 * LANES : p1 * LANES].reshape(4 * BS, (p1 - p0) * LANES)
                    acc = acc + dot(jnp.concatenate(lhs, axis=1), rhs)
                    ip += 2
            for p in range(p0, p1):
                scr[p, 0 : rows * ac] = acc[:, (p - p0) * LANES : (p - p0 + 1) * LANES]
        for p in range(tiles):
            for a in range(0, ac, 2):
                x0 = scr[p, pl.ds(a, rows, stride=ac), :]
                x1 = scr[p, pl.ds(a + 1, rows, stride=ac), :]
                at = slice(a * BS, (a + 2) * BS)
                out[p, :, at] = jnp.where(low, x0, pltpu.roll(x1, BS, 1)).astype(out.dtype)
                out[tiles + p, :, at] = jnp.where(low, pltpu.roll(x0, BS, 1), x1).astype(out.dtype)


def coarse_rows(left, aps, sets, a0, a1, dtype, us):
    tiles = aps[0].shape[2] // LANES
    return pl.pallas_call(
        functools.partial(coarse_kernel, sets, a0, a1),
        out_shape=[jax.ShapeDtypeStruct((2 * tiles, i1 - i0, (a1 - a0) * BS), dtype) for i0, i1 in sets],
        in_specs=[VM] * (1 + len(aps)),
        out_specs=[VM] * len(sets),
        scratch_shapes=[pltpu.VMEM((tiles, max(i1 - i0 for i0, i1 in sets) * (a1 - a0), LANES), F32)],
        compiler_params=params(12),
        cost_estimate=cost(us),
        name="coarse",
    )(left, *aps)


def assemble_kernel(order_ref, *refs):
    out = refs[-1]
    srcs = refs[:-1] if len(refs) % 2 else refs[1:-1]
    x = jnp.concatenate([s[...].reshape(-1, s.shape[2]) for s in srcs], axis=0)
    res = dot(order_ref[...], x)
    wide = out.shape[1]
    for i in range(CB):
        out[i] = res[i * wide : (i + 1) * wide].astype(BF)


def assemble(order, srcs, a0, total, before):
    n, _, lanes = srcs[0].shape
    step = lanes
    per = lanes // step
    wide = n * len(srcs)
    specs = [pl.BlockSpec(order.shape, lambda i: (0, 0))]
    args = [order]
    alias = {}
    if before is not None:
        specs.append(pl.BlockSpec(memory_space=pl.ANY))
        args.append(before)
        alias = {1: 0}
    specs += [pl.BlockSpec((n, CB, step), lambda i: (0, 0, i))] * len(srcs)
    return pl.pallas_call(
        assemble_kernel,
        grid=(per,),
        out_shape=jax.ShapeDtypeStruct((CB, wide, total), BF),
        in_specs=specs,
        out_specs=pl.BlockSpec((CB, wide, step), lambda i: (0, 0, a0 * BS // step + i)),
        input_output_aliases=alias,
        compiler_params=params(12),
        cost_estimate=cost(2.9),
        name="assemble",
    )(*args, *srcs)


def assembly_order(shifts, ncol, share):
    col = lax.axis_index("col")
    y, core = col // 2, col % 2
    groups = GROUPS + 2
    size = ncol * share * groups * CB
    out_row = lax.broadcasted_iota(jnp.int32, (size, size), 0)
    src_row = lax.broadcasted_iota(jnp.int32, (size, size), 1)
    per = share * groups * CB
    which, rest = src_row // per, src_row % per
    e, g, i = rest // (groups * CB), rest // CB % groups, rest % CB
    src_col = jnp.zeros_like(which)
    for z, (s, flip) in enumerate(shifts):
        c = (y - s) % (ncol // 2) * 2 + (core + flip) % 2
        src_col = jnp.where(which == z, c, src_col)
    return (out_row == i * (groups * CB) + g * CB + share * src_col + e).astype(BF)


def body(a_blocks, a_cols, counts, p_blocks, p_cols):
    rb, ks, _ = a_blocks.shape
    nrow, ncol = lax.axis_size("row"), lax.axis_size("col")
    ny = ncol // 2
    nfb = p_cols.shape[0]
    share = CB // ncol
    tiles = (GROUPS * share + 1) // 2
    parts = ((0, rb * 2 // 3), (rb * 2 // 3, rb // 3))
    chunks = ((0, 24), (24, 48), (48, 64))

    def outward(x):
        pairs = [(r * ncol + c, (r + 1 - 2 * (c % 2)) * ncol + c) for r in range(nrow) for c in range(ncol)]
        return lax.ppermute(x, ("row", "col"), [(a, b) for a, b in pairs if 0 <= b < nrow * ncol])

    def over_y(x, s):
        return lax.ppermute(x, "col", [(y * 2 + c, (y + s) % ny * 2 + c) for y in range(ny) for c in range(2)])

    def over_core(x):
        return lax.ppermute(x, "col", [(c, c ^ 1) for c in range(ncol)])

    def upward(x):
        return lax.ppermute(x, "row", [(i, i + 1) for i in range(nrow - 1)])

    def downward(x):
        return lax.ppermute(x, "row", [(i + 1, i) for i in range(nrow - 1)])

    shifts = tuple((s, f) for s in range(ny) for f in range(2))
    pct = p_cols.T

    own_a, side_a, far_a = [], [], []
    for h, (first, rows) in enumerate(parts):
        x = relayout(a_blocks, first, rows)
        own_a.append(x)
        far_a.append([over_y(x, s) for s in range(1, ny)])
        side_a.append(over_core(x))
        if h == 0:
            p_own = relayout_rows(p_blocks)
            a_blocks, p_own, side_a[0] = lax.optimization_barrier((a_blocks, p_own, side_a[0]))
    beside = outward(p_own)
    p_blocks, p_own, side_a[1] = lax.optimization_barrier((p_blocks, p_own, side_a[1]))
    table = column_table(pct, rb, share)
    left = left_factor(pct, relayout(p_blocks, 0, rb))
    own = right_factor(0, table, [p_own], tiles, 1.4)
    order = assembly_order(shifts, ncol, share)
    place = slot_places(a_cols, counts)
    bands = [near_band(place, [own_a[h], side_a[h]], shifts[:2], parts[h][0]) for h in range(2)]
    beside, far_a[0], left, own, order, bands = lax.optimization_barrier((beside, far_a[0], left, own, order, bands))
    near = right_factor(1, table, [beside], tiles, 1.2)
    near = right_factor(2, table, [near, over_core(beside)], tiles, 1.4)
    aps = []
    for h in range(2):
        srcs = [z for g in far_a[h] for z in (g, over_core(g))]
        aps.append(product(place, own, near, bands[h], srcs, shifts[2:], parts[h][0], 0.3 * parts[h][1]))
        if h == 0:
            far_a[1], aps[0] = lax.optimization_barrier((far_a[1], aps[0]))
            early = downward(coarse_rows(left, aps, ((0, CB // 2),), 0, BS, BF, 1.0)[0])

    def columns(x, g):
        y = x[: GROUPS * share].reshape((share, GROUPS) + x.shape[1:])
        return jnp.pad(y.astype(F32), ((0, 0), (g, 2 - g), (0, 0), (0, 0)))

    cut = chunks[0][1]
    lows = [coarse_rows(left, aps, ((CB // 2, CB),), a0, a1, BF, 1.0)[0] for a0, a1 in ((0, cut), (cut, BS))]
    raw = [coarse_rows(left, aps, ((2 * CB, 3 * CB),), a0, a1, BF, 1.0)[0] for a0, a1 in chunks]
    late = [downward(lows[0])]
    early, raw[0] = lax.optimization_barrier((early, raw[0]))
    highs = [upward(raw[0])]
    late[0], lows[1] = lax.optimization_barrier((late[0], lows[1]))
    late.append(downward(lows[1]))
    highs[0], raw[1] = lax.optimization_barrier((highs[0], raw[1]))
    highs.append(upward(raw[1]))
    late[1], raw[2] = lax.optimization_barrier((late[1], raw[2]))
    highs.append(upward(raw[2]))
    mids = [coarse_rows(left, aps, ((CB, 2 * CB),), a0, a1, F32, 1.0)[0] for a0, a1 in chunks]
    lower = [
        jnp.concatenate([early[:, :, : cut * BS], late[0]], axis=1),
        jnp.concatenate([early[:, :, cut * BS :], late[1]], axis=1),
    ]
    totals, sides, fars = [], [], []
    for z, (a0, a1) in enumerate(chunks):
        low = lower[0] if z == 0 else lower[1][:, :, (a0 - cut) * BS : (a1 - cut) * BS]
        total = columns(highs[z], 0) + columns(mids[z], 1) + columns(low, 2)
        total = total.astype(BF).reshape((share * (GROUPS + 2),) + total.shape[2:])
        totals.append(total)
        sides.append(over_core(total))
        fars.append([over_y(total, s) for s in range(1, ny)])
    for z in range(len(chunks) - 1):
        fars[z], _ = lax.optimization_barrier((fars[z], totals[z + 1]))
    out = None
    for z, (a0, a1) in enumerate(chunks):
        if z == 1:
            fars[1:], out = lax.optimization_barrier((fars[1:], out))
        srcs = [totals[z], sides[z]] + [q for x in fars[z] for q in (x, over_core(x))]
        out = assemble(order, srcs, a0, BS * BS, out)
    return out


def solution(mesh):
    return jax.shard_map(
        body,
        mesh=mesh,
        in_specs=(P("row", "col", None), P("row", None), P("row"), P("row", None, None), P()),
        out_specs=P("row", None, None),
        check_vma=False,
    )
```

```python
import functools

import jax
import jax.numpy as jnp
from jax import lax
from jax.experimental import pallas as pl
from jax.experimental.pallas import tpu as pltpu
from jax.sharding import PartitionSpec as P

BS = 64
CB = 8
GROUPS = 5
LANES = 128
BF = jnp.bfloat16
F32 = jnp.float32
MIB = 1 << 20

VM = pl.BlockSpec(memory_space=pltpu.VMEM)
SM = pl.BlockSpec(memory_space=pltpu.SMEM)


def params(mib):
    return pltpu.CompilerParams(vmem_limit_bytes=mib * MIB)


def cost(us):
    return pl.CostEstimate(flops=int(us * 1e8), bytes_accessed=int(us * 3.7e6), transcendentals=0)


def low_lanes(rows):
    return lax.broadcasted_iota(jnp.int32, (rows, LANES), 1) < BS


def dot(a, b):
    return lax.dot_general(a, b, (((1,), (0,)), ((), ())), preferred_element_type=F32)


def relayout_kernel(x_ref, o_ref, scr):
    rows, nb, _ = x_ref.shape
    low = low_lanes(32)
    for r in range(rows):
        for q in range(32):
            scr[r, pl.ds(q * 8, nb), :] = x_ref[r, :, q * LANES : (q + 1) * LANES].astype(F32)
        for k in range(0, nb, 2):
            x0 = scr[r, pl.ds(k, 32, stride=8), :]
            x1 = scr[r, pl.ds(k + 1, 32, stride=8), :]
            o_ref[r, k // 2, 0:32] = jnp.where(low, x0, pltpu.roll(x1, BS, 1)).astype(BF)
            o_ref[r, k // 2, 32:64] = jnp.where(low, pltpu.roll(x0, BS, 1), x1).astype(BF)


def relayout(x, first, rows):
    nb = x.shape[1]
    step = 4
    return pl.pallas_call(
        relayout_kernel,
        grid=(rows // step,),
        out_shape=jax.ShapeDtypeStruct((rows, nb // 2, BS, LANES), BF),
        in_specs=[pl.BlockSpec((step, nb, BS * BS), lambda i: (i + first // step, 0, 0))],
        out_specs=pl.BlockSpec((step, nb // 2, BS, LANES), lambda i: (i, 0, 0, 0)),
        scratch_shapes=[pltpu.VMEM((step, 256, LANES), F32)],
        compiler_params=params(4),
        cost_estimate=cost(0.6),
        name="relayout",
    )(x)


def relayout_rows_kernel(x_ref, o_ref, scr, mix):
    rows, nb, _ = x_ref.shape
    low = low_lanes(32)
    for r in range(rows):
        for q in range(32):
            scr[r, pl.ds(q * 8, nb), :] = x_ref[r, :, q * LANES : (q + 1) * LANES].astype(F32)
        for k in range(0, nb, 2):
            x0 = scr[r, pl.ds(k, 32, stride=8), :]
            x1 = scr[r, pl.ds(k + 1, 32, stride=8), :]
            mix[r, k // 2, pl.ds(0, 32, stride=2), :] = jnp.where(low, x0, pltpu.roll(x1, BS, 1))
            mix[r, k // 2, pl.ds(1, 32, stride=2), :] = jnp.where(low, pltpu.roll(x0, BS, 1), x1)
            o_ref[r, k // 2] = mix[r, k // 2].astype(BF)


def relayout_rows(x):
    rows, nb, _ = x.shape
    step = 4
    return pl.pallas_call(
        relayout_rows_kernel,
        grid=(rows // step,),
        out_shape=jax.ShapeDtypeStruct((rows, nb // 2, BS, LANES), BF),
        in_specs=[pl.BlockSpec((step, nb, BS * BS), lambda i: (i, 0, 0))],
        out_specs=pl.BlockSpec((step, nb // 2, BS, LANES), lambda i: (i, 0, 0, 0)),
        scratch_shapes=[pltpu.VMEM((step, 256, LANES), F32), pltpu.VMEM((step, nb // 2, BS, LANES), F32)],
        compiler_params=params(4),
        cost_estimate=cost(1.0),
        name="relayout_rows",
    )(x)


def left_kernel(rb, pct_ref, pl_ref, o_ref):
    slab = lax.axis_index("row")
    low = low_lanes(4 * BS)
    o_ref[...] = jnp.zeros_like(o_ref)

    def pair(ip, carry):
        for half in range(2):
            i = ip * 2 + half
            x = jnp.concatenate([pl_ref[i, 0], pl_ref[i, 1]], axis=1).astype(F32)
            xt = jnp.concatenate([x, x], axis=0).T
            keep = jnp.where(low if half == 0 else jnp.logical_not(low), xt, 0.0)
            for s in range(4):
                w = pct_ref[s, slab * rb + i] - (slab - 1) * CB
                o_ref[ip, w] = (o_ref[ip, w].astype(F32) + keep[s * BS : (s + 1) * BS]).astype(BF)
        return carry

    lax.fori_loop(0, rb // 2, pair, 0)


def left_factor(pct, p_own):
    rb = p_own.shape[0]
    return pl.pallas_call(
        functools.partial(left_kernel, rb),
        out_shape=jax.ShapeDtypeStruct((rb // 2, 3 * CB, BS, LANES), BF),
        in_specs=[SM, VM],
        out_specs=VM,
        compiler_params=params(12),
        cost_estimate=cost(2.9),
        name="left_factor",
    )(pct, p_own)


def column_table(pct, rb, share):
    slab = lax.axis_index("row")
    padded = jnp.pad(pct, ((0, 0), (rb, rb)), constant_values=-1000000)
    near = lax.dynamic_slice_in_dim(padded, slab * rb, 3 * rb, 1)
    w = near - (slab - 2) * CB
    e = (w & (CB - 1)) - share * lax.axis_index("col")
    return jnp.where((w >= 0) & (e >= 0) & (e < share), e * GROUPS + (w >> 3), -1)


def touched(side, tiles):
    return (side, side + 3) if tiles == GROUPS else (0, tiles)


def right_kernel(kind, rb, tiles, table_ref, *refs):
    o_ref = refs[-1]
    core = lax.rem(lax.axis_index("col"), 2)
    low = lax.broadcasted_iota(jnp.int32, (1, LANES), 1) < BS
    wants = [jnp.where(low, p, tiles + p) for p in range(tiles)]

    def fill(src, side, out_first):
        def four(jq, carry):
            for d in range(4):
                jj = 4 * jq + d
                dups = []
                for t in range(4):
                    x = src[jj, t // 2, :, t % 2 * BS : (t % 2 + 1) * BS]
                    dups.append(jnp.concatenate([x, x], axis=1))
                at = [table_ref[t, side * rb + jj] for t in range(4)]
                for p in range(*touched(side, tiles)):
                    total = None
                    for t in range(4):
                        keep = dups[t] * jnp.where(wants[p] == at[t], 1.0, 0.0).astype(BF)
                        total = keep if total is None else total + keep
                    o_ref[out_first + jq, p, d * BS : (d + 1) * BS] = total
            return carry

        lax.fori_loop(0, rb // 4, four, 0)

    quads = rb // 4
    if kind == 0:
        fill(refs[0], 1, 0)
    elif kind == 1:

        @pl.when(core == 0)
        def _():
            fill(refs[0], 0, 0)

        @pl.when(core == 1)
        def _():
            fill(refs[0], 2, 0)
    else:

        def keep(side, out_first):
            def one(jq, carry):
                for p in range(*touched(side, tiles)):
                    o_ref[out_first + jq, p] = refs[0][jq, p]
                return carry

            lax.fori_loop(0, quads, one, 0)

        @pl.when(core == 0)
        def _():
            keep(0, 0)
            fill(refs[1], 2, quads)

        @pl.when(core == 1)
        def _():
            fill(refs[1], 0, 0)
            keep(2, quads)


def right_factor(kind, table, srcs, tiles, us):
    rb = table.shape[1] // 3
    quads = rb // 4 * (2 if kind == 2 else 1)
    return pl.pallas_call(
        functools.partial(right_kernel, kind, rb, tiles),
        out_shape=jax.ShapeDtypeStruct((quads, tiles, 4 * BS, LANES), BF),
        in_specs=[SM] + [VM] * len(srcs),
        out_specs=VM,
        compiler_params=params(8),
        cost_estimate=cost(us),
        name="right_factor",
    )(table, *srcs)


def slot_places(a_cols, counts):
    rb, ka = a_cols.shape
    row = jnp.arange(rb, dtype=jnp.int32)[:, None]
    near = a_cols - (lax.axis_index("row") - 1) * rb - row // 4 * 4
    live = jnp.arange(ka, dtype=jnp.int32)[None, :] < counts[:, None]
    return jnp.where(live, near, 2 * (rb + 2))


def first_slots(shifts, ks):
    col = lax.axis_index("col")
    ny = lax.axis_size("col") // 2
    y, core = col // 2, lax.rem(col, 2)
    slots = []
    for s, flip in shifts:
        c = core if flip == 0 else 1 - core
        slots.append((lax.rem(y - s + ny, ny) * 2 + c) * ks)
    return slots


def lay(first, place_ref, srcs, slots, band, start):
    low = low_lanes(BS)
    zero = jnp.zeros((BS, LANES), BF)

    def group(g, carry):
        for t in range(band.shape[1]):
            band[g, t] = start(g, t)
        for src, slot in zip(srcs, slots):
            for k in range(src.shape[1]):
                for d0 in range(0, 4, 2):
                    cuts = []
                    for d in range(d0, d0 + 2):
                        x = src[4 * g + d, k]
                        r = jnp.concatenate([x[:, BS:], x[:, :BS]], axis=1)
                        cuts.append(
                            (
                                (jnp.where(low, x, zero), jnp.where(low, zero, r)),
                                (jnp.where(low, r, zero), jnp.where(low, zero, x)),
                            )
                        )
                    for e in range(2):
                        at = [place_ref[first + 4 * g + d0 + d, slot + 2 * k + e] for d in range(2)]
                        spots = [(g, a >> 1, slice((d0 + d) * BS, (d0 + d + 1) * BS)) for d, a in enumerate(at)]
                        old = [band[spot] for spot in spots]
                        for spot, a, x, cut in zip(spots, at, old, cuts):
                            band[spot] = x + jnp.where((a & 1) == 0, cut[e][0], cut[e][1])
        return carry

    lax.fori_loop(0, band.shape[0], group, 0)


def band_kernel(first, shifts, place_ref, *refs):
    srcs, band = refs[:-1], refs[-1]
    slots = first_slots(shifts, srcs[0].shape[1] * 2)
    lay(first, place_ref, srcs, slots, band, lambda g, t: jnp.zeros((4 * BS, LANES), BF))


def near_band(place, srcs, shifts, first):
    rows = srcs[0].shape[0]
    return pl.pallas_call(
        functools.partial(band_kernel, first, shifts),
        out_shape=jax.ShapeDtypeStruct((rows // 4, place.shape[0] + 3, 4 * BS, LANES), BF),
        in_specs=[SM] + [VM] * len(srcs),
        out_specs=VM,
        compiler_params=params(12),
        cost_estimate=cost(0.16 * rows),
        name="near_band",
    )(place, *srcs)


def product_kernel(first, rb, shifts, place_ref, own_ref, near_ref, start_ref, *refs):
    srcs = refs[: len(shifts)]
    o_ref, band, acc = refs[len(shifts) :]
    rows = o_ref.shape[0]
    tiles = own_ref.shape[1]
    wide = rb + 2
    slots = first_slots(shifts, srcs[0].shape[1] * 2)
    lay(first, place_ref, srcs, slots, band, lambda g, t: start_ref[g, t])
    quads = rb // 4
    for g in range(rows // 4):
        start = first // 4 + g
        acc[...] = jnp.zeros_like(acc)
        for side in range(3):
            k0, k1 = max(start, side * quads), min(start + wide // 2, (side + 1) * quads)
            if k0 >= k1:
                continue
            p0, p1 = touched(side, tiles)
            ref, base = (own_ref, quads) if side == 1 else (near_ref, 0 if side == 0 else quads)
            total = None
            for k in range(k0, k1):
                lhs = jnp.concatenate([band[g, 2 * (k - start)], band[g, 2 * (k - start) + 1]], axis=1)
                rhs = jnp.concatenate([ref[k - base, p] for p in range(p0, p1)], axis=1)
                part = dot(lhs, rhs)
                total = part if total is None else total + part
            acc[:, p0 * LANES : p1 * LANES] += total
        for d in range(4):
            o_ref[4 * g + d] = acc[d * BS : (d + 1) * BS].astype(BF)


def product(place, own, near, start, srcs, shifts, first, us):
    rows = srcs[0].shape[0]
    rb = place.shape[0]
    tiles = own.shape[1]
    return pl.pallas_call(
        functools.partial(product_kernel, first, rb, shifts),
        out_shape=jax.ShapeDtypeStruct((rows, BS, tiles * LANES), BF),
        in_specs=[SM] + [VM] * (3 + len(srcs)),
        out_specs=VM,
        scratch_shapes=[
            pltpu.VMEM(start.shape, BF),
            pltpu.VMEM((4 * BS, tiles * LANES), F32),
        ],
        compiler_params=params(16),
        cost_estimate=cost(us),
        name="product",
    )(place, own, near, start, *srcs)


def coarse_kernel(sets, a0, a1, left_ref, *refs):
    outs = refs[-1 - len(sets) : -1]
    aps = refs[: -1 - len(sets)]
    scr = refs[-1]
    ac = a1 - a0
    tiles = aps[0].shape[2] // LANES
    for out, (i0, i1) in zip(outs, sets):
        rows = i1 - i0
        low = low_lanes(rows)
        for p0 in range(0, tiles, 2):
            p1 = min(p0 + 2, tiles)
            acc = jnp.zeros((rows * ac, (p1 - p0) * LANES), F32)
            ip = 0
            for ap in aps:
                for g in range(0, ap.shape[0] // 2, 2):
                    lhs = [left_ref[ip + d, i0:i1, a0:a1].reshape(rows * ac, LANES) for d in range(2)]
                    rhs = ap[2 * g : 2 * g + 4, :, p0 * LANES : p1 * LANES].reshape(4 * BS, (p1 - p0) * LANES)
                    acc = acc + dot(jnp.concatenate(lhs, axis=1), rhs)
                    ip += 2
            for p in range(p0, p1):
                scr[p, 0 : rows * ac] = acc[:, (p - p0) * LANES : (p - p0 + 1) * LANES]
        for p in range(tiles):
            for a in range(0, ac, 2):
                x0 = scr[p, pl.ds(a, rows, stride=ac), :]
                x1 = scr[p, pl.ds(a + 1, rows, stride=ac), :]
                at = slice(a * BS, (a + 2) * BS)
                out[p, :, at] = jnp.where(low, x0, pltpu.roll(x1, BS, 1)).astype(out.dtype)
                out[tiles + p, :, at] = jnp.where(low, pltpu.roll(x0, BS, 1), x1).astype(out.dtype)


def coarse_rows(left, aps, sets, a0, a1, dtype, us):
    tiles = aps[0].shape[2] // LANES
    return pl.pallas_call(
        functools.partial(coarse_kernel, sets, a0, a1),
        out_shape=[jax.ShapeDtypeStruct((2 * tiles, i1 - i0, (a1 - a0) * BS), dtype) for i0, i1 in sets],
        in_specs=[VM] * (1 + len(aps)),
        out_specs=[VM] * len(sets),
        scratch_shapes=[pltpu.VMEM((tiles, max(i1 - i0 for i0, i1 in sets) * (a1 - a0), LANES), F32)],
        compiler_params=params(12),
        cost_estimate=cost(us),
        name="coarse",
    )(left, *aps)


def assemble_kernel(order_ref, *refs):
    out = refs[-1]
    srcs = refs[:-1] if len(refs) % 2 else refs[1:-1]
    x = jnp.concatenate([s[...].reshape(-1, s.shape[2]) for s in srcs], axis=0)
    res = dot(order_ref[...], x)
    wide = out.shape[1]
    for i in range(CB):
        out[i] = res[i * wide : (i + 1) * wide].astype(BF)


def assemble(order, srcs, a0, total, before):
    n, _, lanes = srcs[0].shape
    step = lanes
    per = lanes // step
    wide = n * len(srcs)
    specs = [pl.BlockSpec(order.shape, lambda i: (0, 0))]
    args = [order]
    alias = {}
    if before is not None:
        specs.append(pl.BlockSpec(memory_space=pl.ANY))
        args.append(before)
        alias = {1: 0}
    specs += [pl.BlockSpec((n, CB, step), lambda i: (0, 0, i))] * len(srcs)
    return pl.pallas_call(
        assemble_kernel,
        grid=(per,),
        out_shape=jax.ShapeDtypeStruct((CB, wide, total), BF),
        in_specs=specs,
        out_specs=pl.BlockSpec((CB, wide, step), lambda i: (0, 0, a0 * BS // step + i)),
        input_output_aliases=alias,
        compiler_params=params(12),
        cost_estimate=cost(2.9),
        name="assemble",
    )(*args, *srcs)


def assembly_order(shifts, ncol, share):
    col = lax.axis_index("col")
    y, core = col // 2, col % 2
    groups = GROUPS + 2
    size = ncol * share * groups * CB
    out_row = lax.broadcasted_iota(jnp.int32, (size, size), 0)
    src_row = lax.broadcasted_iota(jnp.int32, (size, size), 1)
    per = share * groups * CB
    which, rest = src_row // per, src_row % per
    e, g, i = rest // (groups * CB), rest // CB % groups, rest % CB
    src_col = jnp.zeros_like(which)
    for z, (s, flip) in enumerate(shifts):
        c = (y - s) % (ncol // 2) * 2 + (core + flip) % 2
        src_col = jnp.where(which == z, c, src_col)
    return (out_row == i * (groups * CB) + g * CB + share * src_col + e).astype(BF)


def body(a_blocks, a_cols, counts, p_blocks, p_cols):
    rb, ks, _ = a_blocks.shape
    nrow, ncol = lax.axis_size("row"), lax.axis_size("col")
    ny = ncol // 2
    nfb = p_cols.shape[0]
    share = CB // ncol
    tiles = (GROUPS * share + 1) // 2
    parts = ((0, rb * 2 // 3), (rb * 2 // 3, rb // 3))
    chunks = ((0, 24), (24, 48), (48, 64))

    def outward(x):
        pairs = [(r * ncol + c, (r + 1 - 2 * (c % 2)) * ncol + c) for r in range(nrow) for c in range(ncol)]
        return lax.ppermute(x, ("row", "col"), [(a, b) for a, b in pairs if 0 <= b < nrow * ncol])

    def over_y(x, s):
        return lax.ppermute(x, "col", [(y * 2 + c, (y + s) % ny * 2 + c) for y in range(ny) for c in range(2)])

    def over_core(x):
        return lax.ppermute(x, "col", [(c, c ^ 1) for c in range(ncol)])

    def upward(x):
        return lax.ppermute(x, "row", [(i, i + 1) for i in range(nrow - 1)])

    def downward(x):
        return lax.ppermute(x, "row", [(i + 1, i) for i in range(nrow - 1)])

    shifts = tuple((s, f) for s in range(ny) for f in range(2))
    pct = p_cols.T

    own_a, side_a, far_a = [], [], []
    for h, (first, rows) in enumerate(parts):
        x = relayout(a_blocks, first, rows)
        own_a.append(x)
        far_a.append([over_y(x, s) for s in range(1, ny)])
        side_a.append(over_core(x))
        if h == 0:
            p_own = relayout_rows(p_blocks)
            a_blocks, p_own, side_a[0] = lax.optimization_barrier((a_blocks, p_own, side_a[0]))
    beside = outward(p_own)
    p_blocks, p_own, side_a[1] = lax.optimization_barrier((p_blocks, p_own, side_a[1]))
    table = column_table(pct, rb, share)
    left = left_factor(pct, relayout(p_blocks, 0, rb))
    own = right_factor(0, table, [p_own], tiles, 1.4)
    order = assembly_order([(s, f) for f in range(2) for s in range(ny)], ncol, share)
    place = slot_places(a_cols, counts)
    bands = [near_band(place, [own_a[h], side_a[h]], shifts[:2], parts[h][0]) for h in range(2)]
    beside, far_a[0], left, own, order, bands = lax.optimization_barrier((beside, far_a[0], left, own, order, bands))
    near = right_factor(1, table, [beside], tiles, 1.2)
    near = right_factor(2, table, [near, over_core(beside)], tiles, 1.4)
    aps = []
    for h in range(2):
        srcs = [z for g in far_a[h] for z in (g, over_core(g))]
        aps.append(product(place, own, near, bands[h], srcs, shifts[2:], parts[h][0], 0.3 * parts[h][1]))
        if h == 0:
            far_a[1], aps[0] = lax.optimization_barrier((far_a[1], aps[0]))
            early = downward(coarse_rows(left, aps, ((0, CB // 2),), 0, BS, BF, 1.0)[0])

    def columns(x, g):
        y = x[: GROUPS * share].reshape((share, GROUPS) + x.shape[1:])
        return jnp.pad(y.astype(F32), ((0, 0), (g, 2 - g), (0, 0), (0, 0)))

    cut = chunks[0][1]
    lows = [coarse_rows(left, aps, ((CB // 2, CB),), a0, a1, BF, 1.0)[0] for a0, a1 in ((0, cut), (cut, BS))]
    raw = [coarse_rows(left, aps, ((2 * CB, 3 * CB),), a0, a1, BF, 1.0)[0] for a0, a1 in chunks]
    late = [downward(lows[0])]
    early, raw[0] = lax.optimization_barrier((early, raw[0]))
    highs = [upward(raw[0])]
    late[0], lows[1] = lax.optimization_barrier((late[0], lows[1]))
    late.append(downward(lows[1]))
    highs[0], raw[1] = lax.optimization_barrier((highs[0], raw[1]))
    highs.append(upward(raw[1]))
    late[1], raw[2] = lax.optimization_barrier((late[1], raw[2]))
    highs.append(upward(raw[2]))
    mids = [coarse_rows(left, aps, ((CB, 2 * CB),), a0, a1, F32, 1.0)[0] for a0, a1 in chunks]
    lower = [
        jnp.concatenate([early[:, :, : cut * BS], late[0]], axis=1),
        jnp.concatenate([early[:, :, cut * BS :], late[1]], axis=1),
    ]
    totals, fars = [], []
    for z, (a0, a1) in enumerate(chunks):
        low = lower[0] if z == 0 else lower[1][:, :, (a0 - cut) * BS : (a1 - cut) * BS]
        total = columns(highs[z], 0) + columns(mids[z], 1) + columns(low, 2)
        total = total.astype(BF).reshape((share * (GROUPS + 2),) + total.shape[2:])
        totals.append(total)
        fars.append([over_y(total, s) for s in range(1, ny)])
    for z in range(len(chunks) - 1):
        fars[z], _ = lax.optimization_barrier((fars[z], totals[z + 1]))
    out = None
    for z, (a0, a1) in enumerate(chunks):
        if z == 2:
            fars[2], out = lax.optimization_barrier((fars[2], out))
        mine = jnp.concatenate([totals[z]] + fars[z], axis=0)
        out = assemble(order, [mine, over_core(mine)], a0, BS * BS, out)
    return out


def solution(mesh):
    return jax.shard_map(
        body,
        mesh=mesh,
        in_specs=(P("row", "col", None), P("row", None), P("row"), P("row", None, None), P()),
        out_specs=P("row", None, None),
        check_vma=False,
    )
```
